32 devices in a mesh: batch: 4 (over y, x), seq: 4 (over z), fsdp: 2 (over core).
Axes of the slice: x: 2, y: 2, z: 4, core: 2. Of those that a mesh axis runs over, the one named last changes fastest.
Arguments:
- stream: bfloat16 [16, 8192, 512], P(('batch', 'fsdp'), 'seq'), may hold values from -8 to 8
- norm_gain: bfloat16 [512], P('fsdp'), may hold values from 0.5 to 1.5
- norm_bias: bfloat16 [512], P('fsdp'), may hold values from -3 to 3
- in_real: bfloat16 [512, 256], P('fsdp'), may hold values from -0.1875 to 0.1875
- in_imag: bfloat16 [512, 256], P('fsdp'), may hold values from -0.1875 to 0.1875
- nu_log: bfloat16 [256], P('fsdp'), may hold values from -12 to -2
- theta_log: bfloat16 [256], P('fsdp'), may hold values from -4.59375 to 1.09375
- gamma_log: bfloat16 [256], P('fsdp'), may hold values from -6 to 0
- out_real: bfloat16 [256, 512], P('fsdp'), may hold values from -0.375 to 0.375
- out_imag: bfloat16 [256, 512], P('fsdp'), may hold values from -0.375 to 0.375
- skip_scale: bfloat16 [512], P('fsdp'), may hold values from -4 to 4
- glu_weight: bfloat16 [512, 1024], P('fsdp'), may hold values from -0.5 to 0.5
- glu_bias: bfloat16 [1024], P('fsdp'), may hold values from -3 to 3
- cotangent: bfloat16 [16, 8192, 512], P(('batch', 'fsdp'), 'seq'), may hold values from -6 to 6
Outputs:
- mixed: bfloat16 [16, 8192, 512], P(('batch', 'fsdp'), 'seq')
- grad_stream: float32 [16, 8192, 512], P(('batch', 'fsdp'), 'seq')
- grad_norm_gain: float32 [512], P('fsdp')
- grad_norm_bias: float32 [512], P('fsdp')
- grad_in_real: float32 [512, 256], P('fsdp')
- grad_in_imag: float32 [512, 256], P('fsdp')
- grad_nu_log: float32 [256], P('fsdp')
- grad_theta_log: float32 [256], P('fsdp')
- grad_gamma_log: float32 [256], P('fsdp')
- grad_out_real: float32 [256, 512], P('fsdp')
- grad_out_imag: float32 [256, 512], P('fsdp')
- grad_skip_scale: float32 [512], P('fsdp')
- grad_glu_weight: float32 [512, 1024], P('fsdp')
- grad_glu_bias: float32 [1024], P('fsdp')
- rms_values: float32 [3], replicated
The draws below stay inside these ranges and needn't reach their ends.
All inputs are finite; a program needn't handle non-finite values.
Results may differ from the reference program's by a relative error of at most 0.014.
Values may be sent and summed in bfloat16 or wider, within the bound.
No kernel may reach another device: no remote copies, remote signals or barrier semaphores. Data moves between devices by JAX's collectives and lax.ppermute only.
A program may use at most 192 MiB of HBM per device.

```python
import math
import jax
import jax.numpy as jnp
from jax import lax

H = 512
N = 256
SEQS = 16
LENGTH = 8192


def state_rates(key, slow_share):
    key_pick, key_slow, key_fast = jax.random.split(jax.random.fold_in(key, 11), 3)
    slow_rate = jnp.exp(jax.random.uniform(key_slow, (N,), jnp.float32, math.log(0.3), math.log(2.0))) / LENGTH
    fast_rate = jnp.exp(jax.random.uniform(key_fast, (N,), jnp.float32, math.log(1.0 / 50.0), math.log(1.0 / 8.0)))
    picked = jax.random.uniform(key_pick, (N,), jnp.float32) < slow_share
    return jnp.where(picked, slow_rate, fast_rate)


def draw_nu_log(key, part):
    slow_share = 0.5
    state_rate = state_rates(key, slow_share)
    return jnp.log(state_rate).astype(jnp.bfloat16)


def draw_gamma_log(key, part):
    slow_share = 0.5
    state_rate = state_rates(key, slow_share)
    key = jax.random.fold_in(key, 5)
    jitter = jax.random.uniform(key, (N,), jnp.float32, -0.4, 0.4)
    return (0.5 * jnp.log(-jnp.expm1(-2.0 * state_rate)) + jitter).astype(jnp.bfloat16)


def draw_stream(key, part):
    key = jax.random.fold_in(key, 7)
    key_noise = jax.random.fold_in(key, 0)
    position = jnp.arange(LENGTH, dtype=jnp.float32)
    position_ramp = 0.7 + 0.6 * position / LENGTH
    order = jnp.arange(SEQS, dtype=jnp.float32) / max(SEQS - 1, 1)
    noise_base = jnp.clip(jax.random.normal(key_noise, (SEQS, LENGTH, H), jnp.float32), -3.0, 3.0)
    sequence_ramp = 0.5 * jnp.exp(order * math.log(4.0))
    scaled = noise_base * position_ramp[None, :, None] * sequence_ramp[:, None, None]
    return scaled.astype(jnp.bfloat16)


def steps_of(stream_key, extent, shards, least, top_value):
    def one(dim, blocks):
        steps = jax.random.uniform(jax.random.fold_in(jax.random.fold_in(stream_key, 6), dim), (blocks,), jnp.float32, least / len(shards), top_value / len(shards))
        return jnp.repeat(jnp.exp(steps), extent[dim] // blocks).reshape((-1,) + (1,) * (len(extent) - dim - 1))

    gain = one(*shards[0])
    for cut in shards[1:]:
        gain = gain * one(*cut)
    return gain


def bell_draw(key, extent, scale, limit, shards=(), kind=jnp.bfloat16):
    gain = steps_of(key, extent, shards, -0.22, 0.18) if shards else 1.0
    result = jax.random.normal(key, extent, jnp.float32) * scale * gain
    return jnp.minimum(jnp.maximum(result, -limit), limit).astype(kind)


def setup_inputs(seed: int = 0) -> dict:
    arg_keys = jax.random.split(jax.random.key(seed), 15)
    stream = draw_stream(jax.random.fold_in(arg_keys[14], 71), 0)
    norm_gain = jnp.clip(1.0 + 0.1 * jax.random.normal(arg_keys[1], (H,), jnp.float32), 0.5, 1.5).astype(jnp.bfloat16)
    norm_bias = bell_draw(arg_keys[2], (H,), 0.3, 3.0, ((0, 2),))
    in_real = bell_draw(arg_keys[3], (H, N), (2 * H) ** -0.5, 0.1875, ((0, 2),))
    in_imag = bell_draw(arg_keys[4], (H, N), (2 * H) ** -0.5, 0.1875, ((0, 2),))
    nu_log = draw_nu_log(jax.random.fold_in(arg_keys[14], 71), 0)
    theta_log = jnp.clip(-4.59375 + 5.6875 * jax.random.uniform(arg_keys[6], (N,), jnp.float32) ** steps_of(arg_keys[6], (N,), ((0, 2),), -0.2, 0.2), -4.59375, 1.09375).astype(jnp.bfloat16)
    gamma_log = draw_gamma_log(jax.random.fold_in(arg_keys[14], 71), 0)
    out_real = bell_draw(arg_keys[8], (N, H), N ** -0.5, 0.375, ((0, 2),))
    out_imag = bell_draw(arg_keys[9], (N, H), N ** -0.5, 0.375, ((0, 2),))
    skip_scale = bell_draw(arg_keys[10], (H,), 1.0, 4.0, ((0, 2),))
    glu_weight = bell_draw(arg_keys[11], (H, 2 * H), (H // 4) ** -0.5, 0.5, ((0, 2),))
    glu_bias = bell_draw(arg_keys[12], (2 * H,), 0.3, 3.0, ((0, 2),))
    cotangent = bell_draw(arg_keys[13], (SEQS, LENGTH, H), 1.0, 6.0, ((0, 8), (1, 4)))
    return {"stream": stream, "norm_gain": norm_gain, "norm_bias": norm_bias, "in_real": in_real, "in_imag": in_imag, "nu_log": nu_log, "theta_log": theta_log, "gamma_log": gamma_log, "out_real": out_real, "out_imag": out_imag, "skip_scale": skip_scale, "glu_weight": glu_weight, "glu_bias": glu_bias, "cotangent": cotangent}


@jax.custom_vjp
def low(v):
    return lax.optimization_barrier(v.astype(jnp.bfloat16)).astype(jnp.float32)

@jax.custom_vjp
def low_back(v):
    return v

def low_keep(v):
    return (low(v), None)

def low_pass(kept, grad):
    return (grad,)

def back_keep(v):
    return (v, None)

def back_low(kept, grad):
    return (low(grad),)
low.defvjp(low_keep, low_pass)
low_back.defvjp(back_keep, back_low)
HIGHEST = lax.Precision.HIGHEST

def product(left_side, right_side):
    return jnp.dot(left_side, right_side, precision=HIGHEST, preferred_element_type=jnp.float32)

def layer_norm(sequence, norm_gain, norm_bias):
    centre = sequence - lax.optimization_barrier(jnp.mean(sequence, axis=-1, keepdims=True))
    spread = lax.optimization_barrier(jnp.mean(centre * centre, axis=-1, keepdims=True))
    return centre * lax.rsqrt(spread + 1e-05) * norm_gain + norm_bias

def chain_join(earlier, later):
    real_part = earlier[0] * later[0] - earlier[1] * later[1]
    imag_part = earlier[0] * later[1] + earlier[1] * later[0]
    state_real = later[0] * earlier[2] - later[1] * earlier[3] + later[2]
    state_imag = later[0] * earlier[3] + later[1] * earlier[2] + later[3]
    return (real_part, imag_part, state_real, state_imag)

def glu_gate(projected):
    half_width = projected.shape[-1] // 2
    return projected[..., :half_width] * jax.nn.sigmoid(projected[..., half_width:])

def one_sequence(sequence, weights):
    norm_gain, norm_bias, in_real, in_imag, nu_log, theta_log, gamma_log, out_real, out_imag, skip_scale, glu_weight, glu_bias = weights
    normed = low(layer_norm(sequence, norm_gain, norm_bias))
    drive_real = low_back(product(normed, in_real))
    drive_imag = low_back(product(normed, in_imag))
    input_scale = jnp.exp(gamma_log)
    decay_rate = jnp.exp(nu_log)
    rotation = jnp.exp(theta_log)
    modulus = jnp.exp(-decay_rate)
    lam_real = modulus * jnp.cos(rotation)
    lam_imag = modulus * jnp.sin(rotation)
    elements = (jnp.broadcast_to(lam_real, drive_real.shape), jnp.broadcast_to(lam_imag, drive_real.shape), input_scale * drive_real, input_scale * drive_imag)
    scanned = lax.associative_scan(chain_join, elements, axis=0)
    state_real = low(scanned[2])
    state_imag = low(scanned[3])
    lru_out = low_back(product(state_real, out_real) - product(state_imag, out_imag) + skip_scale * normed)
    activated = low(jax.nn.gelu(lru_out))
    projected = low_back(product(activated, glu_weight) + glu_bias)
    branch = glu_gate(projected)
    squares = jnp.stack([jnp.sum(sequence * sequence), jnp.sum(lru_out * lru_out), jnp.sum(branch * branch)])
    return (sequence + branch, squares)

def reference(stream, norm_gain, norm_bias, in_real, in_imag, nu_log, theta_log, gamma_log, out_real, out_imag, skip_scale, glu_weight, glu_bias, cotangent):
    weights = tuple((tensor.astype(jnp.float32) for tensor in (norm_gain, norm_bias, in_real, in_imag, nu_log, theta_log, gamma_log, out_real, out_imag, skip_scale, glu_weight, glu_bias)))
    stream_wide = stream.astype(jnp.float32)

    def forward(inputs, params):

        def per_sequence(sequence):
            return one_sequence(sequence, params)
        results, squares = lax.map(jax.checkpoint(per_sequence), inputs)
        return (results, lax.optimization_barrier(jnp.sum(squares, axis=0)))
    (results, totals), pull = jax.vjp(forward, stream_wide, weights)
    grad_stream, grads = pull((cotangent.astype(jnp.float32), jnp.zeros_like(totals)))
    rms_values = jnp.sqrt(totals / (SEQS * LENGTH * H))
    return (results.astype(jnp.bfloat16), grad_stream, grads[0], grads[1], grads[2], grads[3], grads[4], grads[5], grads[6], grads[7], grads[8], grads[9], grads[10], grads[11], rms_values)
```

```python
import functools

import jax
import jax.numpy as jnp
from jax import lax
from jax.experimental import pallas as pl
from jax.experimental.pallas import tpu as pltpu
from jax.sharding import PartitionSpec as P

F32 = jnp.float32
BF16 = jnp.bfloat16
HIGHEST = lax.Precision.HIGHEST
CHUNK = 128
HALF = 64
GELU_C = 0.7978845608028654
GELU_K = 0.044715
VMEM_BYTES = 56 * 1024 * 1024


def dot_nn(a, b):
    return jnp.dot(a, b, preferred_element_type=F32)


def dot_tn(a, b):
    return lax.dot_general(a, b, (((0,), (0,)), ((), ())), preferred_element_type=F32)


def dot_nt(a, b):
    return lax.dot_general(a, b, (((1,), (1,)), ((), ())), preferred_element_type=F32)


def dot_nt_wide(a, b):
    return lax.dot_general(
        a, b, (((1,), (1,)), ((), ())), precision=HIGHEST, preferred_element_type=F32
    )


def cmul(ar, ai, br, bi):
    return ar * br - ai * bi, ar * bi + ai * br


def split_low(v):
    high = v.astype(BF16)
    return high, (v - high.astype(F32)).astype(BF16)


ROW_STEP = 0
ROW_LAST = 1
ROW_ENTER = 2
ROW_FIRST = 3
ROW_BACK = 4
ROW_ONE = 5
ROW_SCALE = 6
ROW_RATE = 7


def tables_kernel(rate_ref, p_ref, q_ref, small_ref):
    states = rate_ref.shape[1]
    decay = jnp.exp(rate_ref[0:1, :])
    rotation = jnp.exp(rate_ref[1:2, :])
    scale = jnp.exp(rate_ref[2:3, :])
    steps = (lax.broadcasted_iota(jnp.int32, (CHUNK, states), 0) - HALF).astype(F32)
    turn = steps * rotation
    cos = jnp.cos(turn)
    sin = jnp.sin(turn)
    grow = jnp.exp(-steps * decay)
    p_ref[:, :states] = grow * cos
    p_ref[:, states:] = grow * sin
    shrink = scale * jnp.exp(steps * decay)
    q_ref[:, :states] = shrink * cos
    q_ref[:, states:] = -shrink * sin

    def power(row, count):
        angle = count * rotation
        size = jnp.exp(-count * decay)
        small_ref[row : row + 1, :states] = size * jnp.cos(angle)
        small_ref[row : row + 1, states:] = size * jnp.sin(angle)

    power(ROW_STEP, float(CHUNK))
    power(ROW_LAST, float(CHUNK - 1 - HALF))
    power(ROW_ENTER, float(HALF + 1))
    power(ROW_FIRST, float(HALF))
    power(ROW_BACK, float(CHUNK - HALF))
    power(ROW_ONE, 1.0)
    small_ref[ROW_SCALE : ROW_SCALE + 1, :states] = scale
    small_ref[ROW_SCALE : ROW_SCALE + 1, states:] = 1.0 / scale
    small_ref[ROW_RATE : ROW_RATE + 1, :states] = decay
    small_ref[ROW_RATE : ROW_RATE + 1, states:] = rotation


def make_tables(rates):
    states = rates.shape[1]
    return pl.pallas_call(
        tables_kernel,
        out_shape=(
            jax.ShapeDtypeStruct((CHUNK, 2 * states), F32),
            jax.ShapeDtypeStruct((CHUNK, 2 * states), F32),
            jax.ShapeDtypeStruct((8, 2 * states), F32),
        ),
        name="tables",
    )(rates)


def pair(ref, row, states):
    return ref[row : row + 1, :states], ref[row : row + 1, states:]


def norm_drive_kernel(
    stream_ref, vec_ref, win_ref, q_ref, tri_ref, small_ref,
    normed_ref, sums_ref, end_ref, square_ref, carry, stack,
):
    states = q_ref.shape[1] // 2
    rows = stream_ref.shape[0]
    first = pl.program_id(1) == 0

    @pl.when(first)
    def _():
        carry[...] = jnp.zeros_like(carry)

    @pl.when(first & (pl.program_id(0) == 0))
    def _():
        square_ref[...] = jnp.zeros_like(square_ref)

    gain = vec_ref[0:1, :]
    bias = vec_ref[1:2, :]
    step_r, step_i = pair(small_ref, ROW_STEP, states)
    last_r, last_i = pair(small_ref, ROW_LAST, states)
    cr, ci = carry[0:1, :states], carry[0:1, states:]
    for k in range(rows // CHUNK):
        at = pl.ds(k * CHUNK, CHUNK)
        x = stream_ref[at, :].astype(F32)
        square_ref[...] += jnp.sum((x * x).reshape(CHUNK // 8, 8, x.shape[1]), axis=0)
        centre = x - jnp.mean(x, axis=-1, keepdims=True)
        spread = jnp.mean(centre * centre, axis=-1, keepdims=True)
        normed = (centre * lax.rsqrt(spread + 1e-05) * gain + bias).astype(BF16)
        normed_ref[at, :] = normed
        drive = dot_nn(normed, win_ref[...])
        zr, zi = cmul(drive[:, :states], drive[:, states:], q_ref[:, :states], q_ref[:, states:])
        hr, lr = split_low(zr)
        hi, li = split_low(zi)
        stack[k, :CHUNK, :states] = hr
        stack[k, CHUNK:, :states] = lr
        stack[k, :CHUNK, states:] = hi
        stack[k, CHUNK:, states:] = li
        s = dot_nn(tri_ref[...], stack[k])
        sums_ref[at, :] = s
        er, ei = cmul(s[CHUNK - 1 :, :states], s[CHUNK - 1 :, states:], last_r, last_i)
        nr, ni = cmul(cr, ci, step_r, step_i)
        cr, ci = nr + er, ni + ei
    carry[0:1, :states] = cr
    carry[0:1, states:] = ci
    end_ref[0, 0:1, :states] = cr
    end_ref[0, 0:1, states:] = ci


def whole(shape):
    return pl.BlockSpec(shape, lambda *_: (0,) * len(shape))


def norm_drive(stream, vec, win, q, tri, small, block=512):
    seqs, length, width = stream.shape
    states2 = q.shape[1]
    blocks = length // block
    token = lambda w: pl.BlockSpec((None, block, w), lambda s, i: (s, i, 0))
    return pl.pallas_call(
        norm_drive_kernel,
        grid=(seqs, blocks),
        in_specs=[
            token(width), whole(vec.shape), whole(win.shape), whole(q.shape), whole(tri.shape),
            whole(small.shape),
        ],
        out_specs=[
            token(width),
            token(states2),
            pl.BlockSpec((1, 1, states2), lambda s, i: (s, 0, 0)),
            whole((8, width)),
        ],
        out_shape=[
            jax.ShapeDtypeStruct((seqs, length, width), BF16),
            jax.ShapeDtypeStruct((seqs, length, states2), F32),
            jax.ShapeDtypeStruct((seqs, 1, states2), F32),
            jax.ShapeDtypeStruct((8, width), F32),
        ],
        scratch_shapes=[
            pltpu.VMEM((8, states2), F32),
            pltpu.VMEM((block // CHUNK, 2 * CHUNK, states2), BF16),
        ],
        compiler_params=pltpu.CompilerParams(vmem_limit_bytes=VMEM_BYTES),
        name="norm_drive",
    )(stream, vec, win, q, tri, small)


def block_kernel(
    sums_ref, normed_ref, stream_ref, cot_ref, vec_ref, gluvec_ref, wout_ref, wglu_ref, p_ref,
    tri_ref, small_ref, enter_ref,
    mixed_ref, state_ref, dlru_ref, back_ref, start_ref, dglu_ref, dout_ref, acc_ref, gacc_ref,
    carry, stack, act, dproj, slope,
):
    states = p_ref.shape[1] // 2
    rows = sums_ref.shape[0]
    width = stream_ref.shape[1]
    first = pl.program_id(1) == 0

    @pl.when(first)
    def _():
        carry[0:1, :] = enter_ref[0]
        carry[1:2, :] = jnp.zeros_like(carry[1:2, :])
        carry[2:3, :states] = jnp.ones_like(carry[2:3, :states])
        carry[2:3, states:] = jnp.zeros_like(carry[2:3, states:])

    @pl.when(first & (pl.program_id(0) == 0))
    def _():
        acc_ref[...] = jnp.zeros_like(acc_ref)
        gacc_ref[...] = jnp.zeros_like(gacc_ref)
        dglu_ref[...] = jnp.zeros_like(dglu_ref)
        dout_ref[...] = jnp.zeros_like(dout_ref)

    step_r, step_i = pair(small_ref, ROW_STEP, states)
    last_r, last_i = pair(small_ref, ROW_LAST, states)
    enter_r, enter_i = pair(small_ref, ROW_ENTER, states)
    first_r, first_i = pair(small_ref, ROW_FIRST, states)
    skip = vec_ref[2:3, :]
    value_bias = gluvec_ref[0:1, :width]
    gate_bias = gluvec_ref[0:1, width:]
    cr, ci = carry[0:1, :states], carry[0:1, states:]
    ar, ai = carry[1:2, :states], carry[1:2, states:]
    wr, wi = carry[2:3, :states], carry[2:3, states:]
    fold = lambda v: jnp.sum(v.reshape(CHUNK // 8, 8, v.shape[1]), axis=0)
    for k in range(rows // CHUNK):
        at = pl.ds(k * CHUNK, CHUNK)
        qr, qi = cmul(cr, ci, enter_r, enter_i)
        sr = sums_ref[at, :states]
        si = sums_ref[at, states:]
        er, ei = cmul(sr[CHUNK - 1 :], si[CHUNK - 1 :], last_r, last_i)
        nr, ni = cmul(cr, ci, step_r, step_i)
        cr, ci = nr + er, ni + ei
        hr, hi = cmul(sr + qr, si + qi, p_ref[:, :states], p_ref[:, states:])
        state_ref[at, :states] = hr.astype(BF16)
        state_ref[at, states:] = hi.astype(BF16)
        lru = dot_nn(state_ref[at, :], wout_ref[...])
        lru = lru + skip * normed_ref[at, :].astype(F32)
        lru2 = lru * lru
        acc_ref[0:8, :] += fold(lru2)
        inner = lru * (GELU_C + GELU_C * GELU_K * lru2)
        gate = 0.5 + 0.5 * jnp.tanh(inner)
        gelu = lru * gate
        slope[at, :] = gate + (gelu - gelu * gate) * (2 * GELU_C + 6 * GELU_C * GELU_K * lru2)
        act[at, :] = gelu.astype(BF16)
        projected = dot_nn(act[at, :], wglu_ref[...])
        value = projected[:, :width] + value_bias
        gate2 = 0.5 + 0.5 * jnp.tanh(0.5 * (projected[:, width:] + gate_bias))
        branch = value * gate2
        mixed_ref[at, :] = (stream_ref[at, :].astype(F32) + branch).astype(BF16)
        acc_ref[8:16, :] += fold(branch * branch)
        cot = cot_ref[at, :].astype(F32)
        part = cot * branch
        dvalue = (cot * gate2).astype(BF16)
        dgate = (part - part * gate2).astype(BF16)
        dproj[at, :width] = dvalue
        dproj[at, width:] = dgate
        gacc_ref[:, :width] += fold(dvalue.astype(F32))
        gacc_ref[:, width:] += fold(dgate.astype(F32))
        dact = dot_nt(dproj[at, :], wglu_ref[...])
        dlru = (dact * slope[at, :]).astype(BF16)
        dlru_ref[at, :] = dlru
        wide = dlru.astype(F32)
        acc_ref[16:24, :] += fold(wide)
        acc_ref[24:32, :] += fold(wide * normed_ref[at, :].astype(F32))
        pull = dot_nt(dlru, wout_ref[...])
        zr, zi = cmul(pull[:, :states], pull[:, states:], p_ref[:, :states], -p_ref[:, states:])
        ahr, alr = split_low(zr)
        ahi, ali = split_low(zi)
        stack[k, :CHUNK, :states] = ahr
        stack[k, CHUNK:, :states] = alr
        stack[k, :CHUNK, states:] = ahi
        stack[k, CHUNK:, states:] = ali
        back = dot_nn(tri_ref[...], stack[k])
        back_ref[at, :] = back
        fr, fi = cmul(back[0:1, :states], back[0:1, states:], first_r, -first_i)
        gr, gi = cmul(fr, fi, wr, wi)
        ar, ai = ar + gr, ai + gi
        wr, wi = cmul(wr, wi, step_r, -step_i)
    dglu_ref[...] += dot_tn(act[...], dproj[...])
    dout_ref[...] += dot_tn(state_ref[...], dlru_ref[...])
    carry[0:1, :states] = cr
    carry[0:1, states:] = ci
    carry[1:2, :states] = ar
    carry[1:2, states:] = ai
    carry[2:3, :states] = wr
    carry[2:3, states:] = wi
    start_ref[0, 0:1, :states] = ar
    start_ref[0, 0:1, states:] = ai


def block_pass(sums, normed, stream, cot, vec, gluvec, wout, wglu, p, tri, small, enter, block=512):
    seqs, length, width = stream.shape
    states2 = p.shape[1]
    blocks = length // block
    token = lambda w: pl.BlockSpec((None, block, w), lambda s, i: (s, i, 0))
    row = pl.BlockSpec((1, 1, states2), lambda s, i: (s, 0, 0))
    return pl.pallas_call(
        block_kernel,
        grid=(seqs, blocks),
        in_specs=[
            token(states2), token(width), token(width), token(width),
            whole(vec.shape), whole(gluvec.shape), whole(wout.shape), whole(wglu.shape),
            whole(p.shape), whole(tri.shape), whole(small.shape), row,
        ],
        out_specs=[
            token(width), token(states2), token(width), token(states2), row,
            whole((width, 2 * width)), whole((states2, width)), whole((32, width)),
            whole((8, 2 * width)),
        ],
        out_shape=[
            jax.ShapeDtypeStruct((seqs, length, width), BF16),
            jax.ShapeDtypeStruct((seqs, length, states2), BF16),
            jax.ShapeDtypeStruct((seqs, length, width), BF16),
            jax.ShapeDtypeStruct((seqs, length, states2), F32),
            jax.ShapeDtypeStruct((seqs, 1, states2), F32),
            jax.ShapeDtypeStruct((width, 2 * width), F32),
            jax.ShapeDtypeStruct((states2, width), F32),
            jax.ShapeDtypeStruct((32, width), F32),
            jax.ShapeDtypeStruct((8, 2 * width), F32),
        ],
        scratch_shapes=[
            pltpu.VMEM((8, states2), F32),
            pltpu.VMEM((block // CHUNK, 2 * CHUNK, states2), BF16),
            pltpu.VMEM((block, width), BF16),
            pltpu.VMEM((block, 2 * width), BF16),
            pltpu.VMEM((block, width), F32),
        ],
        compiler_params=pltpu.CompilerParams(vmem_limit_bytes=VMEM_BYTES),
        name="block_pass",
    )(sums, normed, stream, cot, vec, gluvec, wout, wglu, p, tri, small, enter)


def adjoint_kernel(
    back_ref, state_ref, normed_ref, vec_ref, win_ref, q_ref, small_ref, enter_ref, acc_ref,
    ddrive_ref, din_ref, rows_ref, carry, sums,
):
    states = q_ref.shape[1] // 2
    rows = back_ref.shape[0]
    first = pl.program_id(1) == 0

    @pl.when(first)
    def _():
        carry[0:1, :] = enter_ref[0]

    @pl.when(first & (pl.program_id(0) == 0))
    def _():
        din_ref[...] = jnp.zeros_like(din_ref)
        sums[...] = jnp.zeros_like(sums)

    first_r, first_i = pair(small_ref, ROW_FIRST, states)
    back_r, back_i = pair(small_ref, ROW_BACK, states)
    cr, ci = carry[0:1, :states], carry[0:1, states:]
    fold = lambda v: jnp.sum(v.reshape(CHUNK // 8, 8, v.shape[1]), axis=0)
    for k in reversed(range(rows // CHUNK)):
        at = pl.ds(k * CHUNK, CHUNK)
        qr, qi = cmul(cr, ci, back_r, -back_i)
        vr = back_ref[at, :states] + qr
        vi = back_ref[at, states:] + qi
        cr, ci = cmul(vr[0:1], vi[0:1], first_r, -first_i)
        ar, ai = cmul(vr, vi, q_ref[:, :states], -q_ref[:, states:])
        hr = state_ref[at, :states].astype(F32)
        hi = state_ref[at, states:].astype(F32)
        sums[0:8, :states] += fold(ar * hr + ai * hi)
        sums[0:8, states:] += fold(ai * hr - ar * hi)
        lr, li = ar.astype(BF16), ai.astype(BF16)
        sums[8:16, :states] += fold(lr.astype(F32))
        sums[8:16, states:] += fold(li.astype(F32))
        ddrive_ref[at, :states] = lr
        ddrive_ref[at, states:] = li
    carry[0:1, :states] = cr
    carry[0:1, states:] = ci
    din_ref[...] += dot_tn(normed_ref[...], ddrive_ref[...])

    @pl.when((pl.program_id(1) == pl.num_programs(1) - 1) & (pl.program_id(0) == pl.num_programs(0) - 1))
    def _():
        win = win_ref[...].astype(F32)
        din = din_ref[...]
        width = win.shape[0]
        gain = vec_ref[0:1, :]
        bias = vec_ref[1:2, :]
        skip = vec_ref[2:3, :]
        in_r, in_i = win[:, :states], win[:, states:]
        g_r, g_i = din[:, :states], din[:, states:]
        x_r = jnp.sum(g_r * in_r + g_i * in_i, axis=0, keepdims=True)
        x_i = jnp.sum(g_i * in_r - g_r * in_i, axis=0, keepdims=True)
        inverse = small_ref[ROW_SCALE : ROW_SCALE + 1, states:]
        d = jnp.sum(sums[0:8, :], axis=0, keepdims=True)
        d_r = d[:, :states] * inverse - x_r
        d_i = d[:, states:] * inverse - x_i
        decay, rotation = pair(small_ref, ROW_RATE, states)
        ones = jnp.ones((8, 2 * states), F32)
        gathered = dot_nt_wide(ones, win * din)[0:1]
        total = jnp.broadcast_to(jnp.sum(sums[8:16, :], axis=0, keepdims=True), (8, 2 * states))
        d_lru = jnp.sum(acc_ref[16:24, :], axis=0, keepdims=True)
        d_skip = jnp.sum(acc_ref[24:32, :], axis=0, keepdims=True)
        d_bias = dot_nt_wide(total, win)[0:1] + skip * d_lru
        d_gain = (gathered + skip * d_skip - bias * d_bias) / gain
        rows_ref[...] = jnp.zeros_like(rows_ref)
        rows_ref[0:1, :] = d_gain
        rows_ref[1:2, :] = d_bias
        rows_ref[2:3, :states] = -decay * d_r
        rows_ref[2:3, states:] = rotation * d_i
        rows_ref[3:4, :states] = x_r
        rows_ref[4:5, :] = d_skip


def adjoint_pass(back, state, normed, vec, win, q, small, enter, acc, block=512):
    seqs, length, width = normed.shape
    states2 = q.shape[1]
    blocks = length // block
    token = lambda w: pl.BlockSpec((None, block, w), lambda s, i: (s, blocks - 1 - i, 0))
    row = pl.BlockSpec((1, 1, states2), lambda s, i: (s, 0, 0))
    return pl.pallas_call(
        adjoint_kernel,
        grid=(seqs, blocks),
        in_specs=[
            token(states2), token(states2), token(width), whole(vec.shape), whole(win.shape),
            whole(q.shape), whole(small.shape), row, whole(acc.shape),
        ],
        out_specs=[token(states2), whole((width, states2)), whole((8, width))],
        out_shape=[
            jax.ShapeDtypeStruct((seqs, length, states2), BF16),
            jax.ShapeDtypeStruct((width, states2), F32),
            jax.ShapeDtypeStruct((8, width), F32),
        ],
        scratch_shapes=[
            pltpu.VMEM((8, states2), F32),
            pltpu.VMEM((16, states2), F32),
        ],
        compiler_params=pltpu.CompilerParams(vmem_limit_bytes=VMEM_BYTES),
        name="adjoint_pass",
    )(back, state, normed, vec, win, q, small, enter, acc)


def input_kernel(ddrive_ref, dlru_ref, stream_ref, cot_ref, vec_ref, win_ref, out_ref):
    rows = stream_ref.shape[0]
    gain = vec_ref[0:1, :]
    skip = vec_ref[2:3, :]
    for k in range(rows // CHUNK):
        at = pl.ds(k * CHUNK, CHUNK)
        d = dot_nt(ddrive_ref[at, :], win_ref[...]) + skip * dlru_ref[at, :].astype(F32)
        x = stream_ref[at, :].astype(F32)
        centre = x - jnp.mean(x, axis=-1, keepdims=True)
        spread = jnp.mean(centre * centre, axis=-1, keepdims=True)
        inverse = lax.rsqrt(spread + 1e-05)
        hat = centre * inverse
        dhat = d * gain
        m1 = jnp.mean(dhat, axis=-1, keepdims=True)
        m2 = jnp.mean(dhat * hat, axis=-1, keepdims=True)
        out_ref[at, :] = (dhat - m1 - hat * m2) * inverse + cot_ref[at, :].astype(F32)


def input_pass(ddrive, dlru, stream, cot, vec, win, block=512):
    seqs, length, width = stream.shape
    states2 = ddrive.shape[2]
    token = lambda w: pl.BlockSpec((None, block, w), lambda s, i: (s, i, 0))
    return pl.pallas_call(
        input_kernel,
        grid=(seqs, length // block),
        in_specs=[
            token(states2), token(width), token(width), token(width), whole(vec.shape),
            whole(win.shape),
        ],
        out_specs=token(width),
        out_shape=jax.ShapeDtypeStruct((seqs, length, width), F32),
        compiler_params=pltpu.CompilerParams(vmem_limit_bytes=VMEM_BYTES),
        name="input_pass",
    )(ddrive, dlru, stream, cot, vec, win)


def carried(ends, whole_r, whole_i, axis, reverse):
    count = lax.axis_size(axis)
    place = lax.axis_index(axis)
    states = whole_r.shape[-1]
    total_r = jnp.zeros_like(ends[..., :states])
    total_i = total_r
    if count <= 4:
        power_r, power_i = jnp.ones_like(whole_r), jnp.zeros_like(whole_i)
        for hop in range(1, count):
            moves = [(i + hop, i) if reverse else (i, i + hop) for i in range(count - hop)]
            came = lax.ppermute(ends, axis, moves)
            gr, gi = cmul(came[..., :states], came[..., states:], power_r, power_i)
            total_r, total_i = total_r + gr, total_i + gi
            power_r, power_i = cmul(power_r, power_i, whole_r, whole_i)
        return jnp.concatenate([total_r, total_i], axis=-1)
    every = lax.all_gather(ends, axis)
    ahead = count - 1 - place if reverse else place

    def one(step, state):
        source = count - 1 - step if reverse else step
        item = lax.dynamic_index_in_dim(every, source, 0, False)
        gr, gi = cmul(state[0], state[1], whole_r, whole_i)
        return gr + item[..., :states], gi + item[..., states:]

    total_r, total_i = lax.fori_loop(0, ahead, one, (total_r, total_i))
    return jnp.concatenate([total_r, total_i], axis=-1)


def swap_moves(axis, bit):
    return [(i, i ^ bit) for i in range(lax.axis_size(axis))]


def sum_all(parts):
    me = lax.axis_index("fsdp")
    mine = lax.dynamic_index_in_dim(parts, me, 0, False)
    other = lax.dynamic_index_in_dim(parts, 1 - me, 0, False)
    came = lax.ppermute(other, "fsdp", [(0, 1), (1, 0)])
    halves = (mine.astype(F32) + came.astype(F32)).astype(BF16)
    count = lax.axis_size("batch")
    place = lax.axis_index("batch")
    got = [lax.dynamic_index_in_dim(halves, place, 0, False)]
    for hop in range(1, count):
        piece = lax.dynamic_index_in_dim(halves, place ^ hop, 0, False)
        got.append(lax.ppermute(piece, "batch", swap_moves("batch", hop)))
    piece = sum(g.astype(F32) for g in got).astype(BF16)
    ring = lax.axis_size("seq")
    if ring <= 4:
        got = [piece]
        for hop in range(1, ring):
            got.append(lax.ppermute(piece, "seq", [(i, (i + hop) % ring) for i in range(ring)]))
        piece = sum(g.astype(F32) for g in got).astype(BF16)
    else:
        piece = lax.psum(piece.astype(F32), "seq").astype(BF16)
    got = [piece]
    for hop in range(1, count):
        got.append(lax.ppermute(piece, "batch", swap_moves("batch", hop)))
    full = jnp.zeros((count,) + piece.shape, BF16)
    for hop in range(count):
        full = lax.dynamic_update_index_in_dim(full, got[hop], place ^ hop, 0)
    return full


def on_device(
    stream, norm_gain, norm_bias, in_real, in_imag, nu_log, theta_log, gamma_log, out_real,
    out_imag, skip_scale, glu_weight, glu_bias, cotangent,
):
    seqs, length, width = stream.shape
    gather = lambda a, axis=0: lax.all_gather(a, "fsdp", axis=axis, tiled=True)
    states = 2 * nu_log.shape[0]
    win = gather(jnp.concatenate([in_real, in_imag], axis=1))
    wout = gather(jnp.stack([out_real, -out_imag]), 1).reshape(2 * states, width)
    wglu = gather(glu_weight)
    vec = gather(jnp.stack([norm_gain, norm_bias, skip_scale]), 1).astype(F32)
    gluvec = gather(glu_bias)[None, :].astype(F32)
    rates = gather(jnp.stack([nu_log, theta_log, gamma_log]), 1).astype(F32)
    p, q, small = make_tables(rates)
    row = lax.broadcasted_iota(jnp.int32, (CHUNK, CHUNK), 0)
    column = lax.broadcasted_iota(jnp.int32, (CHUNK, CHUNK), 1)
    lower = (column <= row).astype(BF16)
    upper = (column >= row).astype(BF16)
    tri = jnp.concatenate([lower, lower], axis=1)
    tri_back = jnp.concatenate([upper, upper], axis=1)
    decay, rotation = small[ROW_RATE, :states], small[ROW_RATE, states:]
    size = jnp.exp(-decay * length)
    whole_r = size * jnp.cos(rotation * length)
    whole_i = size * jnp.sin(rotation * length)

    normed, sums, ends, square = norm_drive(stream, vec, win, q, tri, small)
    enter = carried(ends, whole_r, whole_i, "seq", False)
    mixed, state, dlru, back, starts, dglu, dout, acc, gacc = block_pass(
        sums, normed, stream, cotangent, vec, gluvec, wout, wglu, p, tri_back, small, enter
    )
    later = carried(starts, whole_r, -whole_i, "seq", True)
    ddrive, din, rows = adjoint_pass(back, state, normed, vec, win, q, small, later, acc)
    grad_stream = input_pass(ddrive, dlru, stream, cotangent, vec, win)

    batch = lax.axis_size("batch")
    first = jnp.concatenate(
        [
            dglu.reshape(2, batch, -1, 2 * width),
            jnp.moveaxis(dout.reshape(2, 2, batch, -1, width), 0, 3).reshape(
                2, batch, -1, 2 * width
            ),
        ],
        axis=2,
    ).astype(BF16)
    squares = jnp.stack([jnp.sum(square), jnp.sum(acc[0:8]), jnp.sum(acc[8:16])])
    squares = jnp.pad(squares, (0, width // 2 - 3))
    d_glu_bias = jnp.sum(gacc, axis=0).reshape(2, 2, width // 2)
    pieces = [
        rows[0].reshape(2, -1),
        rows[1].reshape(2, -1),
        jnp.moveaxis(rows[2].reshape(2, 2, -1), 0, 1).reshape(2, -1),
        jnp.pad(rows[3, :states].reshape(2, -1), ((0, 0), (0, states // 2))),
        rows[4].reshape(2, -1),
        d_glu_bias[:, 0],
        d_glu_bias[:, 1],
        jnp.broadcast_to(squares, (2, width // 2)),
    ]
    tail = jnp.stack(pieces, axis=1).reshape(2, batch, -1, width)
    tail = jnp.pad(tail, ((0, 0), (0, 0), (0, 16 - tail.shape[2]), (0, 0)))
    second = jnp.concatenate([din.reshape(2, batch, -1, 2 * states), tail], axis=2).astype(BF16)
    first = sum_all(first)
    second = sum_all(second)
    glu_rows = width // (2 * batch)
    out_glu = first[:, :glu_rows].reshape(width // 2, 2 * width).astype(F32)
    out_out = first[:, glu_rows:].reshape(states // 2, 2, width).astype(F32)
    out_in = second[:, :glu_rows].reshape(width // 2, 2 * states).astype(F32)
    line = second[:, glu_rows : glu_rows + 8 // batch * (width // 2) // width].reshape(8, width // 2).astype(F32)
    token_count = stream.size * lax.axis_size("batch") * lax.axis_size("seq") * lax.axis_size("fsdp")
    half = states // 2
    return (
        mixed,
        grad_stream,
        line[0],
        line[1],
        out_in[:, :states],
        out_in[:, states:],
        line[2, :half],
        line[2, half:],
        line[3, :half],
        out_out[:, 0],
        -out_out[:, 1],
        line[4],
        out_glu,
        line[5:7].reshape(-1),
        jnp.sqrt(line[7, :3] / token_count),
    )


def solution(mesh):
    tokens = P(("batch", "fsdp"), "seq", None)
    vector = P("fsdp")
    matrix = P("fsdp", None)
    weights = (
        vector, vector, matrix, matrix, vector, vector, vector, matrix, matrix, vector, matrix,
        vector,
    )
    return jax.shard_map(
        on_device,
        mesh=mesh,
        in_specs=(tokens,) + weights + (tokens,),
        out_specs=(tokens, tokens) + weights + (P(),),
        check_vma=False,
    )
```

```python
import jax
import jax.numpy as jnp
from jax import lax
from jax.experimental import pallas as pl
from jax.experimental.pallas import tpu as pltpu
from jax.sharding import PartitionSpec as P

F32 = jnp.float32
BF16 = jnp.bfloat16
HIGHEST = lax.Precision.HIGHEST
CHUNK = 128
HALF = 64
BLOCK = 512
SUB = 64
GELU_C = 0.7978845608028654
GELU_K = 0.044715
MIB = 1024 * 1024


def dot_nn(a, b):
    return jnp.dot(a, b, preferred_element_type=F32)


def dot_tn(a, b):
    return lax.dot_general(a, b, (((0,), (0,)), ((), ())), preferred_element_type=F32)


def dot_nt(a, b):
    return lax.dot_general(a, b, (((1,), (1,)), ((), ())), preferred_element_type=F32)


def dot_nt_wide(a, b):
    return lax.dot_general(
        a, b, (((1,), (1,)), ((), ())), precision=HIGHEST, preferred_element_type=F32
    )


def cmul(ar, ai, br, bi):
    return ar * br - ai * bi, ar * bi + ai * br


def fold(v):
    return jnp.sum(v.reshape(v.shape[0] // 8, 8, v.shape[1]), axis=0)


def split_store(stack, k, zr, zi):
    states = zr.shape[1]
    for part, v in enumerate((zr, zi)):
        columns = pl.ds(part * states, states)
        high = v.astype(BF16)
        stack[k, :CHUNK, columns] = high
        stack[k, CHUNK:, columns] = (v - high.astype(F32)).astype(BF16)


def fill_triangle(tri, upper):
    row = lax.broadcasted_iota(jnp.int32, (CHUNK, CHUNK), 0)
    column = lax.broadcasted_iota(jnp.int32, (CHUNK, CHUNK), 1)
    inside = (column >= row) if upper else (column <= row)
    ones = jnp.where(inside, 1.0, 0.0).astype(BF16)
    tri[:, :CHUNK] = ones
    tri[:, CHUNK:] = ones


ROW_STEP = 0
ROW_LAST = 1
ROW_ENTER = 2
ROW_FIRST = 3
ROW_BACK = 4
ROW_WHOLE = 5
ROW_SCALE = 6
ROW_RATE = 7
ROW_GAIN = 8
ROW_BIAS = 9
ROW_SKIP = 10
ROW_GLU = 11
TABLE_ROWS = 16


def pair(ref, row, states):
    return ref[row : row + 1, :states], ref[row : row + 1, states:]


def row_of(ref, row):
    return ref[row : row + 1, :]


def fill_tables(me, own_ref, other_ref, p_ref, q_ref, small_ref, length):
    states = q_ref.shape[1] // 2
    width = q_ref.shape[1]
    own = own_ref[...].astype(F32)
    other = other_ref[...].astype(F32)
    low = jnp.where(me == 0, own, other)
    high = jnp.where(me == 0, other, own)

    def both(first, count):
        rows = [h[first + i : first + i + 1] for h in (low, high) for i in range(count)]
        return jnp.concatenate(rows, axis=1)

    small_ref[...] = jnp.zeros_like(small_ref)
    for row, first in ((ROW_GAIN, 0), (ROW_BIAS, 2), (ROW_SKIP, 4)):
        small_ref[row : row + 1, :] = both(first, 2)
    glu = both(6, 4)
    small_ref[ROW_GLU : ROW_GLU + 1, :] = glu[:, :width]
    small_ref[ROW_GLU + 1 : ROW_GLU + 2, :] = glu[:, width:]
    decay = jnp.exp(both(10, 1))
    rotation = jnp.exp(both(11, 1))
    scale = jnp.exp(both(12, 1))
    steps = (lax.broadcasted_iota(jnp.int32, (CHUNK, states), 0) - HALF).astype(F32)
    turn = steps * rotation
    cos = jnp.cos(turn)
    sin = jnp.sin(turn)
    grow = jnp.exp(-steps * decay)
    p_ref[:, :states] = grow * cos
    p_ref[:, states:] = grow * sin
    shrink = scale * jnp.exp(steps * decay)
    q_ref[:, :states] = shrink * cos
    q_ref[:, states:] = -shrink * sin
    counts = {
        ROW_STEP: CHUNK,
        ROW_LAST: CHUNK - 1 - HALF,
        ROW_ENTER: HALF + 1,
        ROW_FIRST: HALF,
        ROW_BACK: CHUNK - HALF,
        ROW_WHOLE: length,
    }
    assert sorted(counts) == list(range(6))
    index = lax.broadcasted_iota(jnp.int32, (8, states), 0)
    count = jnp.zeros((8, states), F32)
    for row, steps in counts.items():
        count = jnp.where(index == row, float(steps), count)
    size = jnp.exp(-count * decay)
    small_ref[:6, :states] = (size * jnp.cos(count * rotation))[:6]
    small_ref[:6, states:] = (size * jnp.sin(count * rotation))[:6]
    small_ref[ROW_SCALE : ROW_SCALE + 1, :states] = scale
    small_ref[ROW_SCALE : ROW_SCALE + 1, states:] = 1.0 / scale
    small_ref[ROW_RATE : ROW_RATE + 1, :states] = decay
    small_ref[ROW_RATE : ROW_RATE + 1, states:] = rotation


def join_halves(me, whole, own, other, columns=slice(None)):
    rows = own.shape[0]
    whole[pl.ds(pl.multiple_of(me * rows, rows), rows), columns] = own[...]
    whole[pl.ds(pl.multiple_of((1 - me) * rows, rows), rows), columns] = other[...]


def cost(microseconds):
    return pl.CostEstimate(
        flops=0, transcendentals=0, bytes_accessed=int(microseconds * 3.6e6)
    )


def norm_kernel(
    length, place_ref, stream_hbm, cot_hbm, inr_hbm, ini_hbm, glu_hbm, outr_hbm, outi_hbm,
    vec_own, vec_other, inr_other, ini_other,
    normed_ref, sums_ref, end_ref, p_ref, q_ref, small_ref, win_ref, wback_ref, square_ref,
    stream_ref, cot_ref, glu_ref, outr_ref, outi_ref,
    carry, stack, tri, inr_own, ini_own, sems,
):
    states = q_ref.shape[1] // 2
    seq = pl.program_id(0)
    step = pl.program_id(1)
    steps = length // BLOCK
    base = step * BLOCK
    copy = lambda source, target, k: pltpu.make_async_copy(source, target, sems.at[k])

    def stream_copy(n):
        at = (n // steps, pl.ds(pl.multiple_of(n % steps * BLOCK, BLOCK), BLOCK))
        return copy(stream_hbm.at[at], stream_ref.at[at], n)

    after = stream_ref.shape[0] * steps
    weights = [copy(inr_hbm, inr_own, after), copy(ini_hbm, ini_own, after + 1)]
    onward = [
        copy(source, target, after + 2 + k)
        for k, (source, target) in enumerate(
            ((glu_hbm, glu_ref), (outr_hbm, outr_ref), (outi_hbm, outi_ref), (cot_hbm, cot_ref))
        )
    ]

    @pl.when((step == 0) & (seq == 0))
    def _():
        me = place_ref[0]
        for c in weights:
            c.start()
        for n in range(after):
            stream_copy(n).start()
        for c in onward:
            c.start()
        fill_tables(me, vec_own, vec_other, p_ref, q_ref, small_ref, length)
        fill_triangle(tri, False)
        square_ref[...] = jnp.zeros_like(square_ref)
        for c in weights:
            c.wait()
        join_halves(me, win_ref, inr_own, inr_other, slice(0, states))
        join_halves(me, win_ref, ini_own, ini_other, slice(states, 2 * states))
        wback_ref[:, :states] = win_ref[:, :states]
        wback_ref[:, states:] = -win_ref[:, states:]

    stream_copy(seq * steps + step).wait()

    @pl.when(step == 0)
    def _():
        carry[...] = jnp.zeros_like(carry)

    gain = row_of(small_ref, ROW_GAIN)
    bias = row_of(small_ref, ROW_BIAS)
    step_r, step_i = pair(small_ref, ROW_STEP, states)
    last_r, last_i = pair(small_ref, ROW_LAST, states)
    cr, ci = carry[0:1, :states], carry[0:1, states:]
    squares = jnp.zeros_like(square_ref)
    for r in range(0, BLOCK, SUB):
        at = pl.ds(pl.multiple_of(base + r, SUB), SUB)
        x = stream_ref[seq, at, :].astype(F32)
        squares += fold(x * x)
        centre = x - jnp.mean(x, axis=-1, keepdims=True)
        spread = jnp.mean(centre * centre, axis=-1, keepdims=True)
        normed_ref[seq, at, :] = (centre * lax.rsqrt(spread + 1e-05) * gain + bias).astype(BF16)
    square_ref[...] += squares
    rows = pl.ds(pl.multiple_of(base, BLOCK), BLOCK)
    drive = dot_nn(normed_ref[seq, rows, :], win_ref[...])
    for k in range(BLOCK // CHUNK):
        part = drive[k * CHUNK : (k + 1) * CHUNK]
        zr, zi = cmul(part[:, :states], part[:, states:], q_ref[:, :states], q_ref[:, states:])
        split_store(stack, k, zr, zi)
        s = dot_nn(tri[...], stack[k])
        sums_ref[seq, pl.ds(pl.multiple_of(base + k * CHUNK, CHUNK), CHUNK), :] = s
        er, ei = cmul(s[CHUNK - 1 :, :states], s[CHUNK - 1 :, states:], last_r, last_i)
        nr, ni = cmul(cr, ci, step_r, step_i)
        cr, ci = nr + er, ni + ei
    carry[0:1, :states] = cr
    carry[0:1, states:] = ci
    end_ref[seq, :, :states] = cr
    end_ref[seq, :, states:] = ci

    @pl.when((seq == pl.num_programs(0) - 1) & (step == steps - 1))
    def _():
        for c in onward:
            c.wait()


HBM_SPEC = pl.BlockSpec(memory_space=pltpu.HBM)
VMEM_SPEC = pl.BlockSpec(memory_space=pltpu.VMEM)
SMEM_SPEC = pl.BlockSpec(memory_space=pltpu.SMEM)


def kept(*arrays):
    return [pltpu.with_memory_space_constraint(a, pltpu.VMEM) for a in arrays]


def large(a):
    return a.size * a.dtype.itemsize > 2 * MIB


def specs_of(arrays):
    return [HBM_SPEC if large(a) else VMEM_SPEC for a in arrays]


def placed(arrays):
    return [in_hbm(a)[0] if large(a) else kept(a)[0] for a in arrays]


def in_hbm(*arrays):
    return [pltpu.with_memory_space_constraint(a, pltpu.HBM) for a in arrays]


def norm_pass(place, stream, cot, into, onward, vectors):
    seqs, length, width = stream.shape
    half, states = into[0].shape
    states2 = 2 * states
    return pl.pallas_call(
        lambda *refs: norm_kernel(length, *refs),
        grid=(seqs, length // BLOCK),
        in_specs=[SMEM_SPEC] + [HBM_SPEC] * 7 + [VMEM_SPEC] * 4,
        out_specs=[VMEM_SPEC] * 14,
        out_shape=[
            pltpu.VMEM((seqs, length, width), BF16),
            pltpu.VMEM((seqs, length, states2), F32),
            pltpu.VMEM((seqs, 1, states2), F32),
            pltpu.VMEM((CHUNK, states2), F32),
            pltpu.VMEM((CHUNK, states2), F32),
            pltpu.VMEM((TABLE_ROWS, states2), F32),
            pltpu.VMEM((width, states2), BF16),
            pltpu.VMEM((width, states2), BF16),
            pltpu.VMEM((8, width), F32),
            pltpu.VMEM(stream.shape, BF16),
            pltpu.VMEM(cot.shape, BF16),
        ]
        + [pltpu.VMEM(a.shape, BF16) for a in onward],
        scratch_shapes=[
            pltpu.VMEM((8, states2), F32),
            pltpu.VMEM((BLOCK // CHUNK, 2 * CHUNK, states2), BF16),
            pltpu.VMEM((CHUNK, 2 * CHUNK), BF16),
            pltpu.VMEM((half, states), BF16),
            pltpu.VMEM((half, states), BF16),
            pltpu.SemaphoreType.DMA((seqs * (length // BLOCK) + 6,)),
        ],
        compiler_params=pltpu.CompilerParams(vmem_limit_bytes=8 * MIB),
        cost_estimate=cost(9),
        name="norm_pass",
    )(
        place,
        *in_hbm(stream, cot, into[0], into[2], *onward),
        *kept(*vectors, into[1], into[3]),
    )


def entering(carry, came, seq, small_ref, states):
    whole_r, whole_i = pair(small_ref, ROW_WHOLE, states)
    total_r = came[0][seq, :, :states]
    total_i = came[0][seq, :, states:]
    power_r, power_i = whole_r, whole_i
    for ref in came[1:]:
        gr, gi = cmul(ref[seq, :, :states], ref[seq, :, states:], power_r, power_i)
        total_r, total_i = total_r + gr, total_i + gi
        power_r, power_i = cmul(power_r, power_i, whole_r, whole_i)
    carry[0:1, :states] = total_r
    carry[0:1, states:] = total_i


def block_kernel(
    hops, place_ref, _, normed_ref, stream_ref, cot_ref, p_ref, small_ref, glu_own, glu_other,
    outr_own, outr_other, outi_own, outi_other, *rest,
):
    came = rest[:hops]
    (
        mixed_ref, back_ref, state_ref, dlru_ref, start_ref, keep_ref, send_ref, acc_ref, gacc_ref,
        carry, stack, tri, act, dproj, slope, wglu, wout, dglu, dout,
    ) = rest[hops:]
    states = p_ref.shape[1] // 2
    width = stream_ref.shape[2]
    seq = pl.program_id(0)
    step = pl.program_id(1)
    base = step * BLOCK

    @pl.when((step == 0) & (seq == 0))
    def _():
        me = place_ref[0]
        join_halves(me, wglu, glu_own, glu_other)
        join_halves(me, wout.at[pl.ds(0, states)], outr_own, outr_other)
        join_halves(me, wout.at[pl.ds(states, states)], outi_own, outi_other)
        fill_triangle(tri, True)
        acc_ref[...] = jnp.zeros_like(acc_ref)
        gacc_ref[...] = jnp.zeros_like(gacc_ref)
        dglu[...] = jnp.zeros_like(dglu)
        dout[...] = jnp.zeros_like(dout)

    @pl.when(step == 0)
    def _():
        entering(carry, came, seq, small_ref, states)
        carry[1:2, :] = jnp.zeros_like(carry[1:2, :])
        carry[2:3, :states] = jnp.ones_like(carry[2:3, :states])
        carry[2:3, states:] = jnp.zeros_like(carry[2:3, states:])

    step_r, step_i = pair(small_ref, ROW_STEP, states)
    last_r, last_i = pair(small_ref, ROW_LAST, states)
    enter_r, enter_i = pair(small_ref, ROW_ENTER, states)
    first_r, first_i = pair(small_ref, ROW_FIRST, states)
    skip = row_of(small_ref, ROW_SKIP)
    value_bias = row_of(small_ref, ROW_GLU)
    gate_bias = row_of(small_ref, ROW_GLU + 1)
    cr, ci = carry[0:1, :states], carry[0:1, states:]
    ar, ai = carry[1:2, :states], carry[1:2, states:]
    wr, wi = carry[2:3, :states], carry[2:3, states:]
    rows = pl.ds(pl.multiple_of(base, BLOCK), BLOCK)
    for k in range(BLOCK // CHUNK):
        at = pl.ds(pl.multiple_of(base + k * CHUNK, CHUNK), CHUNK)
        qr, qi = cmul(cr, ci, enter_r, enter_i)
        sr = back_ref[seq, at, :states]
        si = back_ref[seq, at, states:]
        er, ei = cmul(sr[CHUNK - 1 :], si[CHUNK - 1 :], last_r, last_i)
        nr, ni = cmul(cr, ci, step_r, step_i)
        cr, ci = nr + er, ni + ei
        hr, hi = cmul(sr + qr, si + qi, p_ref[:, :states], p_ref[:, states:])
        state_ref[seq, at, :states] = hr.astype(BF16)
        state_ref[seq, at, states:] = (-hi).astype(BF16)
    readout = dot_nn(state_ref[seq, rows, :], wout[...])
    squares = jnp.zeros((8, width), F32)
    for r in range(0, BLOCK, SUB):
        at = pl.ds(pl.multiple_of(base + r, SUB), SUB)
        lru = readout[r : r + SUB] + skip * normed_ref[seq, at, :].astype(F32)
        lru2 = lru * lru
        squares += fold(lru2)
        inner = lru * (GELU_C + GELU_C * GELU_K * lru2)
        gate = 0.5 + 0.5 * jnp.tanh(inner)
        gelu = lru * gate
        slope[r : r + SUB, :] = gate + (gelu - gelu * gate) * (
            2 * GELU_C + 6 * GELU_C * GELU_K * lru2
        )
        act[r : r + SUB, :] = gelu.astype(BF16)
    acc_ref[0:8, :] += squares
    projected = dot_nn(act[...], wglu[...])
    squares = jnp.zeros((8, width), F32)
    value_sum = jnp.zeros((8, width), F32)
    gate_sum = jnp.zeros((8, width), F32)
    for r in range(0, BLOCK, SUB):
        at = pl.ds(pl.multiple_of(base + r, SUB), SUB)
        value = projected[r : r + SUB, :width] + value_bias
        gate = 0.5 + 0.5 * jnp.tanh(0.5 * (projected[r : r + SUB, width:] + gate_bias))
        branch = value * gate
        mixed_ref[r : r + SUB, :] = (stream_ref[seq, at, :].astype(F32) + branch).astype(BF16)
        squares += fold(branch * branch)
        cot = cot_ref[seq, at, :].astype(F32)
        part = cot * branch
        dvalue = (cot * gate).astype(BF16)
        dgate = (part - part * gate).astype(BF16)
        dproj[r : r + SUB, :width] = dvalue
        dproj[r : r + SUB, width:] = dgate
        value_sum += fold(dvalue.astype(F32))
        gate_sum += fold(dgate.astype(F32))
    acc_ref[8:16, :] += squares
    gacc_ref[0:8, :] += value_sum
    gacc_ref[8:16, :] += gate_sum
    dact = dot_nt(dproj[...], wglu[...])
    total = jnp.zeros((8, width), F32)
    skips = jnp.zeros((8, width), F32)
    for r in range(0, BLOCK, SUB):
        at = pl.ds(pl.multiple_of(base + r, SUB), SUB)
        dlru = (dact[r : r + SUB] * slope[r : r + SUB, :]).astype(BF16)
        dlru_ref[seq, at, :] = dlru
        wide = dlru.astype(F32)
        total += fold(wide)
        skips += fold(wide * normed_ref[seq, at, :].astype(F32))
    acc_ref[16:24, :] += total
    acc_ref[24:32, :] += skips
    pull = dot_nt(dlru_ref[seq, rows, :], wout[...])
    dglu[...] += dot_tn(act[...], dproj[...])
    dout[...] += dot_tn(state_ref[seq, rows, :], dlru_ref[seq, rows, :])
    for k in range(BLOCK // CHUNK):
        at = pl.ds(pl.multiple_of(base + k * CHUNK, CHUNK), CHUNK)
        part = pull[k * CHUNK : (k + 1) * CHUNK]
        zr, zi = cmul(part[:, :states], part[:, states:], p_ref[:, :states], p_ref[:, states:])
        split_store(stack, k, zr, zi)
        back = dot_nn(tri[...], stack[k])
        back_ref[seq, at, :] = back
        fr, fi = cmul(back[0:1, :states], back[0:1, states:], first_r, first_i)
        gr, gi = cmul(fr, fi, wr, wi)
        ar, ai = ar + gr, ai + gi
        wr, wi = cmul(wr, wi, step_r, step_i)
    carry[0:1, :states] = cr
    carry[0:1, states:] = ci
    carry[1:2, :states] = ar
    carry[1:2, states:] = ai
    carry[2:3, :states] = wr
    carry[2:3, states:] = wi
    start_ref[seq, :, :states] = ar
    start_ref[seq, :, states:] = ai

    @pl.when((seq == pl.num_programs(0) - 1) & (step == pl.num_programs(1) - 1))
    def _():
        batch, height, _ = keep_ref.shape
        high = width // (2 * batch)
        part = height - high
        for ref, f in ((keep_ref, place_ref[0]), (send_ref, 1 - place_ref[0])):
            for b in range(batch):
                first = pl.multiple_of((f * batch + b) * high, high)
                ref[b, :high, :] = dglu[pl.ds(first, high), :].astype(BF16)
                first = pl.multiple_of((f * batch + b) * part, part)
                ref[b, high:, :width] = dout[pl.ds(first, part), :].astype(BF16)
                ref[b, high:, width:] = dout[pl.ds(states + first, part), :].astype(BF16)


def block_pass(place, batch, sums, normed, stream, cot, p, small, halves, came):
    seqs, length, width = stream.shape
    states2 = p.shape[1]
    height = width // (2 * batch) + states2 // (4 * batch)
    return pl.pallas_call(
        lambda *refs: block_kernel(len(came), *refs),
        grid=(seqs, length // BLOCK),
        in_specs=[SMEM_SPEC] + [VMEM_SPEC] * (12 + len(came)),
        out_specs=[pl.BlockSpec((None, BLOCK, width), lambda s, i: (s, i, 0))] + [VMEM_SPEC] * 8,
        out_shape=[
            jax.ShapeDtypeStruct((seqs, length, width), BF16),
            pltpu.VMEM((seqs, length, states2), F32),
            pltpu.VMEM((seqs, length, states2), BF16),
            pltpu.VMEM((seqs, length, width), BF16),
            jax.ShapeDtypeStruct((seqs, 1, states2), F32),
            pltpu.VMEM((batch, height, 2 * width), BF16),
            pltpu.VMEM((batch, height, 2 * width), BF16),
            pltpu.VMEM((32, width), F32),
            pltpu.VMEM((16, width), F32),
        ],
        scratch_shapes=[
            pltpu.VMEM((8, states2), F32),
            pltpu.VMEM((BLOCK // CHUNK, 2 * CHUNK, states2), BF16),
            pltpu.VMEM((CHUNK, 2 * CHUNK), BF16),
            pltpu.VMEM((BLOCK, width), BF16),
            pltpu.VMEM((BLOCK, 2 * width), BF16),
            pltpu.VMEM((BLOCK, width), F32),
            pltpu.VMEM((width, 2 * width), BF16),
            pltpu.VMEM((states2, width), BF16),
            pltpu.VMEM((width, 2 * width), F32),
            pltpu.VMEM((states2, width), F32),
        ],
        input_output_aliases={1: 1},
        compiler_params=pltpu.CompilerParams(vmem_limit_bytes=14 * MIB),
        cost_estimate=cost(36),
        name="block_pass",
    )(place, *kept(sums, normed, stream, cot, p, small, *halves, *came))


def adjoint_kernel(
    hops, others, place_ref, back_ref, _, normed_ref, win_ref, q_ref, small_ref, square_ref, acc_ref, gacc_ref,
    *rest,
):
    came = rest[:hops]
    ddrive_ref, keep_ref, send_ref, carry, sums, din = rest[hops + others :]
    states = q_ref.shape[1] // 2
    seq = pl.program_id(0)
    step = pl.program_id(1)
    base = (pl.num_programs(1) - 1 - step) * BLOCK

    @pl.when(step == 0)
    def _():
        entering(carry, came, seq, small_ref, states)

    @pl.when((step == 0) & (seq == 0))
    def _():
        din[...] = jnp.zeros_like(din)
        sums[...] = jnp.zeros_like(sums)

    first_r, first_i = pair(small_ref, ROW_FIRST, states)
    back_r, back_i = pair(small_ref, ROW_BACK, states)
    cr, ci = carry[0:1, :states], carry[0:1, states:]
    zeros = jnp.zeros((8, states), F32)
    real_sum = imag_sum = real_total = imag_total = zeros
    for k in reversed(range(BLOCK // CHUNK)):
        at = pl.ds(pl.multiple_of(base + k * CHUNK, CHUNK), CHUNK)
        qr, qi = cmul(cr, ci, back_r, back_i)
        vr = back_ref[seq, at, :states] + qr
        vi = back_ref[seq, at, states:] + qi
        cr, ci = cmul(vr[0:1], vi[0:1], first_r, first_i)
        ar, ai = cmul(vr, vi, q_ref[:, :states], q_ref[:, states:])
        hr = ddrive_ref[seq, at, :states].astype(F32)
        hi = ddrive_ref[seq, at, states:].astype(F32)
        real_sum += fold(ar * hr + ai * hi)
        imag_sum += fold(ar * hi - ai * hr)
        lr, li = ar.astype(BF16), ai.astype(BF16)
        real_total += fold(lr.astype(F32))
        imag_total += fold(li.astype(F32))
        ddrive_ref[seq, at, :states] = lr
        ddrive_ref[seq, at, states:] = li
    carry[0:1, :states] = cr
    carry[0:1, states:] = ci
    sums[0:8, :states] += real_sum
    sums[0:8, states:] += imag_sum
    sums[8:16, :states] += real_total
    sums[8:16, states:] += imag_total
    rows = pl.ds(pl.multiple_of(base, BLOCK), BLOCK)
    din[...] += dot_tn(normed_ref[seq, rows, :], ddrive_ref[seq, rows, :])

    @pl.when((step == pl.num_programs(1) - 1) & (seq == pl.num_programs(0) - 1))
    def _():
        width = din.shape[0]
        gain = row_of(small_ref, ROW_GAIN)
        bias = row_of(small_ref, ROW_BIAS)
        skip = row_of(small_ref, ROW_SKIP)
        weight = win_ref[...].astype(F32)
        grad = din[...]
        in_r, in_i = weight[:, :states], weight[:, states:]
        g_r, g_i = grad[:, :states], grad[:, states:]
        x_r = jnp.sum(g_r * in_r + g_i * in_i, axis=0, keepdims=True)
        x_i = jnp.sum(g_r * in_i - g_i * in_r, axis=0, keepdims=True)
        inverse = small_ref[ROW_SCALE : ROW_SCALE + 1, states:]
        column = lambda v: jnp.sum(v, axis=0, keepdims=True)
        d = column(sums[0:8, :])
        d_r = d[:, :states] * inverse - x_r
        d_i = d[:, states:] * inverse - x_i
        decay, rotation = pair(small_ref, ROW_RATE, states)
        gathered = dot_nt_wide(jnp.ones((8, 2 * states), F32), weight * grad)[0:1]
        total = jnp.broadcast_to(column(sums[8:16, :]), (8, 2 * states))
        d_lru = column(acc_ref[16:24, :])
        d_skip = column(acc_ref[24:32, :])
        d_bias = dot_nt_wide(total, weight)[0:1] + skip * d_lru
        d_gain = (gathered + skip * d_skip - bias * d_bias) / gain
        d_nu = -decay * d_r
        d_theta = rotation * d_i
        d_values = column(gacc_ref[0:8, :])
        d_gates = column(gacc_ref[8:16, :])
        lane = lax.broadcasted_iota(jnp.int32, (1, width // 2), 1)
        squares = jnp.zeros((1, width // 2), F32)
        for place, v in enumerate((square_ref[...], acc_ref[0:8, :], acc_ref[8:16, :])):
            squares = jnp.where(lane == place, jnp.sum(v), squares)
        half, some = width // 2, states // 2
        batch, height, _ = keep_ref.shape
        high = width // (2 * batch)
        me = place_ref[0]

        def chosen(f, low, up):
            return jnp.where(f == 0, low, up)

        for ref, f in ((keep_ref, me), (send_ref, 1 - me)):
            wide = lambda v: chosen(f, v[:, :half], v[:, half:])
            thin = lambda v: chosen(f, v[:, :some], v[:, some:])
            d_glu = chosen(f, d_values, d_gates)
            lines = (
                wide(d_gain),
                wide(d_bias),
                jnp.concatenate([thin(d_nu), thin(d_theta)], axis=1),
                jnp.concatenate([thin(x_r), jnp.zeros((1, some), F32)], axis=1),
                wide(d_skip),
                d_glu[:, :half],
                d_glu[:, half:],
                squares,
            )
            for b in range(batch):
                first = pl.multiple_of((f * batch + b) * high, high)
                ref[b, :high, :states] = din[pl.ds(first, high), :states].astype(BF16)
                ref[b, :high, states:] = (-din[pl.ds(first, high), states:]).astype(BF16)
                line = jnp.concatenate(lines[b * 8 // batch : (b + 1) * 8 // batch], axis=1)
                line = jnp.broadcast_to(line, (height - high, width)).astype(BF16)
                ref[b, high:, :] = line


def adjoint_pass(
    place, batch, back, state, normed, wback, q, small, square, acc, gacc, came, after
):
    seqs, length, width = normed.shape
    states2 = q.shape[1]
    return pl.pallas_call(
        lambda *refs: adjoint_kernel(len(came), len(after), *refs),
        grid=(seqs, length // BLOCK),
        in_specs=[SMEM_SPEC] + [VMEM_SPEC] * (9 + len(came)) + specs_of(after),
        out_specs=[VMEM_SPEC] * 3,
        out_shape=[
            pltpu.VMEM((seqs, length, states2), BF16),
            pltpu.VMEM((batch, width // (2 * batch) + 16, states2), BF16),
            pltpu.VMEM((batch, width // (2 * batch) + 16, states2), BF16),
        ],
        scratch_shapes=[
            pltpu.VMEM((8, states2), F32),
            pltpu.VMEM((16, states2), F32),
            pltpu.VMEM((width, states2), F32),
        ],
        input_output_aliases={2: 0},
        compiler_params=pltpu.CompilerParams(vmem_limit_bytes=8 * MIB),
        cost_estimate=cost(11),
        name="adjoint_pass",
    )(place, *kept(back, state, normed, wback, q, small, square, acc, gacc, *came), *placed(after))


def input_kernel(seq, ddrive_ref, dlru_ref, stream_ref, cot_ref, small_ref, win_ref, *rest):
    out_ref = rest[-1]
    base = pl.program_id(0) * BLOCK
    gain = row_of(small_ref, ROW_GAIN)
    skip = row_of(small_ref, ROW_SKIP)
    rows = pl.ds(pl.multiple_of(base, BLOCK), BLOCK)
    pulled = dot_nt(ddrive_ref[seq, rows, :], win_ref[...])
    for r in range(0, BLOCK, SUB):
        at = pl.ds(pl.multiple_of(base + r, SUB), SUB)
        d = pulled[r : r + SUB] + skip * dlru_ref[seq, at, :].astype(F32)
        x = stream_ref[seq, at, :].astype(F32)
        centre = x - jnp.mean(x, axis=-1, keepdims=True)
        spread = jnp.mean(centre * centre, axis=-1, keepdims=True)
        inverse = lax.rsqrt(spread + 1e-05)
        hat = centre * inverse
        dhat = d * gain
        m1 = jnp.mean(dhat, axis=-1, keepdims=True)
        m2 = jnp.mean(dhat * hat, axis=-1, keepdims=True)
        out_ref[r : r + SUB, :] = (dhat - m1 - hat * m2) * inverse + cot_ref[seq, at, :].astype(F32)


def input_pass(seq, ddrive, dlru, stream, cot, small, win, earlier, after):
    seqs, length, width = stream.shape
    earlier = in_hbm(*earlier)
    return pl.pallas_call(
        lambda *refs: input_kernel(seq, *refs),
        grid=(length // BLOCK,),
        in_specs=[VMEM_SPEC] * 6 + [HBM_SPEC] * len(earlier) + specs_of(after),
        out_specs=pl.BlockSpec((None, BLOCK, width), lambda i: (seq, i, 0)),
        out_shape=pltpu.HBM((seqs, length, width), F32),
        input_output_aliases={6: 0} if earlier else {},
        compiler_params=pltpu.CompilerParams(vmem_limit_bytes=8 * MIB),
        cost_estimate=cost(4),
        name="input_pass",
    )(*kept(ddrive, dlru, stream, cot, small, win), *earlier, *placed(after))


def pack_kernel(count, *refs):
    out_ref = refs[count]
    parts = refs[count + 1 : -1]
    copies = [
        pltpu.make_async_copy(source, target, refs[-1].at[k])
        for k, (source, target) in enumerate(zip(refs[:count], parts))
    ]
    for c in copies:
        c.start()
    for c in copies:
        c.wait()
    row = 0
    for ref in parts:
        for first in range(0, ref.shape[0], 128):
            out_ref[row : row + 1, :] = ref[first : first + 128].reshape(1, 128)
            row += 1


def pack_vectors(*vectors):
    rows = sum(v.shape[0] for v in vectors) // 128
    return pl.pallas_call(
        lambda *refs: pack_kernel(len(vectors), *refs),
        in_specs=[HBM_SPEC] * len(vectors),
        out_specs=VMEM_SPEC,
        out_shape=pltpu.VMEM((rows, 128), BF16),
        scratch_shapes=[pltpu.VMEM(v.shape, BF16) for v in vectors]
        + [pltpu.SemaphoreType.DMA((len(vectors),))],
        compiler_params=pltpu.CompilerParams(vmem_limit_bytes=2 * MIB),
        name="pack_vectors",
    )(*in_hbm(*vectors))


def pair_kernel(others, place_ref, keep_ref, came_ref, *rest):
    for hop, ref in enumerate(rest[others:]):
        at = place_ref[1] ^ hop
        ref[...] = (keep_ref[at].astype(F32) + came_ref[at].astype(F32)).astype(BF16)


def pair_sum(place, keep, came, after=()):
    count = keep.shape[0]
    return pl.pallas_call(
        lambda *refs: pair_kernel(len(after), *refs),
        in_specs=[SMEM_SPEC] + [VMEM_SPEC] * 2 + specs_of(after),
        out_specs=[VMEM_SPEC] * count,
        out_shape=[pltpu.VMEM(keep.shape[1:], BF16)] * count,
        compiler_params=pltpu.CompilerParams(vmem_limit_bytes=4 * MIB),
        cost_estimate=cost(0.7),
        name="pair_sum",
    )(place, *kept(keep, came), *placed(after))


def add_kernel(count, *refs):
    total = refs[0][...].astype(F32)
    for ref in refs[1:count]:
        total += ref[...].astype(F32)
    refs[-1][...] = total.astype(BF16)


def add_up(got, after=()):
    return pl.pallas_call(
        lambda *refs: add_kernel(len(got), *refs),
        in_specs=[VMEM_SPEC] * len(got) + specs_of(after),
        out_specs=VMEM_SPEC,
        out_shape=pltpu.VMEM(got[0].shape, BF16),
        compiler_params=pltpu.CompilerParams(vmem_limit_bytes=4 * MIB),
        cost_estimate=cost(0.2),
        name="add_up",
    )(*kept(*got), *placed(after))


def unpack_kernel(count, tokens, place_ref, *refs):
    first = refs[:count]
    second = refs[count : 2 * count]
    (
        glu_ref, outr_ref, outi_ref, inr_ref, ini_ref, gain_ref, bias_ref, nu_ref, theta_ref,
        gamma_ref, skip_ref, glub_ref, rms_ref, lines,
    ) = refs[2 * count :]
    width = glu_ref.shape[1] // 2
    states = inr_ref.shape[1]
    high = glu_ref.shape[0] // count
    part = outr_ref.shape[0] // count
    for hop in range(count):
        at = place_ref[1] ^ hop
        rows = pl.ds(pl.multiple_of(at * high, high), high)
        glu_ref[rows, :] = first[hop][:high, :].astype(F32)
        inr_ref[rows, :] = second[hop][:high, :states].astype(F32)
        ini_ref[rows, :] = second[hop][:high, states:].astype(F32)
        few = pl.ds(pl.multiple_of(at * part, part), part)
        outr_ref[few, :] = first[hop][high:, :width].astype(F32)
        outi_ref[few, :] = first[hop][high:, width:].astype(F32)
        lines[pl.ds(pl.multiple_of(at * 8, 8), 8), :] = second[hop][high:, :].astype(F32)[:8]
    half, some = width // 2, states // 2
    per = 8 // count
    line = lambda k: lines[k // per * 8 : k // per * 8 + 1, k % per * half : (k % per + 1) * half]
    gain_ref[...] = line(0)
    bias_ref[...] = line(1)
    nu_ref[...] = line(2)[:, :some]
    theta_ref[...] = line(2)[:, some:]
    gamma_ref[...] = line(3)[:, :some]
    skip_ref[...] = line(4)
    glub_ref[:, :half] = line(5)
    glub_ref[:, half:] = line(6)
    rms_ref[...] = jnp.sqrt(line(7)[:, :3] / tokens)


def unpack(place, first, second, width, states, tokens):
    count = len(first)
    flat = [width // 2, width // 2, states // 2, states // 2, states // 2, width // 2, width, 3]
    return pl.pallas_call(
        lambda *refs: unpack_kernel(count, tokens, *refs),
        in_specs=[SMEM_SPEC] + [VMEM_SPEC] * (2 * count),
        out_specs=[VMEM_SPEC] * 13,
        out_shape=[
            jax.ShapeDtypeStruct((width // 2, 2 * width), F32),
            jax.ShapeDtypeStruct((states // 2, width), F32),
            jax.ShapeDtypeStruct((states // 2, width), F32),
            jax.ShapeDtypeStruct((width // 2, states), F32),
            jax.ShapeDtypeStruct((width // 2, states), F32),
        ]
        + [jax.ShapeDtypeStruct((1, n), F32) for n in flat],
        scratch_shapes=[pltpu.VMEM((8 * count, width), F32)],
        compiler_params=pltpu.CompilerParams(vmem_limit_bytes=8 * MIB),
        name="unpack",
    )(place, *first, *second)


def hops_of(ends, axis, reverse):
    count = lax.axis_size(axis)
    if count <= 4:
        return [
            lax.ppermute(
                ends,
                axis,
                [(i + hop, i) if reverse else (i, i + hop) for i in range(count - hop)],
            )
            for hop in range(1, count)
        ]
    place = lax.axis_index(axis)
    every = lax.all_gather(ends, axis)
    came = []
    for hop in range(1, count):
        source = place + hop if reverse else place - hop
        inside = (source >= 0) & (source < count)
        item = lax.dynamic_index_in_dim(every, jnp.clip(source, 0, count - 1), 0, False)
        came.append(jnp.where(inside, item, 0.0))
    return came


def swap(a):
    return lax.ppermute(a, "fsdp", [(0, 1), (1, 0)])


def swap_moves(axis, bit):
    return [(i, i ^ bit) for i in range(lax.axis_size(axis))]


def scatter_batch(pieces):
    return [pieces[0]] + [
        lax.ppermute(pieces[hop], "batch", swap_moves("batch", hop))
        for hop in range(1, len(pieces))
    ]


def share_seq(piece):
    ring = lax.axis_size("seq")
    if ring > 4:
        return [lax.psum(piece.astype(F32), "seq").astype(BF16)]
    return [piece] + [
        lax.ppermute(piece, "seq", [(i, (i + hop) % ring) for i in range(ring)])
        for hop in range(1, ring)
    ]


def gather_batch(piece):
    count = lax.axis_size("batch")
    return [piece] + [
        lax.ppermute(piece, "batch", swap_moves("batch", hop)) for hop in range(1, count)
    ]


def on_device(
    stream, norm_gain, norm_bias, in_real, in_imag, nu_log, theta_log, gamma_log, out_real,
    out_imag, skip_scale, glu_weight, glu_bias, cotangent,
):
    seqs, length, width = stream.shape
    states = 2 * nu_log.shape[0]
    batch = lax.axis_size("batch")
    place = jnp.stack([lax.axis_index("fsdp"), lax.axis_index("batch")]).astype(jnp.int32)
    vectors = pack_vectors(
        norm_gain, norm_bias, skip_scale, glu_bias, nu_log, theta_log, gamma_log
    )
    into = [in_real, swap(in_real), in_imag, swap(in_imag)]
    others = [swap(glu_weight), swap(out_real), swap(out_imag)]
    (
        normed, sums, ends, p, q, small, win, wback, square, stream_kept, cot_kept, *own,
    ) = norm_pass(
        place, stream, cotangent, into, [glu_weight, out_real, out_imag], [vectors, swap(vectors)]
    )
    halves = [a for pair_of in zip(own, others) for a in pair_of]
    came = hops_of(ends, "seq", False)
    mixed, back, state, dlru, starts, keep, send, acc, gacc = block_pass(
        place, batch, sums, normed, stream_kept, cot_kept, p, small, halves, came
    )
    later = hops_of(starts, "seq", True)
    pieces = pair_sum(place, keep, swap(send), later)
    first = scatter_batch(pieces)
    ddrive, keep, send = adjoint_pass(
        place, batch, back, state, normed, wback, q, small, square, acc, gacc, later, pieces
    )
    send, first = lax.optimization_barrier((send, add_up(first, [send])))
    pieces = pair_sum(place, keep, swap(send))
    second = scatter_batch(pieces)
    last = lambda seq, earlier, after: input_pass(
        seq, ddrive, dlru, stream_kept, cot_kept, small, wback, earlier, after
    )
    first = share_seq(first)
    grads = ()
    for seq in range(seqs - 1):
        grads = (last(seq, grads, [first[0]]),)
    second = add_up(second, grads)
    second = share_seq(second)
    grads = (last(seqs - 1, grads, [second[0]]),)
    second = add_up(second, grads)
    second = gather_batch(second)
    first = gather_batch(add_up(first, [second[0]]))
    grad_stream = grads[0]
    tokens = stream.size * batch * lax.axis_size("seq") * lax.axis_size("fsdp")
    (
        glu, out_r, out_i, in_r, in_i, gain, bias, nu, theta, gamma, skip, glub, rms,
    ) = unpack(place, first, second, width, states, float(tokens))
    flat = lambda a: a.reshape(-1)
    return (
        mixed, grad_stream, flat(gain), flat(bias), in_r, in_i, flat(nu), flat(theta), flat(gamma),
        out_r, out_i, flat(skip), glu, flat(glub), flat(rms),
    )


def solution(mesh):
    tokens = P(("batch", "fsdp"), "seq", None)
    vector = P("fsdp")
    matrix = P("fsdp", None)
    weights = (
        vector, vector, matrix, matrix, vector, vector, vector, matrix, matrix, vector, matrix,
        vector,
    )
    return jax.shard_map(
        on_device,
        mesh=mesh,
        in_specs=(tokens,) + weights + (tokens,),
        out_specs=(tokens, tokens) + weights + (P(),),
        check_vma=False,
    )
```

```python
import functools

import jax
import jax.numpy as jnp
from jax import lax
from jax.experimental import pallas as pl
from jax.experimental.pallas import tpu as pltpu
from jax.sharding import PartitionSpec as P

F32 = jnp.float32
BF16 = jnp.bfloat16
HIGHEST = lax.Precision.HIGHEST
CHUNK = 128
HALF = 64
BLOCK = 512
SUB = 64
TILE = 256
GELU_C = 0.7978845608028654
GELU_K = 0.044715
MIB = 1024 * 1024


def dot_nn(a, b):
    return jnp.dot(a, b, preferred_element_type=F32)


def dot_tn(a, b):
    return lax.dot_general(a, b, (((0,), (0,)), ((), ())), preferred_element_type=F32)


def dot_nt(a, b):
    return lax.dot_general(a, b, (((1,), (1,)), ((), ())), preferred_element_type=F32)


def dot_nt_wide(a, b):
    return lax.dot_general(
        a, b, (((1,), (1,)), ((), ())), precision=HIGHEST, preferred_element_type=F32
    )


def cmul(ar, ai, br, bi):
    return ar * br - ai * bi, ar * bi + ai * br


def fold(v):
    return jnp.sum(v.reshape(v.shape[0] // 8, 8, v.shape[1]), axis=0)


def fold_low(v):
    rows = v.shape[0] // 4
    v = (v[:rows] + v[rows : 2 * rows]) + (v[2 * rows : 3 * rows] + v[3 * rows :])
    return fold(v.astype(F32))


def split_store(stack, k, zr, zi):
    states = zr.shape[1]
    for part, v in enumerate((zr, zi)):
        columns = pl.ds(part * states, states)
        high = v.astype(BF16)
        stack[k, :CHUNK, columns] = high
        stack[k, CHUNK:, columns] = (v - high.astype(F32)).astype(BF16)


def fill_triangle(tri, upper):
    row = lax.broadcasted_iota(jnp.int32, (CHUNK, CHUNK), 0)
    column = lax.broadcasted_iota(jnp.int32, (CHUNK, CHUNK), 1)
    inside = (column >= row) if upper else (column <= row)
    ones = jnp.where(inside, 1.0, 0.0).astype(BF16)
    tri[:, :CHUNK] = ones
    tri[:, CHUNK:] = ones


ROW_STEP = 0
ROW_LAST = 1
ROW_ENTER = 2
ROW_FIRST = 3
ROW_BACK = 4
ROW_WHOLE = 5
ROW_SCALE = 6
ROW_RATE = 7
ROW_GAIN = 8
ROW_BIAS = 9
ROW_SKIP = 10
ROW_GLU = 11
TABLE_ROWS = 16


def pair(ref, row, states):
    return ref[row : row + 1, :states], ref[row : row + 1, states:]


def row_of(ref, row):
    return ref[row : row + 1, :]


def fill_tables(me, own_ref, other_ref, p_ref, q_ref, small_ref, length):
    states = q_ref.shape[1] // 2
    width = q_ref.shape[1]
    own = own_ref[...].astype(F32)
    other = other_ref[...].astype(F32)
    low = jnp.where(me == 0, own, other)
    high = jnp.where(me == 0, other, own)

    def both(first, count):
        rows = [h[first + i : first + i + 1] for h in (low, high) for i in range(count)]
        return jnp.concatenate(rows, axis=1)

    small_ref[...] = jnp.zeros_like(small_ref)
    for row, first in ((ROW_GAIN, 0), (ROW_BIAS, 2), (ROW_SKIP, 4)):
        small_ref[row : row + 1, :] = both(first, 2)
    glu = both(6, 4)
    small_ref[ROW_GLU : ROW_GLU + 1, :] = glu[:, :width]
    small_ref[ROW_GLU + 1 : ROW_GLU + 2, :] = glu[:, width:]
    decay = jnp.exp(both(10, 1))
    rotation = jnp.exp(both(11, 1))
    scale = jnp.exp(both(12, 1))
    steps = (lax.broadcasted_iota(jnp.int32, (CHUNK, states), 0) - HALF).astype(F32)
    turn = steps * rotation
    cos = jnp.cos(turn)
    sin = jnp.sin(turn)
    grow = jnp.exp(-steps * decay)
    p_ref[:, :states] = grow * cos
    p_ref[:, states:] = grow * sin
    shrink = scale * jnp.exp(steps * decay)
    q_ref[:, :states] = shrink * cos
    q_ref[:, states:] = -shrink * sin
    counts = {
        ROW_STEP: CHUNK,
        ROW_LAST: CHUNK - 1 - HALF,
        ROW_ENTER: HALF + 1,
        ROW_FIRST: HALF,
        ROW_BACK: CHUNK - HALF,
        ROW_WHOLE: length,
    }
    assert sorted(counts) == list(range(6))
    index = lax.broadcasted_iota(jnp.int32, (8, states), 0)
    count = jnp.zeros((8, states), F32)
    for row, steps in counts.items():
        count = jnp.where(index == row, float(steps), count)
    size = jnp.exp(-count * decay)
    small_ref[:6, :states] = (size * jnp.cos(count * rotation))[:6]
    small_ref[:6, states:] = (size * jnp.sin(count * rotation))[:6]
    small_ref[ROW_SCALE : ROW_SCALE + 1, :states] = scale
    small_ref[ROW_SCALE : ROW_SCALE + 1, states:] = 1.0 / scale
    small_ref[ROW_RATE : ROW_RATE + 1, :states] = decay
    small_ref[ROW_RATE : ROW_RATE + 1, states:] = rotation


def join_halves(me, whole, own, other, columns=slice(None)):
    rows = own.shape[0]
    whole[pl.ds(pl.multiple_of(me * rows, rows), rows), columns] = own[...]
    whole[pl.ds(pl.multiple_of((1 - me) * rows, rows), rows), columns] = other[...]


def cost(microseconds):
    return pl.CostEstimate(
        flops=0, transcendentals=0, bytes_accessed=int(microseconds * 3.6e6)
    )


def norm_kernel(
    length, place_ref, stream_hbm, cot_hbm, inr_hbm, ini_hbm, glu_hbm, outr_hbm, outi_hbm,
    vec_own, vec_other, inr_other, ini_other,
    normed_ref, sums_ref, end_ref, p_ref, q_ref, small_ref, win_ref, wback_ref, square_ref,
    stream_ref, cot_ref, glu_ref, outr_ref, outi_ref,
    stack, tri, inr_own, ini_own, sems,
):
    states = q_ref.shape[1] // 2
    seqs = stream_ref.shape[0]
    every = range(seqs)
    copy = lambda source, target, k: pltpu.make_async_copy(source, target, sems.at[k])
    weights = [copy(inr_hbm, inr_own, 0), copy(ini_hbm, ini_own, 1)]
    onward = [
        copy(source, target, 2 + k)
        for k, (source, target) in enumerate(
            ((glu_hbm, glu_ref), (outr_hbm, outr_ref), (outi_hbm, outi_ref), (cot_hbm, cot_ref))
        )
    ]
    blocks = []
    for step in range(length // BLOCK):
        at = (slice(None), pl.ds(step * BLOCK, BLOCK))
        blocks.append(copy(stream_hbm.at[at], stream_ref.at[at], 6 + step))
    for c in blocks[:1] + weights + blocks[1:] + onward:
        c.start()
    me = place_ref[0]
    fill_tables(me, vec_own, vec_other, p_ref, q_ref, small_ref, length)
    fill_triangle(tri, False)
    for c in weights:
        c.wait()
    join_halves(me, win_ref, inr_own, inr_other, slice(0, states))
    join_halves(me, win_ref, ini_own, ini_other, slice(states, 2 * states))
    wback_ref[:, :states] = win_ref[:, :states]
    wback_ref[:, states:] = -win_ref[:, states:]

    gain = row_of(small_ref, ROW_GAIN)
    bias = row_of(small_ref, ROW_BIAS)
    step_r, step_i = pair(small_ref, ROW_STEP, states)
    last_r, last_i = pair(small_ref, ROW_LAST, states)
    squares = jnp.zeros((8, 1), F32)
    ends = [(jnp.zeros((1, states), F32),) * 2] * seqs
    for step, block in enumerate(blocks):
        base = step * BLOCK
        rows = pl.ds(base, BLOCK)
        block.wait()
        for r in range(0, BLOCK, SUB):
            for seq in every:
                at = pl.ds(base + r, SUB)
                x = stream_ref[seq, at, :].astype(F32)
                mean = jnp.mean(x, axis=-1, keepdims=True)
                centre = x - mean
                spread = jnp.mean(centre * centre, axis=-1, keepdims=True)
                squares += fold(mean * mean + spread)
                normed_ref[seq, at, :] = (
                    centre * lax.rsqrt(spread + 1e-05) * gain + bias
                ).astype(BF16)
        left = jnp.concatenate([normed_ref[seq, rows, :] for seq in every], axis=0)
        drive = dot_nn(left, win_ref[...])
        for k in range(BLOCK // CHUNK):
            for seq in every:
                first = seq * BLOCK + k * CHUNK
                part = drive[first : first + CHUNK]
                zr, zi = cmul(
                    part[:, :states], part[:, states:], q_ref[:, :states], q_ref[:, states:]
                )
                slot = stack.at[step % 2, seq]
                split_store(slot, k, zr, zi)
                s = dot_nn(tri[...], slot[k])
                sums_ref[seq, pl.ds(base + k * CHUNK, CHUNK), :] = s
                er, ei = cmul(s[CHUNK - 1 :, :states], s[CHUNK - 1 :, states:], last_r, last_i)
                nr, ni = cmul(*ends[seq], step_r, step_i)
                ends[seq] = nr + er, ni + ei
    square_ref[...] = jnp.broadcast_to(squares, square_ref.shape)
    for seq in every:
        end_ref[seq, :, :states], end_ref[seq, :, states:] = ends[seq]
    for c in onward:
        c.wait()


HBM_SPEC = pl.BlockSpec(memory_space=pltpu.HBM)
VMEM_SPEC = pl.BlockSpec(memory_space=pltpu.VMEM)
SMEM_SPEC = pl.BlockSpec(memory_space=pltpu.SMEM)


def kept(*arrays):
    return [pltpu.with_memory_space_constraint(a, pltpu.VMEM) for a in arrays]


def large(a):
    return a.size * a.dtype.itemsize > 2 * MIB


def specs_of(arrays):
    return [HBM_SPEC if large(a) else VMEM_SPEC for a in arrays]


def placed(arrays):
    return [in_hbm(a)[0] if large(a) else kept(a)[0] for a in arrays]


def in_hbm(*arrays):
    return [pltpu.with_memory_space_constraint(a, pltpu.HBM) for a in arrays]


def norm_pass(place, stream, cot, into, onward, vectors):
    seqs, length, width = stream.shape
    half, states = into[0].shape
    states2 = 2 * states
    return pl.pallas_call(
        lambda *refs: norm_kernel(length, *refs),
        in_specs=[SMEM_SPEC] + [HBM_SPEC] * 7 + [VMEM_SPEC] * 4,
        out_specs=[VMEM_SPEC] * 14,
        out_shape=[
            pltpu.VMEM((seqs, length, width), BF16),
            pltpu.VMEM((seqs, length, states2), F32),
            pltpu.VMEM((seqs, 1, states2), F32),
            pltpu.VMEM((CHUNK, states2), F32),
            pltpu.VMEM((CHUNK, states2), F32),
            pltpu.VMEM((TABLE_ROWS, states2), F32),
            pltpu.VMEM((width, states2), BF16),
            pltpu.VMEM((width, states2), BF16),
            pltpu.VMEM((8, 128), F32),
            pltpu.VMEM(stream.shape, BF16),
            pltpu.VMEM(cot.shape, BF16),
        ]
        + [pltpu.VMEM(a.shape, BF16) for a in onward],
        scratch_shapes=[
            pltpu.VMEM((2, seqs, BLOCK // CHUNK, 2 * CHUNK, states2), BF16),
            pltpu.VMEM((CHUNK, 2 * CHUNK), BF16),
            pltpu.VMEM((half, states), BF16),
            pltpu.VMEM((half, states), BF16),
            pltpu.SemaphoreType.DMA((length // BLOCK + 6,)),
        ],
        compiler_params=pltpu.CompilerParams(vmem_limit_bytes=21 * MIB),
        cost_estimate=cost(9),
        name="norm_pass",
    )(
        place,
        *in_hbm(stream, cot, into[0], into[2], *onward),
        *kept(*vectors, into[1], into[3]),
    )


def entering(carry, came, seq, small_ref, states):
    whole_r, whole_i = pair(small_ref, ROW_WHOLE, states)
    total_r = came[0][seq, :, :states]
    total_i = came[0][seq, :, states:]
    power_r, power_i = whole_r, whole_i
    for ref in came[1:]:
        gr, gi = cmul(ref[seq, :, :states], ref[seq, :, states:], power_r, power_i)
        total_r, total_i = total_r + gr, total_i + gi
        power_r, power_i = cmul(power_r, power_i, whole_r, whole_i)
    carry[0:1, :states] = total_r
    carry[0:1, states:] = total_i


def block_kernel(
    hops, place_ref, _, normed_ref, stream_ref, cot_ref, p_ref, small_ref, glu_own, glu_other,
    outr_own, outr_other, outi_own, outi_other, *rest,
):
    came = rest[:hops]
    (
        mixed_hbm, back_ref, state_ref, dlru_ref, start_ref, keep_ref, send_ref, acc_ref, gacc_ref,
        carry, stack, tri, act, dproj, slope, mixed, wglu, wout, dglu, dout, sems,
    ) = rest[hops:]
    states = p_ref.shape[1] // 2
    seqs, _, width = stream_ref.shape
    me = place_ref[0]
    join_halves(me, wglu, glu_own, glu_other)
    join_halves(me, wout.at[pl.ds(0, states)], outr_own, outr_other)
    join_halves(me, wout.at[pl.ds(states, states)], outi_own, outi_other)
    fill_triangle(tri, True)
    acc_ref[...] = jnp.zeros_like(acc_ref)
    gacc_ref[...] = jnp.zeros_like(gacc_ref)
    dglu[...] = jnp.zeros_like(dglu)
    dout[...] = jnp.zeros_like(dout)
    for seq in range(seqs):
        entering(carry.at[seq], came, seq, small_ref, states)
        carry[seq, 1:2, :] = jnp.zeros_like(carry[seq, 1:2, :])
        carry[seq, 2:3, :states] = jnp.ones_like(carry[seq, 2:3, :states])
        carry[seq, 2:3, states:] = jnp.zeros_like(carry[seq, 2:3, states:])

    step_r, step_i = pair(small_ref, ROW_STEP, states)
    last_r, last_i = pair(small_ref, ROW_LAST, states)
    enter_r, enter_i = pair(small_ref, ROW_ENTER, states)
    first_r, first_i = pair(small_ref, ROW_FIRST, states)
    skip = row_of(small_ref, ROW_SKIP)
    value_bias = row_of(small_ref, ROW_GLU)
    gate_bias = row_of(small_ref, ROW_GLU + 1)
    def mixed_copy(step):
        at = pl.ds(step * BLOCK, BLOCK)
        return pltpu.make_async_copy(
            mixed.at[step % 2], mixed_hbm.at[:, at, :], sems.at[step % 2]
        )

    steps = stream_ref.shape[1] // BLOCK
    for step in range(steps):
        base = step * BLOCK
        slot = step % 2
        rows = pl.ds(base, BLOCK)
        pieces = [
            (slice(r, r + SUB), pl.ds(base + r, SUB)) for r in range(0, BLOCK, SUB)
        ]
        chunks = [
            (k, pl.ds(base + k * CHUNK, CHUNK)) for k in range(BLOCK // CHUNK)
        ]
        zeros = jnp.zeros((8, width), F32)
        tiles = lambda count: [pl.ds(n, TILE) for n in range(0, count, TILE)]
        made = {}
        folds = {}

        def make_states(seq):
            def part(k, at):
                cr, ci = made["carry", seq]
                qr, qi = cmul(cr, ci, enter_r, enter_i)
                sr = back_ref[seq, at, :states]
                si = back_ref[seq, at, states:]
                er, ei = cmul(sr[CHUNK - 1 :], si[CHUNK - 1 :], last_r, last_i)
                nr, ni = cmul(cr, ci, step_r, step_i)
                made["carry", seq] = nr + er, ni + ei
                hr, hi = cmul(sr + qr, si + qi, p_ref[:, :states], p_ref[:, states:])
                state_ref[seq, at, :states] = hr.astype(BF16)
                state_ref[seq, at, states:] = (-hi).astype(BF16)

            def first():
                made["carry", seq] = carry[seq, 0:1, :states], carry[seq, 0:1, states:]

            def last():
                carry[seq, 0:1, :states], carry[seq, 0:1, states:] = made["carry", seq]

            return [first] + [functools.partial(part, *c) for c in chunks] + [last]

        every = range(seqs)
        both = lambda one: jnp.concatenate([one(seq) for seq in every], axis=0)

        def products(name, left, right, columns, turned=False):
            def part(n):
                if turned:
                    v = dot_nt(both(left), right[n, :])
                else:
                    v = dot_nn(both(left), right[:, n])
                v = v.astype(BF16) if name == "dact" else v
                for seq in every:
                    made.setdefault((name, seq), []).append(v[seq * BLOCK : (seq + 1) * BLOCK])

            return [functools.partial(part, n) for n in tiles(columns)]

        def taken(name, seq, r, first=0, count=None):
            parts = made[name, seq][first:count]
            return jnp.concatenate([v[r] for v in parts], axis=1)

        def gather(name, v):
            folds[name] = folds[name] + v if name in folds else v

        def read_out():
            return products("lru", lambda seq: state_ref[seq, rows, :], wout, width)

        def activate(seq):
            def part(r, at):
                readout = taken("lru", seq, r)
                lru = readout + skip * normed_ref[seq, at, :].astype(F32)
                lru2 = lru * lru
                gather("lru", fold(lru2))
                gate = 0.5 + 0.5 * jnp.tanh(lru * (GELU_C + GELU_C * GELU_K * lru2))
                gelu = lru * gate
                slope[seq, r, :] = (gate + (gelu - gelu * gate) * (
                    2 * GELU_C + 6 * GELU_C * GELU_K * lru2
                )).astype(BF16)
                act[seq, r, :] = gelu.astype(BF16)

            return [functools.partial(part, *c) for c in pieces]

        def project():
            return products("projected", lambda seq: act[seq], wglu, 2 * width)

        def branch_out(seq):
            def part(r, at):
                middle = width // TILE
                value = taken("projected", seq, r, 0, middle) + value_bias
                gate = taken("projected", seq, r, middle) + gate_bias
                gate = 0.5 + 0.5 * jnp.tanh(0.5 * gate)
                branch = value * gate
                mixed[slot, seq, r, :] = (stream_ref[seq, at, :].astype(F32) + branch).astype(BF16)
                gather("branch", fold(branch * branch))
                cot = cot_ref[seq, at, :].astype(F32)
                part = cot * branch
                dvalue = (cot * gate).astype(BF16)
                dgate = (part - part * gate).astype(BF16)
                dproj[seq, r, :width] = dvalue
                dproj[seq, r, width:] = dgate
                gather("value", fold_low(dvalue))
                gather("gate", fold_low(dgate))

            return [functools.partial(part, *c) for c in pieces]

        def project_back():
            return products("dact", lambda seq: dproj[seq], wglu, width, True)

        def activate_back(seq):
            def part(r, at):
                dlru = taken("dact", seq, r) * slope[seq, r, :]
                dlru_ref[seq, at, :] = dlru
                gather("dlru", fold_low(dlru))
                gather("skip", fold_low(dlru * normed_ref[seq, at, :]))

            return [functools.partial(part, *c) for c in pieces]

        def read_out_back():
            return products("pull", lambda seq: dlru_ref[seq, rows, :], wout, 2 * states, True)

        def glu_back():
            def part(n):
                dglu[:, n] += dot_tn(both(lambda seq: act[seq]), both(lambda seq: dproj[seq, :, n]))

            return [functools.partial(part, n) for n in tiles(2 * width)]

        def out_back():
            def part(n):
                dout[:, n] += dot_tn(
                    both(lambda seq: state_ref[seq, rows, :]), both(lambda seq: dlru_ref[seq, rows, n])
                )

            return [functools.partial(part, n) for n in tiles(width)]

        def turn(seq):
            def part(k, at):
                pull = taken("pull", seq, slice(k * CHUNK, (k + 1) * CHUNK))
                zr, zi = cmul(pull[:, :states], pull[:, states:], p_ref[:, :states], p_ref[:, states:])
                split_store(stack.at[seq], k, zr, zi)

            return [functools.partial(part, *c) for c in chunks]

        def sum_back(seq):
            def part(k, at):
                ar, ai = carry[seq, 1:2, :states], carry[seq, 1:2, states:]
                wr, wi = carry[seq, 2:3, :states], carry[seq, 2:3, states:]
                back = dot_nn(tri[...], stack[seq, k])
                back_ref[seq, at, :] = back
                fr, fi = cmul(back[0:1, :states], back[0:1, states:], first_r, first_i)
                gr, gi = cmul(fr, fi, wr, wi)
                ar, ai = ar + gr, ai + gi
                wr, wi = cmul(wr, wi, step_r, step_i)
                carry[seq, 1:2, :states] = ar
                carry[seq, 1:2, states:] = ai
                carry[seq, 2:3, :states] = wr
                carry[seq, 2:3, states:] = wi
                start_ref[seq, :, :states] = ar
                start_ref[seq, :, states:] = ai

            return [functools.partial(part, *c) for c in chunks]

        def run(*lists):
            parts = [(i / len(one), part) for one in lists for i, part in enumerate(one)]
            for _, part in sorted(parts, key=lambda item: item[0]):
                part()

        run(*[make_states(seq) for seq in every])
        run(read_out())
        run(*[activate(seq) for seq in every])
        run(project())
        if step >= 2:
            mixed_copy(step - 2).wait()
        run(*[branch_out(seq) for seq in every])
        mixed_copy(step).start()
        run(project_back())
        run(*[activate_back(seq) for seq in every], glu_back())
        run(read_out_back())
        run(*[turn(seq) for seq in every], out_back())
        run(*[sum_back(seq) for seq in every])
        for row, name in enumerate(("lru", "branch", "dlru", "skip")):
            acc_ref[8 * row : 8 * row + 8, :] += folds[name]
        for row, name in enumerate(("value", "gate")):
            gacc_ref[8 * row : 8 * row + 8, :] += folds[name]

    for step in range(max(steps - 2, 0), steps):
        mixed_copy(step).wait()
    batch, height, _ = keep_ref.shape
    high = width // (2 * batch)
    part = height - high
    for ref, f in ((keep_ref, place_ref[0]), (send_ref, 1 - place_ref[0])):
        for b in range(batch):
            first = pl.multiple_of((f * batch + b) * high, high)
            ref[b, :high, :] = dglu[pl.ds(first, high), :].astype(BF16)
            first = pl.multiple_of((f * batch + b) * part, part)
            ref[b, high:, :width] = dout[pl.ds(first, part), :].astype(BF16)
            ref[b, high:, width:] = dout[pl.ds(states + first, part), :].astype(BF16)


def block_pass(place, batch, sums, normed, stream, cot, p, small, halves, came):
    seqs, length, width = stream.shape
    states2 = p.shape[1]
    height = width // (2 * batch) + states2 // (4 * batch)
    return pl.pallas_call(
        lambda *refs: block_kernel(len(came), *refs),
        in_specs=[SMEM_SPEC] + [VMEM_SPEC] * (12 + len(came)),
        out_specs=[HBM_SPEC] + [VMEM_SPEC] * 8,
        out_shape=[
            pltpu.HBM((seqs, length, width), BF16),
            pltpu.VMEM((seqs, length, states2), F32),
            pltpu.VMEM((seqs, length, states2), BF16),
            pltpu.VMEM((seqs, length, width), BF16),
            jax.ShapeDtypeStruct((seqs, 1, states2), F32),
            pltpu.VMEM((batch, height, 2 * width), BF16),
            pltpu.VMEM((batch, height, 2 * width), BF16),
            pltpu.VMEM((32, width), F32),
            pltpu.VMEM((16, width), F32),
        ],
        scratch_shapes=[
            pltpu.VMEM((seqs, 8, states2), F32),
            pltpu.VMEM((seqs, BLOCK // CHUNK, 2 * CHUNK, states2), BF16),
            pltpu.VMEM((CHUNK, 2 * CHUNK), BF16),
            pltpu.VMEM((seqs, BLOCK, width), BF16),
            pltpu.VMEM((seqs, BLOCK, 2 * width), BF16),
            pltpu.VMEM((seqs, BLOCK, width), BF16),
            pltpu.VMEM((2, seqs, BLOCK, width), BF16),
            pltpu.VMEM((width, 2 * width), BF16),
            pltpu.VMEM((states2, width), BF16),
            pltpu.VMEM((width, 2 * width), F32),
            pltpu.VMEM((states2, width), F32),
            pltpu.SemaphoreType.DMA((2,)),
        ],
        input_output_aliases={1: 1},
        compiler_params=pltpu.CompilerParams(vmem_limit_bytes=21 * MIB),
        cost_estimate=cost(28),
        name="block_pass",
    )(place, *kept(sums, normed, stream, cot, p, small, *halves, *came))


def adjoint_kernel(
    hops, others, place_ref, back_ref, _, normed_ref, win_ref, q_ref, small_ref, square_ref, acc_ref, gacc_ref,
    *rest,
):
    came = rest[:hops]
    ddrive_ref, keep_ref, send_ref, carry, din = rest[hops + others :]
    states = q_ref.shape[1] // 2
    seqs, length, _ = normed_ref.shape
    every = range(seqs)
    first_r, first_i = pair(small_ref, ROW_FIRST, states)
    back_r, back_i = pair(small_ref, ROW_BACK, states)
    carries = []
    for seq in every:
        entering(carry, came, seq, small_ref, states)
        carries.append((carry[0:1, :states], carry[0:1, states:]))
    real_sum = imag_sum = real_total = imag_total = jnp.zeros((8, states), F32)
    for base in reversed(range(0, length, BLOCK)):
        for k in reversed(range(BLOCK // CHUNK)):
            for seq in every:
                at = pl.ds(base + k * CHUNK, CHUNK)
                qr, qi = cmul(*carries[seq], back_r, back_i)
                vr = back_ref[seq, at, :states] + qr
                vi = back_ref[seq, at, states:] + qi
                carries[seq] = cmul(vr[0:1], vi[0:1], first_r, first_i)
                ar, ai = cmul(vr, vi, q_ref[:, :states], q_ref[:, states:])
                hr = ddrive_ref[seq, at, :states]
                hi = ddrive_ref[seq, at, states:]
                lr, li = ar.astype(BF16), ai.astype(BF16)
                real_sum += fold((lr * hr).astype(F32) + (li * hi).astype(F32))
                imag_sum += fold((lr * hi).astype(F32) - (li * hr).astype(F32))
                real_total += fold_low(lr)
                imag_total += fold_low(li)
                ddrive_ref[seq, at, :states] = lr
                ddrive_ref[seq, at, states:] = li
        rows = pl.ds(base, BLOCK)
        product = dot_tn(
            jnp.concatenate([normed_ref[seq, rows, :] for seq in every], axis=0),
            jnp.concatenate([ddrive_ref[seq, rows, :] for seq in every], axis=0),
        )
        if base == length - BLOCK:
            din[...] = product
        else:
            din[...] += product
    width = din.shape[0]
    gain = row_of(small_ref, ROW_GAIN)
    bias = row_of(small_ref, ROW_BIAS)
    skip = row_of(small_ref, ROW_SKIP)
    weight = win_ref[...].astype(F32)
    grad = din[...]
    in_r, in_i = weight[:, :states], weight[:, states:]
    g_r, g_i = grad[:, :states], grad[:, states:]
    x_r = jnp.sum(g_r * in_r + g_i * in_i, axis=0, keepdims=True)
    x_i = jnp.sum(g_r * in_i - g_i * in_r, axis=0, keepdims=True)
    inverse = small_ref[ROW_SCALE : ROW_SCALE + 1, states:]
    column = lambda v: jnp.sum(v, axis=0, keepdims=True)
    d_r = column(real_sum) * inverse - x_r
    d_i = column(imag_sum) * inverse - x_i
    decay, rotation = pair(small_ref, ROW_RATE, states)
    gathered = dot_nt_wide(jnp.ones((8, 2 * states), F32), weight * grad)[0:1]
    total = jnp.broadcast_to(jnp.concatenate([column(real_total), column(imag_total)], axis=1), (8, 2 * states))
    d_lru = column(acc_ref[16:24, :])
    d_skip = column(acc_ref[24:32, :])
    d_bias = dot_nt_wide(total, weight)[0:1] + skip * d_lru
    d_gain = (gathered + skip * d_skip - bias * d_bias) / gain
    d_nu = -decay * d_r
    d_theta = rotation * d_i
    d_values = column(gacc_ref[0:8, :])
    d_gates = column(gacc_ref[8:16, :])
    lane = lax.broadcasted_iota(jnp.int32, (1, width // 2), 1)
    squares = jnp.zeros((1, width // 2), F32)
    sums = (
        width * jnp.sum(square_ref[:, 0:1]), jnp.sum(acc_ref[0:8, :]), jnp.sum(acc_ref[8:16, :]),
    )
    for place, v in enumerate(sums):
        squares = jnp.where(lane == place, v, squares)
    half, some = width // 2, states // 2
    batch, height, _ = keep_ref.shape
    high = width // (2 * batch)
    me = place_ref[0]

    def chosen(f, low, up):
        return jnp.where(f == 0, low, up)

    for ref, f in ((keep_ref, me), (send_ref, 1 - me)):
        wide = lambda v: chosen(f, v[:, :half], v[:, half:])
        thin = lambda v: chosen(f, v[:, :some], v[:, some:])
        d_glu = chosen(f, d_values, d_gates)
        lines = (
            wide(d_gain),
            wide(d_bias),
            jnp.concatenate([thin(d_nu), thin(d_theta)], axis=1),
            jnp.concatenate([thin(x_r), jnp.zeros((1, some), F32)], axis=1),
            wide(d_skip),
            d_glu[:, :half],
            d_glu[:, half:],
            squares,
        )
        for b in range(batch):
            first = pl.multiple_of((f * batch + b) * high, high)
            ref[b, :high, :states] = din[pl.ds(first, high), :states].astype(BF16)
            ref[b, :high, states:] = (-din[pl.ds(first, high), states:]).astype(BF16)
            line = jnp.concatenate(lines[b * 8 // batch : (b + 1) * 8 // batch], axis=1)
            line = jnp.broadcast_to(line, (height - high, width)).astype(BF16)
            ref[b, high:, :] = line


def adjoint_pass(
    place, batch, back, state, normed, wback, q, small, square, acc, gacc, came, after
):
    seqs, length, width = normed.shape
    states2 = q.shape[1]
    return pl.pallas_call(
        lambda *refs: adjoint_kernel(len(came), len(after), *refs),
        in_specs=[SMEM_SPEC] + [VMEM_SPEC] * (9 + len(came)) + specs_of(after),
        out_specs=[VMEM_SPEC] * 3,
        out_shape=[
            pltpu.VMEM((seqs, length, states2), BF16),
            pltpu.VMEM((batch, width // (2 * batch) + 16, states2), BF16),
            pltpu.VMEM((batch, width // (2 * batch) + 16, states2), BF16),
        ],
        scratch_shapes=[
            pltpu.VMEM((8, states2), F32),
            pltpu.VMEM((width, states2), F32),
        ],
        input_output_aliases={2: 0},
        compiler_params=pltpu.CompilerParams(vmem_limit_bytes=8 * MIB),
        cost_estimate=cost(7),
        name="adjoint_pass",
    )(place, *kept(back, state, normed, wback, q, small, square, acc, gacc, *came), *placed(after))


def input_kernel(seq, ddrive_ref, dlru_ref, stream_ref, cot_ref, small_ref, win_ref, *rest):
    out_ref = rest[-1]
    base = pl.program_id(0) * BLOCK
    gain = row_of(small_ref, ROW_GAIN)
    skip = row_of(small_ref, ROW_SKIP)
    rows = pl.ds(pl.multiple_of(base, BLOCK), BLOCK)
    pulled = dot_nt(ddrive_ref[seq, rows, :], win_ref[...])
    for r in range(0, BLOCK, SUB):
        at = pl.ds(pl.multiple_of(base + r, SUB), SUB)
        d = pulled[r : r + SUB] + skip * dlru_ref[seq, at, :].astype(F32)
        x = stream_ref[seq, at, :].astype(F32)
        centre = x - jnp.mean(x, axis=-1, keepdims=True)
        spread = jnp.mean(centre * centre, axis=-1, keepdims=True)
        inverse = lax.rsqrt(spread + 1e-05)
        hat = centre * inverse
        dhat = d * gain
        m1 = jnp.mean(dhat, axis=-1, keepdims=True)
        m2 = jnp.mean(dhat * hat, axis=-1, keepdims=True)
        out_ref[r : r + SUB, :] = (dhat - m1 - hat * m2) * inverse + cot_ref[seq, at, :].astype(F32)


def input_pass(seq, ddrive, dlru, stream, cot, small, win, earlier, after):
    seqs, length, width = stream.shape
    earlier = in_hbm(*earlier)
    return pl.pallas_call(
        lambda *refs: input_kernel(seq, *refs),
        grid=(length // BLOCK,),
        in_specs=[VMEM_SPEC] * 6 + [HBM_SPEC] * len(earlier) + specs_of(after),
        out_specs=pl.BlockSpec((None, BLOCK, width), lambda i: (seq, i, 0)),
        out_shape=pltpu.HBM((seqs, length, width), F32),
        input_output_aliases={6: 0} if earlier else {},
        compiler_params=pltpu.CompilerParams(vmem_limit_bytes=8 * MIB),
        cost_estimate=cost(4),
        name="input_pass",
    )(*kept(ddrive, dlru, stream, cot, small, win), *earlier, *placed(after))


def pack_kernel(count, *refs):
    out_ref = refs[count]
    parts = refs[count + 1 : -1]
    copies = [
        pltpu.make_async_copy(source, target, refs[-1].at[k])
        for k, (source, target) in enumerate(zip(refs[:count], parts))
    ]
    for c in copies:
        c.start()
    for c in copies:
        c.wait()
    row = 0
    for ref in parts:
        for first in range(0, ref.shape[0], 128):
            out_ref[row : row + 1, :] = ref[first : first + 128].reshape(1, 128)
            row += 1


def pack_vectors(*vectors):
    rows = sum(v.shape[0] for v in vectors) // 128
    return pl.pallas_call(
        lambda *refs: pack_kernel(len(vectors), *refs),
        in_specs=[HBM_SPEC] * len(vectors),
        out_specs=VMEM_SPEC,
        out_shape=pltpu.VMEM((rows, 128), BF16),
        scratch_shapes=[pltpu.VMEM(v.shape, BF16) for v in vectors]
        + [pltpu.SemaphoreType.DMA((len(vectors),))],
        compiler_params=pltpu.CompilerParams(vmem_limit_bytes=2 * MIB),
        name="pack_vectors",
    )(*in_hbm(*vectors))


def pair_kernel(others, place_ref, keep_ref, came_ref, *rest):
    for hop, ref in enumerate(rest[others:]):
        at = place_ref[1] ^ hop
        ref[...] = (keep_ref[at].astype(F32) + came_ref[at].astype(F32)).astype(BF16)


def pair_sum(place, keep, came, after=()):
    count = keep.shape[0]
    return pl.pallas_call(
        lambda *refs: pair_kernel(len(after), *refs),
        in_specs=[SMEM_SPEC] + [VMEM_SPEC] * 2 + specs_of(after),
        out_specs=[VMEM_SPEC] * count,
        out_shape=[pltpu.VMEM(keep.shape[1:], BF16)] * count,
        compiler_params=pltpu.CompilerParams(vmem_limit_bytes=4 * MIB),
        cost_estimate=cost(0.7),
        name="pair_sum",
    )(place, *kept(keep, came), *placed(after))


def add_kernel(count, *refs):
    total = refs[0][...].astype(F32)
    for ref in refs[1:count]:
        total += ref[...].astype(F32)
    refs[-1][...] = total.astype(BF16)


def add_up(got, after=()):
    return pl.pallas_call(
        lambda *refs: add_kernel(len(got), *refs),
        in_specs=[VMEM_SPEC] * len(got) + specs_of(after),
        out_specs=VMEM_SPEC,
        out_shape=pltpu.VMEM(got[0].shape, BF16),
        compiler_params=pltpu.CompilerParams(vmem_limit_bytes=4 * MIB),
        cost_estimate=cost(0.2),
        name="add_up",
    )(*kept(*got), *placed(after))


def split_kernel(count, others, place_ref, *refs):
    total = refs[0]
    pieces = refs[count + others :]
    wide = total.shape[1] // len(pieces)
    for hop, ref in enumerate(pieces):
        at = lax.rem(place_ref[2] + hop, len(pieces))
        columns = pl.ds(pl.multiple_of(at * wide, wide), wide)
        v = refs[0][:, columns].astype(F32)
        for other in refs[1:count]:
            v += other[:, columns].astype(F32)
        ref[...] = v.astype(BF16)


def add_split(place, got, ring, after=()):
    rows, columns = got[0].shape
    return pl.pallas_call(
        lambda *refs: split_kernel(len(got), len(after), *refs),
        in_specs=[SMEM_SPEC] + [VMEM_SPEC] * len(got) + specs_of(after),
        out_specs=[VMEM_SPEC] * ring,
        out_shape=[pltpu.VMEM((rows, columns // ring), BF16)] * ring,
        compiler_params=pltpu.CompilerParams(vmem_limit_bytes=4 * MIB),
        cost_estimate=cost(0.3),
        name="add_split",
    )(place, *kept(*got), *placed(after))


def join_kernel(count, others, place_ref, *refs):
    out_ref = refs[-1]
    wide = refs[0].shape[1]
    for hop in range(count):
        at = lax.rem(place_ref[2] + count - hop, count)
        out_ref[:, pl.ds(pl.multiple_of(at * wide, wide), wide)] = refs[hop][...]


def join_pieces(place, got, after=()):
    rows, columns = got[0].shape
    return pl.pallas_call(
        lambda *refs: join_kernel(len(got), len(after), *refs),
        in_specs=[SMEM_SPEC] + [VMEM_SPEC] * len(got) + specs_of(after),
        out_specs=VMEM_SPEC,
        out_shape=pltpu.VMEM((rows, columns * len(got)), BF16),
        compiler_params=pltpu.CompilerParams(vmem_limit_bytes=4 * MIB),
        cost_estimate=cost(0.3),
        name="join_pieces",
    )(place, *kept(*got), *placed(after))


def unpack_kernel(count, tokens, place_ref, *refs):
    first = refs[:count]
    second = refs[count : 2 * count]
    (
        glu_ref, outr_ref, outi_ref, inr_ref, ini_ref, gain_ref, bias_ref, nu_ref, theta_ref,
        gamma_ref, skip_ref, glub_ref, rms_ref, lines,
    ) = refs[2 * count :]
    width = glu_ref.shape[1] // 2
    states = inr_ref.shape[1]
    high = glu_ref.shape[0] // count
    part = outr_ref.shape[0] // count
    for hop in range(count):
        at = place_ref[1] ^ hop
        rows = pl.ds(pl.multiple_of(at * high, high), high)
        glu_ref[rows, :] = first[hop][:high, :].astype(F32)
        inr_ref[rows, :] = second[hop][:high, :states].astype(F32)
        ini_ref[rows, :] = second[hop][:high, states:].astype(F32)
        few = pl.ds(pl.multiple_of(at * part, part), part)
        outr_ref[few, :] = first[hop][high:, :width].astype(F32)
        outi_ref[few, :] = first[hop][high:, width:].astype(F32)
        lines[pl.ds(pl.multiple_of(at * 8, 8), 8), :] = second[hop][high:, :].astype(F32)[:8]
    half, some = width // 2, states // 2
    per = 8 // count
    line = lambda k: lines[k // per * 8 : k // per * 8 + 1, k % per * half : (k % per + 1) * half]
    gain_ref[...] = line(0)
    bias_ref[...] = line(1)
    nu_ref[...] = line(2)[:, :some]
    theta_ref[...] = line(2)[:, some:]
    gamma_ref[...] = line(3)[:, :some]
    skip_ref[...] = line(4)
    glub_ref[:, :half] = line(5)
    glub_ref[:, half:] = line(6)
    rms_ref[...] = jnp.sqrt(line(7)[:, :3] / tokens)


def unpack(place, first, second, width, states, tokens):
    count = len(first)
    flat = [width // 2, width // 2, states // 2, states // 2, states // 2, width // 2, width, 3]
    return pl.pallas_call(
        lambda *refs: unpack_kernel(count, tokens, *refs),
        in_specs=[SMEM_SPEC] + [VMEM_SPEC] * (2 * count),
        out_specs=[VMEM_SPEC] * 13,
        out_shape=[
            jax.ShapeDtypeStruct((width // 2, 2 * width), F32),
            jax.ShapeDtypeStruct((states // 2, width), F32),
            jax.ShapeDtypeStruct((states // 2, width), F32),
            jax.ShapeDtypeStruct((width // 2, states), F32),
            jax.ShapeDtypeStruct((width // 2, states), F32),
        ]
        + [jax.ShapeDtypeStruct((1, n), F32) for n in flat],
        scratch_shapes=[pltpu.VMEM((8 * count, width), F32)],
        compiler_params=pltpu.CompilerParams(vmem_limit_bytes=8 * MIB),
        name="unpack",
    )(place, *first, *second)


def hops_of(ends, axis, reverse):
    count = lax.axis_size(axis)
    if count <= 4:
        return [
            lax.ppermute(
                ends,
                axis,
                [(i + hop, i) if reverse else (i, i + hop) for i in range(count - hop)],
            )
            for hop in range(1, count)
        ]
    place = lax.axis_index(axis)
    every = lax.all_gather(ends, axis)
    came = []
    for hop in range(1, count):
        source = place + hop if reverse else place - hop
        inside = (source >= 0) & (source < count)
        item = lax.dynamic_index_in_dim(every, jnp.clip(source, 0, count - 1), 0, False)
        came.append(jnp.where(inside, item, 0.0))
    return came


def swap(a):
    return lax.ppermute(a, "fsdp", [(0, 1), (1, 0)])


def swap_moves(axis, bit):
    return [(i, i ^ bit) for i in range(lax.axis_size(axis))]


def scatter_batch(pieces):
    return [pieces[0]] + [
        lax.ppermute(pieces[hop], "batch", swap_moves("batch", hop))
        for hop in range(1, len(pieces))
    ]


def around(pieces):
    ring = lax.axis_size("seq")
    return [pieces[0]] + [
        lax.ppermute(pieces[hop], "seq", [(i, (i + hop) % ring) for i in range(ring)])
        for hop in range(1, ring)
    ]


def share_seq(piece):
    ring = lax.axis_size("seq")
    if ring > 4:
        return [lax.psum(piece.astype(F32), "seq").astype(BF16)]
    return around([piece] * ring)


def gather_batch(piece):
    count = lax.axis_size("batch")
    return [piece] + [
        lax.ppermute(piece, "batch", swap_moves("batch", hop)) for hop in range(1, count)
    ]


def on_device(
    stream, norm_gain, norm_bias, in_real, in_imag, nu_log, theta_log, gamma_log, out_real,
    out_imag, skip_scale, glu_weight, glu_bias, cotangent,
):
    seqs, length, width = stream.shape
    states = 2 * nu_log.shape[0]
    batch = lax.axis_size("batch")
    place = jnp.stack(
        [lax.axis_index("fsdp"), lax.axis_index("batch"), lax.axis_index("seq")]
    ).astype(jnp.int32)
    vectors = pack_vectors(
        norm_gain, norm_bias, skip_scale, glu_bias, nu_log, theta_log, gamma_log
    )
    into = [in_real, swap(in_real), in_imag, swap(in_imag)]
    others = [swap(glu_weight), swap(out_real), swap(out_imag)]
    (
        normed, sums, ends, p, q, small, win, wback, square, stream_kept, cot_kept, *own,
    ) = norm_pass(
        place, stream, cotangent, into, [glu_weight, out_real, out_imag], [vectors, swap(vectors)]
    )
    halves = [a for pair_of in zip(own, others) for a in pair_of]
    came = hops_of(ends, "seq", False)
    mixed, back, state, dlru, starts, keep, send, acc, gacc = block_pass(
        place, batch, sums, normed, stream_kept, cot_kept, p, small, halves, came
    )
    later = hops_of(starts, "seq", True)
    pieces = pair_sum(place, keep, swap(send), later)
    first = scatter_batch(pieces)
    ddrive, keep, send = adjoint_pass(
        place, batch, back, state, normed, wback, q, small, square, acc, gacc, later, pieces
    )
    ring = lax.axis_size("seq")
    short = ring <= 4
    first = add_split(place, first, ring if short else 1, [send])
    send, *first = lax.optimization_barrier((send, *first))
    pieces = pair_sum(place, keep, swap(send))
    second = scatter_batch(pieces)
    first = around(first) if short else share_seq(first[0])
    last = lambda seq, earlier, after: input_pass(
        seq, ddrive, dlru, stream_kept, cot_kept, small, wback, earlier, after
    )
    grads = ()
    for seq in range(seqs - 1):
        grads = (last(seq, grads, [first[0], pieces[0]]),)
    first = add_up(first, grads)
    if short:
        first = around([first] * ring)
    second = share_seq(add_up(second, [first[0], *grads]))
    if short:
        first = join_pieces(place, first, [second[0]])
    first = gather_batch(first)
    grads = (last(seqs - 1, grads, [first[0], second[0]]),)
    second = gather_batch(add_up(second, grads))
    grad_stream = grads[0]
    tokens = stream.size * batch * lax.axis_size("seq") * lax.axis_size("fsdp")
    (
        glu, out_r, out_i, in_r, in_i, gain, bias, nu, theta, gamma, skip, glub, rms,
    ) = unpack(place, first, second, width, states, float(tokens))
    flat = lambda a: a.reshape(-1)
    return (
        mixed, grad_stream, flat(gain), flat(bias), in_r, in_i, flat(nu), flat(theta), flat(gamma),
        out_r, out_i, flat(skip), glu, flat(glub), flat(rms),
    )


def solution(mesh):
    tokens = P(("batch", "fsdp"), "seq", None)
    vector = P("fsdp")
    matrix = P("fsdp", None)
    weights = (
        vector, vector, matrix, matrix, vector, vector, vector, matrix, matrix, vector, matrix,
        vector,
    )
    return jax.shard_map(
        on_device,
        mesh=mesh,
        in_specs=(tokens,) + weights + (tokens,),
        out_specs=(tokens, tokens) + weights + (P(),),
        check_vma=False,
    )
```

```python
import functools

import jax
import jax.numpy as jnp
from jax import lax
from jax.experimental import pallas as pl
from jax.experimental.pallas import tpu as pltpu
from jax.sharding import PartitionSpec as P

F32 = jnp.float32
BF16 = jnp.bfloat16
HIGHEST = lax.Precision.HIGHEST
CHUNK = 128
HALF = 64
BLOCK = 512
SUB = 64
TILE = 256
GELU_C = 0.7978845608028654
GELU_K = 0.044715
MIB = 1024 * 1024


def dot_nn(a, b):
    return jnp.dot(a, b, preferred_element_type=F32)


def dot_tn(a, b):
    return lax.dot_general(a, b, (((0,), (0,)), ((), ())), preferred_element_type=F32)


def dot_nt(a, b):
    return lax.dot_general(a, b, (((1,), (1,)), ((), ())), preferred_element_type=F32)


def dot_nt_wide(a, b):
    return lax.dot_general(
        a, b, (((1,), (1,)), ((), ())), precision=HIGHEST, preferred_element_type=F32
    )


def cmul(ar, ai, br, bi):
    return ar * br - ai * bi, ar * bi + ai * br


def fold(v):
    return jnp.sum(v.reshape(v.shape[0] // 8, 8, v.shape[1]), axis=0)


def fold_low(v):
    rows = v.shape[0] // 4
    v = (v[:rows] + v[rows : 2 * rows]) + (v[2 * rows : 3 * rows] + v[3 * rows :])
    return fold(v.astype(F32))


def split_store(stack, k, zr, zi):
    states = zr.shape[1]
    for part, v in enumerate((zr, zi)):
        columns = pl.ds(part * states, states)
        high = v.astype(BF16)
        stack[k, :CHUNK, columns] = high
        stack[k, CHUNK:, columns] = (v - high.astype(F32)).astype(BF16)


def fill_triangle(tri, upper):
    row = lax.broadcasted_iota(jnp.int32, (CHUNK, CHUNK), 0)
    column = lax.broadcasted_iota(jnp.int32, (CHUNK, CHUNK), 1)
    inside = (column >= row) if upper else (column <= row)
    ones = jnp.where(inside, 1.0, 0.0).astype(BF16)
    tri[:, :CHUNK] = ones
    tri[:, CHUNK:] = ones


ROW_STEP = 0
ROW_LAST = 1
ROW_ENTER = 2
ROW_FIRST = 3
ROW_BACK = 4
ROW_WHOLE = 5
ROW_SCALE = 6
ROW_RATE = 7
ROW_GAIN = 8
ROW_BIAS = 9
ROW_SKIP = 10
ROW_GLU = 11
TABLE_ROWS = 16


def pair(ref, row, states):
    return ref[row : row + 1, :states], ref[row : row + 1, states:]


def row_of(ref, row):
    return ref[row : row + 1, :]


def fill_tables(me, own_ref, other_ref, p_ref, q_ref, small_ref, length):
    states = q_ref.shape[1] // 2
    width = q_ref.shape[1]
    own = own_ref[...].astype(F32)
    other = other_ref[...].astype(F32)
    low = jnp.where(me == 0, own, other)
    high = jnp.where(me == 0, other, own)

    def both(first, count):
        rows = [h[first + i : first + i + 1] for h in (low, high) for i in range(count)]
        return jnp.concatenate(rows, axis=1)

    small_ref[...] = jnp.zeros_like(small_ref)
    for row, first in ((ROW_GAIN, 0), (ROW_BIAS, 2), (ROW_SKIP, 4)):
        small_ref[row : row + 1, :] = both(first, 2)
    glu = both(6, 4)
    small_ref[ROW_GLU : ROW_GLU + 1, :] = glu[:, :width]
    small_ref[ROW_GLU + 1 : ROW_GLU + 2, :] = glu[:, width:]
    decay = jnp.exp(both(10, 1))
    rotation = jnp.exp(both(11, 1))
    scale = jnp.exp(both(12, 1))
    steps = (lax.broadcasted_iota(jnp.int32, (CHUNK, states), 0) - HALF).astype(F32)
    turn = steps * rotation
    cos = jnp.cos(turn)
    sin = jnp.sin(turn)
    grow = jnp.exp(-steps * decay)
    p_ref[:, :states] = grow * cos
    p_ref[:, states:] = grow * sin
    shrink = scale * jnp.exp(steps * decay)
    q_ref[:, :states] = shrink * cos
    q_ref[:, states:] = -shrink * sin
    counts = {
        ROW_STEP: CHUNK,
        ROW_LAST: CHUNK - 1 - HALF,
        ROW_ENTER: HALF + 1,
        ROW_FIRST: HALF,
        ROW_BACK: CHUNK - HALF,
        ROW_WHOLE: length,
    }
    assert sorted(counts) == list(range(6))
    index = lax.broadcasted_iota(jnp.int32, (8, states), 0)
    count = jnp.zeros((8, states), F32)
    for row, steps in counts.items():
        count = jnp.where(index == row, float(steps), count)
    size = jnp.exp(-count * decay)
    small_ref[:6, :states] = (size * jnp.cos(count * rotation))[:6]
    small_ref[:6, states:] = (size * jnp.sin(count * rotation))[:6]
    small_ref[ROW_SCALE : ROW_SCALE + 1, :states] = scale
    small_ref[ROW_SCALE : ROW_SCALE + 1, states:] = 1.0 / scale
    small_ref[ROW_RATE : ROW_RATE + 1, :states] = decay
    small_ref[ROW_RATE : ROW_RATE + 1, states:] = rotation


def join_halves(me, whole, own, other, columns=slice(None)):
    rows = own.shape[0]
    whole[pl.ds(pl.multiple_of(me * rows, rows), rows), columns] = own[...]
    whole[pl.ds(pl.multiple_of((1 - me) * rows, rows), rows), columns] = other[...]


def cost(microseconds):
    return pl.CostEstimate(
        flops=0, transcendentals=0, bytes_accessed=int(microseconds * 3.6e6)
    )


def norm_kernel(
    length, place_ref, stream_hbm, cot_hbm, inr_hbm, ini_hbm, glu_hbm, outr_hbm, outi_hbm,
    vec_own, vec_other, inr_other, ini_other,
    normed_ref, sums_ref, end_ref, p_ref, q_ref, small_ref, win_ref, wback_ref, square_ref,
    stream_ref, cot_ref, glu_ref, outr_ref, outi_ref,
    stack, tri, inr_own, ini_own, sems,
):
    states = q_ref.shape[1] // 2
    seqs = stream_ref.shape[0]
    every = range(seqs)
    copy = lambda source, target, k: pltpu.make_async_copy(source, target, sems.at[k])
    weights = [copy(inr_hbm, inr_own, 0), copy(ini_hbm, ini_own, 1)]
    onward = [
        copy(source, target, 2 + k)
        for k, (source, target) in enumerate(
            ((glu_hbm, glu_ref), (outr_hbm, outr_ref), (outi_hbm, outi_ref), (cot_hbm, cot_ref))
        )
    ]
    blocks = []
    for step in range(length // BLOCK):
        at = (slice(None), pl.ds(step * BLOCK, BLOCK))
        blocks.append(copy(stream_hbm.at[at], stream_ref.at[at], 6 + step))
    for c in blocks[:1] + weights + blocks[1:] + onward:
        c.start()
    me = place_ref[0]
    fill_tables(me, vec_own, vec_other, p_ref, q_ref, small_ref, length)
    fill_triangle(tri, False)
    for c in weights:
        c.wait()
    join_halves(me, win_ref, inr_own, inr_other, slice(0, states))
    join_halves(me, win_ref, ini_own, ini_other, slice(states, 2 * states))
    wback_ref[:, :states] = win_ref[:, :states]
    wback_ref[:, states:] = -win_ref[:, states:]

    gain = row_of(small_ref, ROW_GAIN)
    bias = row_of(small_ref, ROW_BIAS)
    step_r, step_i = pair(small_ref, ROW_STEP, states)
    last_r, last_i = pair(small_ref, ROW_LAST, states)
    squares = jnp.zeros((8, 1), F32)
    ends = [(jnp.zeros((1, states), F32),) * 2] * seqs
    for step, block in enumerate(blocks):
        base = step * BLOCK
        rows = pl.ds(base, BLOCK)
        block.wait()
        for r in range(0, BLOCK, SUB):
            for seq in every:
                at = pl.ds(base + r, SUB)
                x = stream_ref[seq, at, :].astype(F32)
                mean = jnp.mean(x, axis=-1, keepdims=True)
                centre = x - mean
                spread = jnp.mean(centre * centre, axis=-1, keepdims=True)
                squares += fold(mean * mean + spread)
                normed_ref[seq, at, :] = (
                    centre * lax.rsqrt(spread + 1e-05) * gain + bias
                ).astype(BF16)
        left = jnp.concatenate([normed_ref[seq, rows, :] for seq in every], axis=0)
        drive = dot_nn(left, win_ref[...])
        for k in range(BLOCK // CHUNK):
            for seq in every:
                first = seq * BLOCK + k * CHUNK
                part = drive[first : first + CHUNK]
                zr, zi = cmul(
                    part[:, :states], part[:, states:], q_ref[:, :states], q_ref[:, states:]
                )
                slot = stack.at[step % 2, seq]
                split_store(slot, k, zr, zi)
                s = dot_nn(tri[...], slot[k])
                sums_ref[seq, pl.ds(base + k * CHUNK, CHUNK), :] = s
                er, ei = cmul(s[CHUNK - 1 :, :states], s[CHUNK - 1 :, states:], last_r, last_i)
                nr, ni = cmul(*ends[seq], step_r, step_i)
                ends[seq] = nr + er, ni + ei
    square_ref[...] = jnp.broadcast_to(squares, square_ref.shape)
    for seq in every:
        end_ref[seq, :, :states], end_ref[seq, :, states:] = ends[seq]
    for c in onward:
        c.wait()


HBM_SPEC = pl.BlockSpec(memory_space=pltpu.HBM)
VMEM_SPEC = pl.BlockSpec(memory_space=pltpu.VMEM)
SMEM_SPEC = pl.BlockSpec(memory_space=pltpu.SMEM)


def kept(*arrays):
    return [pltpu.with_memory_space_constraint(a, pltpu.VMEM) for a in arrays]


def large(a):
    return a.size * a.dtype.itemsize > 2 * MIB


def specs_of(arrays):
    return [HBM_SPEC if large(a) else VMEM_SPEC for a in arrays]


def placed(arrays):
    return [in_hbm(a)[0] if large(a) else kept(a)[0] for a in arrays]


def in_hbm(*arrays):
    return [pltpu.with_memory_space_constraint(a, pltpu.HBM) for a in arrays]


def norm_pass(place, stream, cot, into, onward, vectors):
    seqs, length, width = stream.shape
    half, states = into[0].shape
    states2 = 2 * states
    return pl.pallas_call(
        lambda *refs: norm_kernel(length, *refs),
        in_specs=[SMEM_SPEC] + [HBM_SPEC] * 7 + [VMEM_SPEC] * 4,
        out_specs=[VMEM_SPEC] * 14,
        out_shape=[
            pltpu.VMEM((seqs, length, width), BF16),
            pltpu.VMEM((seqs, length, states2), F32),
            pltpu.VMEM((seqs, 1, states2), F32),
            pltpu.VMEM((CHUNK, states2), F32),
            pltpu.VMEM((CHUNK, states2), F32),
            pltpu.VMEM((TABLE_ROWS, states2), F32),
            pltpu.VMEM((width, states2), BF16),
            pltpu.VMEM((width, states2), BF16),
            pltpu.VMEM((8, 128), F32),
            pltpu.VMEM(stream.shape, BF16),
            pltpu.VMEM(cot.shape, BF16),
        ]
        + [pltpu.VMEM(a.shape, BF16) for a in onward],
        scratch_shapes=[
            pltpu.VMEM((2, seqs, BLOCK // CHUNK, 2 * CHUNK, states2), BF16),
            pltpu.VMEM((CHUNK, 2 * CHUNK), BF16),
            pltpu.VMEM((half, states), BF16),
            pltpu.VMEM((half, states), BF16),
            pltpu.SemaphoreType.DMA((length // BLOCK + 6,)),
        ],
        compiler_params=pltpu.CompilerParams(vmem_limit_bytes=8 * MIB),
        cost_estimate=cost(9),
        name="norm_pass",
    )(
        place,
        *in_hbm(stream, cot, into[0], into[2], *onward),
        *kept(*vectors, into[1], into[3]),
    )


def entering(carry, came, seq, small_ref, states):
    whole_r, whole_i = pair(small_ref, ROW_WHOLE, states)
    total_r = came[0][seq, :, :states]
    total_i = came[0][seq, :, states:]
    power_r, power_i = whole_r, whole_i
    for ref in came[1:]:
        gr, gi = cmul(ref[seq, :, :states], ref[seq, :, states:], power_r, power_i)
        total_r, total_i = total_r + gr, total_i + gi
        power_r, power_i = cmul(power_r, power_i, whole_r, whole_i)
    carry[0:1, :states] = total_r
    carry[0:1, states:] = total_i


def block_kernel(
    hops, place_ref, _, normed_ref, stream_ref, cot_ref, p_ref, small_ref, glu_own, glu_other,
    outr_own, outr_other, outi_own, outi_other, *rest,
):
    came = rest[:hops]
    (
        mixed_hbm, back_ref, state_ref, dlru_ref, start_ref, keep_ref, send_ref, acc_ref, gacc_ref,
        carry, stack, tri, act, dproj, slope, mixed, wglu, wout, dglu, dout, sems,
    ) = rest[hops:]
    states = p_ref.shape[1] // 2
    seqs, _, width = stream_ref.shape
    me = place_ref[0]
    join_halves(me, wglu, glu_own, glu_other)
    join_halves(me, wout.at[pl.ds(0, states)], outr_own, outr_other)
    join_halves(me, wout.at[pl.ds(states, states)], outi_own, outi_other)
    fill_triangle(tri, True)
    acc_ref[...] = jnp.zeros_like(acc_ref)
    gacc_ref[...] = jnp.zeros_like(gacc_ref)
    dglu[...] = jnp.zeros_like(dglu)
    dout[...] = jnp.zeros_like(dout)
    for seq in range(seqs):
        entering(carry.at[seq], came, seq, small_ref, states)
        carry[seq, 1:2, :] = jnp.zeros_like(carry[seq, 1:2, :])
        carry[seq, 2:3, :states] = jnp.ones_like(carry[seq, 2:3, :states])
        carry[seq, 2:3, states:] = jnp.zeros_like(carry[seq, 2:3, states:])

    step_r, step_i = pair(small_ref, ROW_STEP, states)
    last_r, last_i = pair(small_ref, ROW_LAST, states)
    enter_r, enter_i = pair(small_ref, ROW_ENTER, states)
    first_r, first_i = pair(small_ref, ROW_FIRST, states)
    skip = row_of(small_ref, ROW_SKIP)
    value_bias = row_of(small_ref, ROW_GLU)
    gate_bias = row_of(small_ref, ROW_GLU + 1)
    def mixed_copy(step):
        at = pl.ds(step * BLOCK, BLOCK)
        return pltpu.make_async_copy(
            mixed.at[step % 2], mixed_hbm.at[:, at, :], sems.at[step % 2]
        )

    steps = stream_ref.shape[1] // BLOCK
    for step in range(steps):
        base = step * BLOCK
        slot = step % 2
        rows = pl.ds(base, BLOCK)
        pieces = [
            (slice(r, r + SUB), pl.ds(base + r, SUB)) for r in range(0, BLOCK, SUB)
        ]
        chunks = [
            (k, pl.ds(base + k * CHUNK, CHUNK)) for k in range(BLOCK // CHUNK)
        ]
        zeros = jnp.zeros((8, width), F32)
        tiles = lambda count: [slice(n, n + TILE) for n in range(0, count, TILE)]
        spans = tiles(width)
        made = {}
        folds = {}

        def make_states(seq):
            def part(k, at):
                cr, ci = made["carry", seq]
                qr, qi = cmul(cr, ci, enter_r, enter_i)
                sr = back_ref[seq, at, :states]
                si = back_ref[seq, at, states:]
                er, ei = cmul(sr[CHUNK - 1 :], si[CHUNK - 1 :], last_r, last_i)
                nr, ni = cmul(cr, ci, step_r, step_i)
                made["carry", seq] = nr + er, ni + ei
                hr, hi = cmul(sr + qr, si + qi, p_ref[:, :states], p_ref[:, states:])
                state_ref[seq, at, :states] = hr.astype(BF16)
                state_ref[seq, at, states:] = (-hi).astype(BF16)

            def first():
                made["carry", seq] = carry[seq, 0:1, :states], carry[seq, 0:1, states:]

            def last():
                carry[seq, 0:1, :states], carry[seq, 0:1, states:] = made["carry", seq]

            return [first] + [functools.partial(part, *c) for c in chunks] + [last]

        every = range(seqs)
        both = lambda one: jnp.concatenate([one(seq) for seq in every], axis=0)

        def products(name, left, right, columns, turned=False, order=None):
            def part(n):
                if turned:
                    v = dot_nt(both(left), right[n, :])
                else:
                    v = dot_nn(both(left), right[:, n])
                v = v.astype(BF16) if name == "dact" else v
                for seq in every:
                    made.setdefault((name, seq), []).append(v[seq * BLOCK : (seq + 1) * BLOCK])

            return [functools.partial(part, n) for n in (order or tiles(columns))]

        def taken(name, seq, r, first=0, count=None):
            parts = made[name, seq][first:count]
            return jnp.concatenate([v[r] for v in parts], axis=1)

        def gather(name, n, v):
            key = name, n.start
            folds[key] = folds[key] + v if key in folds else v

        def read_out():
            return products("lru", lambda seq: state_ref[seq, rows, :], wout, width)

        def activate(seq, n):
            def part(r, at):
                readout = made["lru", seq][n.start // TILE][r]
                lru = readout + skip[:, n] * normed_ref[seq, at, n].astype(F32)
                lru2 = lru * lru
                gather("lru", n, fold(lru2))
                gate = 0.5 + 0.5 * jnp.tanh(lru * (GELU_C + GELU_C * GELU_K * lru2))
                gelu = lru * gate
                slope[seq, r, n] = (gate + (gelu - gelu * gate) * (
                    2 * GELU_C + 6 * GELU_C * GELU_K * lru2
                )).astype(BF16)
                act[seq, r, n] = gelu.astype(BF16)

            return [functools.partial(part, *c) for c in pieces]

        def project():
            order = [slice(first + n.start, first + n.stop) for n in spans for first in (0, width)]
            return products("projected", lambda seq: act[seq], wglu, 2 * width, order=order)

        def branch_out(seq, n):
            def part(r, at):
                value = made["projected", seq][2 * (n.start // TILE)][r] + value_bias[:, n]
                gate = made["projected", seq][2 * (n.start // TILE) + 1][r] + gate_bias[:, n]
                gate = 0.5 + 0.5 * jnp.tanh(0.5 * gate)
                branch = value * gate
                mixed[slot, seq, r, n] = (stream_ref[seq, at, n].astype(F32) + branch).astype(BF16)
                gather("branch", n, fold(branch * branch))
                cot = cot_ref[seq, at, n].astype(F32)
                part = cot * branch
                dvalue = (cot * gate).astype(BF16)
                dgate = (part - part * gate).astype(BF16)
                dproj[seq, r, n] = dvalue
                dproj[seq, r, slice(width + n.start, width + n.stop)] = dgate
                gather("value", n, fold_low(dvalue))
                gather("gate", n, fold_low(dgate))

            return [functools.partial(part, *c) for c in pieces]

        def project_back():
            return products("dact", lambda seq: dproj[seq], wglu, width, True)

        def activate_back(seq, n):
            def part(r, at):
                dlru = made["dact", seq][n.start // TILE][r] * slope[seq, r, n]
                dlru_ref[seq, at, n] = dlru
                gather("dlru", n, fold_low(dlru))
                gather("skip", n, fold_low(dlru * normed_ref[seq, at, n]))

            return [functools.partial(part, *c) for c in pieces]

        def read_out_back():
            return products("pull", lambda seq: dlru_ref[seq, rows, :], wout, 2 * states, True)

        def glu_back():
            def part(n):
                dglu[:, n] += dot_tn(both(lambda seq: act[seq]), both(lambda seq: dproj[seq, :, n]))

            return [functools.partial(part, n) for n in tiles(2 * width)]

        def out_back():
            def part(n):
                dout[:, n] += dot_tn(
                    both(lambda seq: state_ref[seq, rows, :]), both(lambda seq: dlru_ref[seq, rows, n])
                )

            return [functools.partial(part, n) for n in tiles(width)]

        def turn(seq):
            def part(k, at):
                pull = taken("pull", seq, slice(k * CHUNK, (k + 1) * CHUNK))
                zr, zi = cmul(pull[:, :states], pull[:, states:], p_ref[:, :states], p_ref[:, states:])
                split_store(stack.at[seq], k, zr, zi)

            return [functools.partial(part, *c) for c in chunks]

        def sum_back(seq):
            def part(k, at):
                ar, ai = carry[seq, 1:2, :states], carry[seq, 1:2, states:]
                wr, wi = carry[seq, 2:3, :states], carry[seq, 2:3, states:]
                back = dot_nn(tri[...], stack[seq, k])
                back_ref[seq, at, :] = back
                fr, fi = cmul(back[0:1, :states], back[0:1, states:], first_r, first_i)
                gr, gi = cmul(fr, fi, wr, wi)
                ar, ai = ar + gr, ai + gi
                wr, wi = cmul(wr, wi, step_r, step_i)
                carry[seq, 1:2, :states] = ar
                carry[seq, 1:2, states:] = ai
                carry[seq, 2:3, :states] = wr
                carry[seq, 2:3, states:] = wi
                start_ref[seq, :, :states] = ar
                start_ref[seq, :, states:] = ai

            return [functools.partial(part, *c) for c in chunks]

        def run(*lists):
            parts = [(i / len(one), part) for one in lists for i, part in enumerate(one)]
            for _, part in sorted(parts, key=lambda item: item[0]):
                part()

        run(*[make_states(seq) for seq in every])
        readout = read_out()
        for n, part in zip(spans, readout):
            run([part])
            run(*[activate(seq, n) for seq in every])
        projected = project()
        if step >= 2:
            mixed_copy(step - 2).wait()
        for k, n in enumerate(spans):
            run(projected[2 * k : 2 * k + 2])
            run(*[branch_out(seq, n) for seq in every])
        mixed_copy(step).start()
        for n, part in zip(spans, project_back()):
            run([part])
            run(*[activate_back(seq, n) for seq in every])
        run(glu_back())
        run(read_out_back())
        run(*[turn(seq) for seq in every], out_back())
        run(*[sum_back(seq) for seq in every])
        for row, name in enumerate(("lru", "branch", "dlru", "skip")):
            for n in spans:
                acc_ref[8 * row : 8 * row + 8, n] += folds[name, n.start]
        for row, name in enumerate(("value", "gate")):
            for n in spans:
                gacc_ref[8 * row : 8 * row + 8, n] += folds[name, n.start]

    for step in range(max(steps - 2, 0), steps):
        mixed_copy(step).wait()
    batch, height, _ = keep_ref.shape
    high = width // (2 * batch)
    part = height - high
    for ref, f in ((keep_ref, place_ref[0]), (send_ref, 1 - place_ref[0])):
        for b in range(batch):
            first = pl.multiple_of((f * batch + b) * high, high)
            ref[b, :high, :] = dglu[pl.ds(first, high), :].astype(BF16)
            first = pl.multiple_of((f * batch + b) * part, part)
            ref[b, high:, :width] = dout[pl.ds(first, part), :].astype(BF16)
            ref[b, high:, width:] = dout[pl.ds(states + first, part), :].astype(BF16)


def block_pass(place, batch, sums, normed, stream, cot, p, small, halves, came):
    seqs, length, width = stream.shape
    states2 = p.shape[1]
    height = width // (2 * batch) + states2 // (4 * batch)
    return pl.pallas_call(
        lambda *refs: block_kernel(len(came), *refs),
        in_specs=[SMEM_SPEC] + [VMEM_SPEC] * (12 + len(came)),
        out_specs=[HBM_SPEC] + [VMEM_SPEC] * 8,
        out_shape=[
            pltpu.HBM((seqs, length, width), BF16),
            pltpu.VMEM((seqs, length, states2), F32),
            pltpu.VMEM((seqs, length, states2), BF16),
            pltpu.VMEM((seqs, length, width), BF16),
            jax.ShapeDtypeStruct((seqs, 1, states2), F32),
            pltpu.VMEM((batch, height, 2 * width), BF16),
            pltpu.VMEM((batch, height, 2 * width), BF16),
            pltpu.VMEM((32, width), F32),
            pltpu.VMEM((16, width), F32),
        ],
        scratch_shapes=[
            pltpu.VMEM((seqs, 8, states2), F32),
            pltpu.VMEM((seqs, BLOCK // CHUNK, 2 * CHUNK, states2), BF16),
            pltpu.VMEM((CHUNK, 2 * CHUNK), BF16),
            pltpu.VMEM((seqs, BLOCK, width), BF16),
            pltpu.VMEM((seqs, BLOCK, 2 * width), BF16),
            pltpu.VMEM((seqs, BLOCK, width), BF16),
            pltpu.VMEM((2, seqs, BLOCK, width), BF16),
            pltpu.VMEM((width, 2 * width), BF16),
            pltpu.VMEM((states2, width), BF16),
            pltpu.VMEM((width, 2 * width), F32),
            pltpu.VMEM((states2, width), F32),
            pltpu.SemaphoreType.DMA((2,)),
        ],
        input_output_aliases={1: 1},
        compiler_params=pltpu.CompilerParams(vmem_limit_bytes=20 * MIB),
        cost_estimate=cost(28),
        name="block_pass",
    )(place, *kept(sums, normed, stream, cot, p, small, *halves, *came))


def adjoint_kernel(
    hops, others, place_ref, back_ref, _, normed_ref, win_ref, q_ref, small_ref, square_ref, acc_ref, gacc_ref,
    *rest,
):
    came = rest[:hops]
    ddrive_ref, keep_ref, send_ref, carry, din = rest[hops + others :]
    states = q_ref.shape[1] // 2
    seqs, length, _ = normed_ref.shape
    every = range(seqs)
    first_r, first_i = pair(small_ref, ROW_FIRST, states)
    back_r, back_i = pair(small_ref, ROW_BACK, states)
    carries = []
    for seq in every:
        entering(carry, came, seq, small_ref, states)
        carries.append((carry[0:1, :states], carry[0:1, states:]))
    real_sum = imag_sum = real_total = imag_total = jnp.zeros((8, states), F32)
    for base in reversed(range(0, length, BLOCK)):
        for k in reversed(range(BLOCK // CHUNK)):
            for seq in every:
                at = pl.ds(base + k * CHUNK, CHUNK)
                qr, qi = cmul(*carries[seq], back_r, back_i)
                vr = back_ref[seq, at, :states] + qr
                vi = back_ref[seq, at, states:] + qi
                carries[seq] = cmul(vr[0:1], vi[0:1], first_r, first_i)
                ar, ai = cmul(vr, vi, q_ref[:, :states], q_ref[:, states:])
                hr = ddrive_ref[seq, at, :states]
                hi = ddrive_ref[seq, at, states:]
                lr, li = ar.astype(BF16), ai.astype(BF16)
                real_sum += fold((lr * hr).astype(F32) + (li * hi).astype(F32))
                imag_sum += fold((lr * hi).astype(F32) - (li * hr).astype(F32))
                real_total += fold_low(lr)
                imag_total += fold_low(li)
                ddrive_ref[seq, at, :states] = lr
                ddrive_ref[seq, at, states:] = li
        rows = pl.ds(base, BLOCK)
        product = dot_tn(
            jnp.concatenate([normed_ref[seq, rows, :] for seq in every], axis=0),
            jnp.concatenate([ddrive_ref[seq, rows, :] for seq in every], axis=0),
        )
        if base == length - BLOCK:
            din[...] = product
        else:
            din[...] += product
    width = din.shape[0]
    gain = row_of(small_ref, ROW_GAIN)
    bias = row_of(small_ref, ROW_BIAS)
    skip = row_of(small_ref, ROW_SKIP)
    weight = win_ref[...].astype(F32)
    grad = din[...]
    in_r, in_i = weight[:, :states], weight[:, states:]
    g_r, g_i = grad[:, :states], grad[:, states:]
    x_r = jnp.sum(g_r * in_r + g_i * in_i, axis=0, keepdims=True)
    x_i = jnp.sum(g_r * in_i - g_i * in_r, axis=0, keepdims=True)
    inverse = small_ref[ROW_SCALE : ROW_SCALE + 1, states:]
    column = lambda v: jnp.sum(v, axis=0, keepdims=True)
    d_r = column(real_sum) * inverse - x_r
    d_i = column(imag_sum) * inverse - x_i
    decay, rotation = pair(small_ref, ROW_RATE, states)
    gathered = dot_nt_wide(jnp.ones((8, 2 * states), F32), weight * grad)[0:1]
    total = jnp.broadcast_to(jnp.concatenate([column(real_total), column(imag_total)], axis=1), (8, 2 * states))
    d_lru = column(acc_ref[16:24, :])
    d_skip = column(acc_ref[24:32, :])
    d_bias = dot_nt_wide(total, weight)[0:1] + skip * d_lru
    d_gain = (gathered + skip * d_skip - bias * d_bias) / gain
    d_nu = -decay * d_r
    d_theta = rotation * d_i
    d_values = column(gacc_ref[0:8, :])
    d_gates = column(gacc_ref[8:16, :])
    lane = lax.broadcasted_iota(jnp.int32, (1, width // 2), 1)
    squares = jnp.zeros((1, width // 2), F32)
    sums = (
        width * jnp.sum(square_ref[:, 0:1]), jnp.sum(acc_ref[0:8, :]), jnp.sum(acc_ref[8:16, :]),
    )
    for place, v in enumerate(sums):
        squares = jnp.where(lane == place, v, squares)
    half, some = width // 2, states // 2
    batch, height, _ = keep_ref.shape
    high = width // (2 * batch)
    me = place_ref[0]

    def chosen(f, low, up):
        return jnp.where(f == 0, low, up)

    for ref, f in ((keep_ref, me), (send_ref, 1 - me)):
        wide = lambda v: chosen(f, v[:, :half], v[:, half:])
        thin = lambda v: chosen(f, v[:, :some], v[:, some:])
        d_glu = chosen(f, d_values, d_gates)
        lines = (
            wide(d_gain),
            wide(d_bias),
            jnp.concatenate([thin(d_nu), thin(d_theta)], axis=1),
            jnp.concatenate([thin(x_r), jnp.zeros((1, some), F32)], axis=1),
            wide(d_skip),
            d_glu[:, :half],
            d_glu[:, half:],
            squares,
        )
        for b in range(batch):
            first = pl.multiple_of((f * batch + b) * high, high)
            ref[b, :high, :states] = din[pl.ds(first, high), :states].astype(BF16)
            ref[b, :high, states:] = (-din[pl.ds(first, high), states:]).astype(BF16)
            line = jnp.concatenate(lines[b * 8 // batch : (b + 1) * 8 // batch], axis=1)
            line = jnp.broadcast_to(line, (height - high, width)).astype(BF16)
            ref[b, high:, :] = line


def adjoint_pass(
    place, batch, back, state, normed, wback, q, small, square, acc, gacc, came, after
):
    seqs, length, width = normed.shape
    states2 = q.shape[1]
    return pl.pallas_call(
        lambda *refs: adjoint_kernel(len(came), len(after), *refs),
        in_specs=[SMEM_SPEC] + [VMEM_SPEC] * (9 + len(came)) + specs_of(after),
        out_specs=[VMEM_SPEC] * 3,
        out_shape=[
            pltpu.VMEM((seqs, length, states2), BF16),
            pltpu.VMEM((batch, width // (2 * batch) + 16, states2), BF16),
            pltpu.VMEM((batch, width // (2 * batch) + 16, states2), BF16),
        ],
        scratch_shapes=[
            pltpu.VMEM((8, states2), F32),
            pltpu.VMEM((width, states2), F32),
        ],
        input_output_aliases={2: 0},
        compiler_params=pltpu.CompilerParams(vmem_limit_bytes=8 * MIB),
        cost_estimate=cost(7),
        name="adjoint_pass",
    )(place, *kept(back, state, normed, wback, q, small, square, acc, gacc, *came), *placed(after))


def input_kernel(seq, ddrive_ref, dlru_ref, stream_ref, cot_ref, small_ref, win_ref, *rest):
    out_ref = rest[-1]
    base = pl.program_id(0) * BLOCK
    gain = row_of(small_ref, ROW_GAIN)
    skip = row_of(small_ref, ROW_SKIP)
    rows = pl.ds(pl.multiple_of(base, BLOCK), BLOCK)
    pulled = dot_nt(ddrive_ref[seq, rows, :], win_ref[...])
    for r in range(0, BLOCK, SUB):
        at = pl.ds(pl.multiple_of(base + r, SUB), SUB)
        d = pulled[r : r + SUB] + skip * dlru_ref[seq, at, :].astype(F32)
        x = stream_ref[seq, at, :].astype(F32)
        centre = x - jnp.mean(x, axis=-1, keepdims=True)
        spread = jnp.mean(centre * centre, axis=-1, keepdims=True)
        inverse = lax.rsqrt(spread + 1e-05)
        hat = centre * inverse
        dhat = d * gain
        m1 = jnp.mean(dhat, axis=-1, keepdims=True)
        m2 = jnp.mean(dhat * hat, axis=-1, keepdims=True)
        out_ref[r : r + SUB, :] = (dhat - m1 - hat * m2) * inverse + cot_ref[seq, at, :].astype(F32)


def input_pass(seq, ddrive, dlru, stream, cot, small, win, earlier, after):
    seqs, length, width = stream.shape
    earlier = in_hbm(*earlier)
    return pl.pallas_call(
        lambda *refs: input_kernel(seq, *refs),
        grid=(length // BLOCK,),
        in_specs=[VMEM_SPEC] * 6 + [HBM_SPEC] * len(earlier) + specs_of(after),
        out_specs=pl.BlockSpec((None, BLOCK, width), lambda i: (seq, i, 0)),
        out_shape=pltpu.HBM((seqs, length, width), F32),
        input_output_aliases={6: 0} if earlier else {},
        compiler_params=pltpu.CompilerParams(vmem_limit_bytes=8 * MIB),
        cost_estimate=cost(4),
        name="input_pass",
    )(*kept(ddrive, dlru, stream, cot, small, win), *earlier, *placed(after))


def pack_kernel(count, *refs):
    out_ref = refs[count]
    parts = refs[count + 1 : -1]
    copies = [
        pltpu.make_async_copy(source, target, refs[-1].at[k])
        for k, (source, target) in enumerate(zip(refs[:count], parts))
    ]
    for c in copies:
        c.start()
    for c in copies:
        c.wait()
    row = 0
    for ref in parts:
        for first in range(0, ref.shape[0], 128):
            out_ref[row : row + 1, :] = ref[first : first + 128].reshape(1, 128)
            row += 1


def pack_vectors(*vectors):
    rows = sum(v.shape[0] for v in vectors) // 128
    return pl.pallas_call(
        lambda *refs: pack_kernel(len(vectors), *refs),
        in_specs=[HBM_SPEC] * len(vectors),
        out_specs=VMEM_SPEC,
        out_shape=pltpu.VMEM((rows, 128), BF16),
        scratch_shapes=[pltpu.VMEM(v.shape, BF16) for v in vectors]
        + [pltpu.SemaphoreType.DMA((len(vectors),))],
        compiler_params=pltpu.CompilerParams(vmem_limit_bytes=2 * MIB),
        name="pack_vectors",
    )(*in_hbm(*vectors))


def pair_kernel(others, place_ref, keep_ref, came_ref, *rest):
    for hop, ref in enumerate(rest[others:]):
        at = place_ref[1] ^ hop
        ref[...] = (keep_ref[at].astype(F32) + came_ref[at].astype(F32)).astype(BF16)


def pair_sum(place, keep, came, after=()):
    count = keep.shape[0]
    return pl.pallas_call(
        lambda *refs: pair_kernel(len(after), *refs),
        in_specs=[SMEM_SPEC] + [VMEM_SPEC] * 2 + specs_of(after),
        out_specs=[VMEM_SPEC] * count,
        out_shape=[pltpu.VMEM(keep.shape[1:], BF16)] * count,
        compiler_params=pltpu.CompilerParams(vmem_limit_bytes=4 * MIB),
        cost_estimate=cost(0.7),
        name="pair_sum",
    )(place, *kept(keep, came), *placed(after))


def add_kernel(count, *refs):
    total = refs[0][...].astype(F32)
    for ref in refs[1:count]:
        total += ref[...].astype(F32)
    refs[-1][...] = total.astype(BF16)


def add_up(got, after=()):
    return pl.pallas_call(
        lambda *refs: add_kernel(len(got), *refs),
        in_specs=[VMEM_SPEC] * len(got) + specs_of(after),
        out_specs=VMEM_SPEC,
        out_shape=pltpu.VMEM(got[0].shape, BF16),
        compiler_params=pltpu.CompilerParams(vmem_limit_bytes=4 * MIB),
        cost_estimate=cost(0.2),
        name="add_up",
    )(*kept(*got), *placed(after))


def split_kernel(count, others, place_ref, *refs):
    total = refs[0]
    pieces = refs[count + others :]
    wide = total.shape[1] // len(pieces)
    for hop, ref in enumerate(pieces):
        at = lax.rem(place_ref[2] + hop, len(pieces))
        columns = pl.ds(pl.multiple_of(at * wide, wide), wide)
        v = refs[0][:, columns].astype(F32)
        for other in refs[1:count]:
            v += other[:, columns].astype(F32)
        ref[...] = v.astype(BF16)


def add_split(place, got, ring, after=()):
    rows, columns = got[0].shape
    return pl.pallas_call(
        lambda *refs: split_kernel(len(got), len(after), *refs),
        in_specs=[SMEM_SPEC] + [VMEM_SPEC] * len(got) + specs_of(after),
        out_specs=[VMEM_SPEC] * ring,
        out_shape=[pltpu.VMEM((rows, columns // ring), BF16)] * ring,
        compiler_params=pltpu.CompilerParams(vmem_limit_bytes=4 * MIB),
        cost_estimate=cost(0.3),
        name="add_split",
    )(place, *kept(*got), *placed(after))


def join_kernel(count, others, place_ref, *refs):
    out_ref = refs[-1]
    wide = refs[0].shape[1]
    for hop in range(count):
        at = lax.rem(place_ref[2] + count - hop, count)
        out_ref[:, pl.ds(pl.multiple_of(at * wide, wide), wide)] = refs[hop][...]


def join_pieces(place, got, after=()):
    rows, columns = got[0].shape
    return pl.pallas_call(
        lambda *refs: join_kernel(len(got), len(after), *refs),
        in_specs=[SMEM_SPEC] + [VMEM_SPEC] * len(got) + specs_of(after),
        out_specs=VMEM_SPEC,
        out_shape=pltpu.VMEM((rows, columns * len(got)), BF16),
        compiler_params=pltpu.CompilerParams(vmem_limit_bytes=4 * MIB),
        cost_estimate=cost(0.3),
        name="join_pieces",
    )(place, *kept(*got), *placed(after))


def unpack_kernel(count, tokens, place_ref, *refs):
    first = refs[:count]
    second = refs[count : 2 * count]
    (
        glu_ref, outr_ref, outi_ref, inr_ref, ini_ref, gain_ref, bias_ref, nu_ref, theta_ref,
        gamma_ref, skip_ref, glub_ref, rms_ref, lines,
    ) = refs[2 * count :]
    width = glu_ref.shape[1] // 2
    states = inr_ref.shape[1]
    high = glu_ref.shape[0] // count
    part = outr_ref.shape[0] // count
    for hop in range(count):
        at = place_ref[1] ^ hop
        rows = pl.ds(pl.multiple_of(at * high, high), high)
        glu_ref[rows, :] = first[hop][:high, :].astype(F32)
        inr_ref[rows, :] = second[hop][:high, :states].astype(F32)
        ini_ref[rows, :] = second[hop][:high, states:].astype(F32)
        few = pl.ds(pl.multiple_of(at * part, part), part)
        outr_ref[few, :] = first[hop][high:, :width].astype(F32)
        outi_ref[few, :] = first[hop][high:, width:].astype(F32)
        lines[pl.ds(pl.multiple_of(at * 8, 8), 8), :] = second[hop][high:, :].astype(F32)[:8]
    half, some = width // 2, states // 2
    per = 8 // count
    line = lambda k: lines[k // per * 8 : k // per * 8 + 1, k % per * half : (k % per + 1) * half]
    gain_ref[...] = line(0)
    bias_ref[...] = line(1)
    nu_ref[...] = line(2)[:, :some]
    theta_ref[...] = line(2)[:, some:]
    gamma_ref[...] = line(3)[:, :some]
    skip_ref[...] = line(4)
    glub_ref[:, :half] = line(5)
    glub_ref[:, half:] = line(6)
    rms_ref[...] = jnp.sqrt(line(7)[:, :3] / tokens)


def unpack(place, first, second, width, states, tokens):
    count = len(first)
    flat = [width // 2, width // 2, states // 2, states // 2, states // 2, width // 2, width, 3]
    return pl.pallas_call(
        lambda *refs: unpack_kernel(count, tokens, *refs),
        in_specs=[SMEM_SPEC] + [VMEM_SPEC] * (2 * count),
        out_specs=[VMEM_SPEC] * 13,
        out_shape=[
            jax.ShapeDtypeStruct((width // 2, 2 * width), F32),
            jax.ShapeDtypeStruct((states // 2, width), F32),
            jax.ShapeDtypeStruct((states // 2, width), F32),
            jax.ShapeDtypeStruct((width // 2, states), F32),
            jax.ShapeDtypeStruct((width // 2, states), F32),
        ]
        + [jax.ShapeDtypeStruct((1, n), F32) for n in flat],
        scratch_shapes=[pltpu.VMEM((8 * count, width), F32)],
        compiler_params=pltpu.CompilerParams(vmem_limit_bytes=8 * MIB),
        name="unpack",
    )(place, *first, *second)


def hops_of(ends, axis, reverse):
    count = lax.axis_size(axis)
    if count <= 4:
        return [
            lax.ppermute(
                ends,
                axis,
                [(i + hop, i) if reverse else (i, i + hop) for i in range(count - hop)],
            )
            for hop in range(1, count)
        ]
    place = lax.axis_index(axis)
    every = lax.all_gather(ends, axis)
    came = []
    for hop in range(1, count):
        source = place + hop if reverse else place - hop
        inside = (source >= 0) & (source < count)
        item = lax.dynamic_index_in_dim(every, jnp.clip(source, 0, count - 1), 0, False)
        came.append(jnp.where(inside, item, 0.0))
    return came


def swap(a):
    return lax.ppermute(a, "fsdp", [(0, 1), (1, 0)])


def swap_moves(axis, bit):
    return [(i, i ^ bit) for i in range(lax.axis_size(axis))]


def scatter_batch(pieces):
    return [pieces[0]] + [
        lax.ppermute(pieces[hop], "batch", swap_moves("batch", hop))
        for hop in range(1, len(pieces))
    ]


def around(pieces):
    ring = lax.axis_size("seq")
    return [pieces[0]] + [
        lax.ppermute(pieces[hop], "seq", [(i, (i + hop) % ring) for i in range(ring)])
        for hop in range(1, ring)
    ]


def share_seq(piece):
    ring = lax.axis_size("seq")
    if ring > 4:
        return [lax.psum(piece.astype(F32), "seq").astype(BF16)]
    return around([piece] * ring)


def gather_batch(piece):
    count = lax.axis_size("batch")
    return [piece] + [
        lax.ppermute(piece, "batch", swap_moves("batch", hop)) for hop in range(1, count)
    ]


def on_device(
    stream, norm_gain, norm_bias, in_real, in_imag, nu_log, theta_log, gamma_log, out_real,
    out_imag, skip_scale, glu_weight, glu_bias, cotangent,
):
    seqs, length, width = stream.shape
    states = 2 * nu_log.shape[0]
    batch = lax.axis_size("batch")
    place = jnp.stack(
        [lax.axis_index("fsdp"), lax.axis_index("batch"), lax.axis_index("seq")]
    ).astype(jnp.int32)
    place, in_real, in_imag, glu_weight, out_real, out_imag = lax.optimization_barrier(
        (place, in_real, in_imag, glu_weight, out_real, out_imag)
    )
    vectors = pack_vectors(
        norm_gain, norm_bias, skip_scale, glu_bias, nu_log, theta_log, gamma_log
    )
    into = [in_real, swap(in_real), in_imag, swap(in_imag)]
    others = [swap(glu_weight), swap(out_real), swap(out_imag)]
    (
        normed, sums, ends, p, q, small, win, wback, square, stream_kept, cot_kept, *own,
    ) = norm_pass(
        place, stream, cotangent, into, [glu_weight, out_real, out_imag], [vectors, swap(vectors)]
    )
    halves = [a for pair_of in zip(own, others) for a in pair_of]
    came = hops_of(ends, "seq", False)
    mixed, back, state, dlru, starts, keep, send, acc, gacc = block_pass(
        place, batch, sums, normed, stream_kept, cot_kept, p, small, halves, came
    )
    later = hops_of(starts, "seq", True)
    pieces = pair_sum(place, keep, swap(send), later)
    first = scatter_batch(pieces)
    ddrive, keep, send = adjoint_pass(
        place, batch, back, state, normed, wback, q, small, square, acc, gacc, later, pieces
    )
    ring = lax.axis_size("seq")
    short = ring <= 4
    first = add_split(place, first, ring if short else 1, [send])
    send, *first = lax.optimization_barrier((send, *first))
    pieces = pair_sum(place, keep, swap(send))
    second = scatter_batch(pieces)
    first = around(first) if short else share_seq(first[0])
    last = lambda seq, earlier, after: input_pass(
        seq, ddrive, dlru, stream_kept, cot_kept, small, wback, earlier, after
    )
    grads = ()
    for seq in range(seqs - 1):
        grads = (last(seq, grads, [first[0], pieces[0]]),)
    first = add_up(first, grads)
    if short:
        first = around([first] * ring)
    second = share_seq(add_up(second, [first[0], *grads]))
    if short:
        first = join_pieces(place, first, [second[0]])
    first = gather_batch(first)
    grads = (last(seqs - 1, grads, [first[0], second[0]]),)
    second = gather_batch(add_up(second, grads))
    grad_stream = grads[0]
    tokens = stream.size * batch * lax.axis_size("seq") * lax.axis_size("fsdp")
    (
        glu, out_r, out_i, in_r, in_i, gain, bias, nu, theta, gamma, skip, glub, rms,
    ) = unpack(place, first, second, width, states, float(tokens))
    flat = lambda a: a.reshape(-1)
    return (
        mixed, grad_stream, flat(gain), flat(bias), in_r, in_i, flat(nu), flat(theta), flat(gamma),
        out_r, out_i, flat(skip), glu, flat(glub), flat(rms),
    )


def solution(mesh):
    tokens = P(("batch", "fsdp"), "seq", None)
    vector = P("fsdp")
    matrix = P("fsdp", None)
    weights = (
        vector, vector, matrix, matrix, vector, vector, vector, matrix, matrix, vector, matrix,
        vector,
    )
    return jax.shard_map(
        on_device,
        mesh=mesh,
        in_specs=(tokens,) + weights + (tokens,),
        out_specs=(tokens, tokens) + weights + (P(),),
        check_vma=False,
    )
```

```python
import functools

import jax
import jax.numpy as jnp
from jax import lax
from jax.experimental import pallas as pl
from jax.experimental.pallas import tpu as pltpu
from jax.sharding import PartitionSpec as P

F32 = jnp.float32
BF16 = jnp.bfloat16
HIGHEST = lax.Precision.HIGHEST
CHUNK = 128
HALF = 64
BLOCK = 512
SUB = 64
TILE = 256
GELU_C = 0.7978845608028654
GELU_K = 0.044715
MIB = 1024 * 1024


def dot_nn(a, b):
    return jnp.dot(a, b, preferred_element_type=F32)


def dot_tn(a, b):
    return lax.dot_general(a, b, (((0,), (0,)), ((), ())), preferred_element_type=F32)


def dot_nt(a, b):
    return lax.dot_general(a, b, (((1,), (1,)), ((), ())), preferred_element_type=F32)


def dot_nt_wide(a, b):
    return lax.dot_general(
        a, b, (((1,), (1,)), ((), ())), precision=HIGHEST, preferred_element_type=F32
    )


def cmul(ar, ai, br, bi):
    return ar * br - ai * bi, ar * bi + ai * br


def fold(v):
    return jnp.sum(v.reshape(v.shape[0] // 8, 8, v.shape[1]), axis=0)


def fold_low(v):
    rows = v.shape[0] // 4
    v = (v[:rows] + v[rows : 2 * rows]) + (v[2 * rows : 3 * rows] + v[3 * rows :])
    return fold(v.astype(F32))


def split_store(stack, k, zr, zi):
    states = zr.shape[1]
    for part, v in enumerate((zr, zi)):
        columns = pl.ds(part * states, states)
        high = v.astype(BF16)
        stack[k, :CHUNK, columns] = high
        stack[k, CHUNK:, columns] = (v - high.astype(F32)).astype(BF16)


def fill_triangle(tri, upper):
    row = lax.broadcasted_iota(jnp.int32, (CHUNK, CHUNK), 0)
    column = lax.broadcasted_iota(jnp.int32, (CHUNK, CHUNK), 1)
    inside = (column >= row) if upper else (column <= row)
    ones = jnp.where(inside, 1.0, 0.0).astype(BF16)
    tri[:, :CHUNK] = ones
    tri[:, CHUNK:] = ones


ROW_STEP = 0
ROW_LAST = 1
ROW_ENTER = 2
ROW_FIRST = 3
ROW_BACK = 4
ROW_WHOLE = 5
ROW_SCALE = 6
ROW_RATE = 7
ROW_GAIN = 8
ROW_BIAS = 9
ROW_SKIP = 10
ROW_GLU = 11
TABLE_ROWS = 16


def pair(ref, row, states):
    return ref[row : row + 1, :states], ref[row : row + 1, states:]


def row_of(ref, row):
    return ref[row : row + 1, :]


def fill_tables(me, own_ref, other_ref, p_ref, q_ref, small_ref, length):
    states = q_ref.shape[1] // 2
    width = q_ref.shape[1]
    own = own_ref[...].astype(F32)
    other = other_ref[...].astype(F32)
    low = jnp.where(me == 0, own, other)
    high = jnp.where(me == 0, other, own)

    def both(first, count):
        rows = [h[first + i : first + i + 1] for h in (low, high) for i in range(count)]
        return jnp.concatenate(rows, axis=1)

    small_ref[...] = jnp.zeros_like(small_ref)
    for row, first in ((ROW_GAIN, 0), (ROW_BIAS, 2), (ROW_SKIP, 4)):
        small_ref[row : row + 1, :] = both(first, 2)
    glu = both(6, 4)
    small_ref[ROW_GLU : ROW_GLU + 1, :] = glu[:, :width]
    small_ref[ROW_GLU + 1 : ROW_GLU + 2, :] = glu[:, width:]
    decay = jnp.exp(both(10, 1))
    rotation = jnp.exp(both(11, 1))
    scale = jnp.exp(both(12, 1))
    steps = (lax.broadcasted_iota(jnp.int32, (CHUNK, states), 0) - HALF).astype(F32)
    turn = steps * rotation
    cos = jnp.cos(turn)
    sin = jnp.sin(turn)
    grow = jnp.exp(-steps * decay)
    p_ref[:, :states] = grow * cos
    p_ref[:, states:] = grow * sin
    shrink = scale * jnp.exp(steps * decay)
    q_ref[:, :states] = shrink * cos
    q_ref[:, states:] = -shrink * sin
    counts = {
        ROW_STEP: CHUNK,
        ROW_LAST: CHUNK - 1 - HALF,
        ROW_ENTER: HALF + 1,
        ROW_FIRST: HALF,
        ROW_BACK: CHUNK - HALF,
        ROW_WHOLE: length,
    }
    assert sorted(counts) == list(range(6))
    index = lax.broadcasted_iota(jnp.int32, (8, states), 0)
    count = jnp.zeros((8, states), F32)
    for row, steps in counts.items():
        count = jnp.where(index == row, float(steps), count)
    size = jnp.exp(-count * decay)
    small_ref[:6, :states] = (size * jnp.cos(count * rotation))[:6]
    small_ref[:6, states:] = (size * jnp.sin(count * rotation))[:6]
    small_ref[ROW_SCALE : ROW_SCALE + 1, :states] = scale
    small_ref[ROW_SCALE : ROW_SCALE + 1, states:] = 1.0 / scale
    small_ref[ROW_RATE : ROW_RATE + 1, :states] = decay
    small_ref[ROW_RATE : ROW_RATE + 1, states:] = rotation


def join_halves(me, whole, own, other, columns=slice(None)):
    rows = own.shape[0]
    whole[pl.ds(pl.multiple_of(me * rows, rows), rows), columns] = own[...]
    whole[pl.ds(pl.multiple_of((1 - me) * rows, rows), rows), columns] = other[...]


def cost(microseconds):
    return pl.CostEstimate(
        flops=0, transcendentals=0, bytes_accessed=int(microseconds * 3.6e6)
    )


def norm_kernel(
    length, place_ref, stream_hbm, cot_hbm, inr_hbm, ini_hbm, glu_hbm, outr_hbm, outi_hbm,
    vec_own, vec_other, inr_other, ini_other,
    normed_ref, sums_ref, end_ref, p_ref, q_ref, small_ref, win_ref, wback_ref, square_ref,
    stream_ref, cot_ref, glu_ref, outr_ref, outi_ref,
    stack, tri, inr_own, ini_own, sems,
):
    states = q_ref.shape[1] // 2
    seqs = stream_ref.shape[0]
    every = range(seqs)
    copy = lambda source, target, k: pltpu.make_async_copy(source, target, sems.at[k])
    weights = [copy(inr_hbm, inr_own, 0), copy(ini_hbm, ini_own, 1)]
    onward = [
        copy(source, target, 2 + k)
        for k, (source, target) in enumerate(
            ((glu_hbm, glu_ref), (outr_hbm, outr_ref), (outi_hbm, outi_ref), (cot_hbm, cot_ref))
        )
    ]

    def stream_copy(step):
        at = (slice(None), pl.ds(pl.multiple_of(step * BLOCK, BLOCK), BLOCK))
        return copy(stream_hbm.at[at], stream_ref.at[at], 6 + step)

    blocks = [stream_copy(step) for step in range(length // BLOCK)]
    for c in blocks[:1] + weights + blocks[1:] + onward:
        c.start()
    me = place_ref[0]
    fill_tables(me, vec_own, vec_other, p_ref, q_ref, small_ref, length)
    fill_triangle(tri, False)
    for c in weights:
        c.wait()
    join_halves(me, win_ref, inr_own, inr_other, slice(0, states))
    join_halves(me, win_ref, ini_own, ini_other, slice(states, 2 * states))
    wback_ref[:, :states] = win_ref[:, :states]
    wback_ref[:, states:] = -win_ref[:, states:]

    gain = row_of(small_ref, ROW_GAIN)
    bias = row_of(small_ref, ROW_BIAS)
    step_r, step_i = pair(small_ref, ROW_STEP, states)
    last_r, last_i = pair(small_ref, ROW_LAST, states)

    def run_block(step, state):
        squares, ends = state
        ends = list(ends)
        base = pl.multiple_of(step * BLOCK, BLOCK)
        rows = pl.ds(base, BLOCK)
        stream_copy(step).wait()
        for r in range(0, BLOCK, SUB):
            for seq in every:
                at = pl.ds(base + r, SUB)
                x = stream_ref[seq, at, :].astype(F32)
                mean = jnp.mean(x, axis=-1, keepdims=True)
                centre = x - mean
                spread = jnp.mean(centre * centre, axis=-1, keepdims=True)
                squares += fold(mean * mean + spread)
                normed_ref[seq, at, :] = (
                    centre * lax.rsqrt(spread + 1e-05) * gain + bias
                ).astype(BF16)
        left = jnp.concatenate([normed_ref[seq, rows, :] for seq in every], axis=0)
        drive = dot_nn(left, win_ref[...])
        for k in range(BLOCK // CHUNK):
            for seq in every:
                first = seq * BLOCK + k * CHUNK
                part = drive[first : first + CHUNK]
                zr, zi = cmul(
                    part[:, :states], part[:, states:], q_ref[:, :states], q_ref[:, states:]
                )
                slot = stack.at[seq]
                split_store(slot, k, zr, zi)
                s = dot_nn(tri[...], slot[k])
                sums_ref[seq, pl.ds(base + k * CHUNK, CHUNK), :] = s
                er, ei = cmul(s[CHUNK - 1 :, :states], s[CHUNK - 1 :, states:], last_r, last_i)
                nr, ni = cmul(*ends[seq], step_r, step_i)
                ends[seq] = nr + er, ni + ei
        return squares, tuple(ends)

    zero = jnp.zeros((1, states), F32)
    squares, ends = lax.fori_loop(
        0, length // BLOCK, run_block, (jnp.zeros((8, 1), F32), ((zero, zero),) * seqs)
    )
    square_ref[...] = jnp.broadcast_to(squares, square_ref.shape)
    for seq in every:
        end_ref[seq, :, :states], end_ref[seq, :, states:] = ends[seq]
    for c in onward:
        c.wait()


HBM_SPEC = pl.BlockSpec(memory_space=pltpu.HBM)
VMEM_SPEC = pl.BlockSpec(memory_space=pltpu.VMEM)
SMEM_SPEC = pl.BlockSpec(memory_space=pltpu.SMEM)


def kept(*arrays):
    return [pltpu.with_memory_space_constraint(a, pltpu.VMEM) for a in arrays]


def large(a):
    return a.size * a.dtype.itemsize > 2 * MIB


def specs_of(arrays):
    return [HBM_SPEC if large(a) else VMEM_SPEC for a in arrays]


def placed(arrays):
    return [in_hbm(a)[0] if large(a) else kept(a)[0] for a in arrays]


def in_hbm(*arrays):
    return [pltpu.with_memory_space_constraint(a, pltpu.HBM) for a in arrays]


def norm_pass(place, stream, cot, into, onward, vectors):
    seqs, length, width = stream.shape
    half, states = into[0].shape
    states2 = 2 * states
    return pl.pallas_call(
        lambda *refs: norm_kernel(length, *refs),
        in_specs=[SMEM_SPEC] + [HBM_SPEC] * 7 + [VMEM_SPEC] * 4,
        out_specs=[VMEM_SPEC] * 14,
        out_shape=[
            pltpu.VMEM((seqs, length, width), BF16),
            pltpu.VMEM((seqs, length, states2), F32),
            pltpu.VMEM((seqs, 1, states2), F32),
            pltpu.VMEM((CHUNK, states2), F32),
            pltpu.VMEM((CHUNK, states2), F32),
            pltpu.VMEM((TABLE_ROWS, states2), F32),
            pltpu.VMEM((width, states2), BF16),
            pltpu.VMEM((width, states2), BF16),
            pltpu.VMEM((8, 128), F32),
            pltpu.VMEM(stream.shape, BF16),
            pltpu.VMEM(cot.shape, BF16),
        ]
        + [pltpu.VMEM(a.shape, BF16) for a in onward],
        scratch_shapes=[
            pltpu.VMEM((seqs, BLOCK // CHUNK, 2 * CHUNK, states2), BF16),
            pltpu.VMEM((CHUNK, 2 * CHUNK), BF16),
            pltpu.VMEM((half, states), BF16),
            pltpu.VMEM((half, states), BF16),
            pltpu.SemaphoreType.DMA((length // BLOCK + 6,)),
        ],
        compiler_params=pltpu.CompilerParams(vmem_limit_bytes=8 * MIB),
        cost_estimate=cost(9),
        name="norm_pass",
    )(
        place,
        *in_hbm(stream, cot, into[0], into[2], *onward),
        *kept(*vectors, into[1], into[3]),
    )


def entering(carry, came, seq, small_ref, states):
    whole_r, whole_i = pair(small_ref, ROW_WHOLE, states)
    total_r = came[0][seq, :, :states]
    total_i = came[0][seq, :, states:]
    power_r, power_i = whole_r, whole_i
    for ref in came[1:]:
        gr, gi = cmul(ref[seq, :, :states], ref[seq, :, states:], power_r, power_i)
        total_r, total_i = total_r + gr, total_i + gi
        power_r, power_i = cmul(power_r, power_i, whole_r, whole_i)
    carry[0:1, :states] = total_r
    carry[0:1, states:] = total_i


def block_kernel(
    hops, place_ref, _, normed_ref, stream_ref, cot_ref, p_ref, small_ref, glu_own, glu_other,
    outr_own, outr_other, outi_own, outi_other, *rest,
):
    came = rest[:hops]
    (
        mixed_hbm, back_ref, state_ref, dlru_ref, start_ref, keep_ref, send_ref, acc_ref, gacc_ref,
        carry, stack, tri, act, dproj, slope, mixed, wglu, wout, dglu, dout, sems,
    ) = rest[hops:]
    states = p_ref.shape[1] // 2
    seqs, _, width = stream_ref.shape
    me = place_ref[0]
    join_halves(me, wglu, glu_own, glu_other)
    join_halves(me, wout.at[pl.ds(0, states)], outr_own, outr_other)
    join_halves(me, wout.at[pl.ds(states, states)], outi_own, outi_other)
    fill_triangle(tri, True)
    acc_ref[...] = jnp.zeros_like(acc_ref)
    gacc_ref[...] = jnp.zeros_like(gacc_ref)
    dglu[...] = jnp.zeros_like(dglu)
    dout[...] = jnp.zeros_like(dout)
    for seq in range(seqs):
        entering(carry.at[seq], came, seq, small_ref, states)
        carry[seq, 1:2, :] = jnp.zeros_like(carry[seq, 1:2, :])
        carry[seq, 2:3, :states] = jnp.ones_like(carry[seq, 2:3, :states])
        carry[seq, 2:3, states:] = jnp.zeros_like(carry[seq, 2:3, states:])

    step_r, step_i = pair(small_ref, ROW_STEP, states)
    last_r, last_i = pair(small_ref, ROW_LAST, states)
    enter_r, enter_i = pair(small_ref, ROW_ENTER, states)
    first_r, first_i = pair(small_ref, ROW_FIRST, states)
    skip = row_of(small_ref, ROW_SKIP)
    value_bias = row_of(small_ref, ROW_GLU)
    gate_bias = row_of(small_ref, ROW_GLU + 1)
    def mixed_copy(step):
        at = pl.ds(pl.multiple_of(step * BLOCK, BLOCK), BLOCK)
        slot = lax.rem(step, 2)
        return pltpu.make_async_copy(mixed.at[slot], mixed_hbm.at[:, at, :], sems.at[slot])

    def run_block(step, _):
        base = pl.multiple_of(step * BLOCK, BLOCK)
        slot = lax.rem(step, 2)
        rows = pl.ds(base, BLOCK)
        pieces = [
            (slice(r, r + SUB), pl.ds(base + r, SUB)) for r in range(0, BLOCK, SUB)
        ]
        chunks = [
            (k, pl.ds(base + k * CHUNK, CHUNK)) for k in range(BLOCK // CHUNK)
        ]
        zeros = jnp.zeros((8, width), F32)
        tiles = lambda count: [slice(n, n + TILE) for n in range(0, count, TILE)]
        spans = tiles(width)
        made = {}
        folds = {}

        def make_states(seq):
            def part(k, at):
                cr, ci = made["carry", seq]
                qr, qi = cmul(cr, ci, enter_r, enter_i)
                sr = back_ref[seq, at, :states]
                si = back_ref[seq, at, states:]
                er, ei = cmul(sr[CHUNK - 1 :], si[CHUNK - 1 :], last_r, last_i)
                nr, ni = cmul(cr, ci, step_r, step_i)
                made["carry", seq] = nr + er, ni + ei
                hr, hi = cmul(sr + qr, si + qi, p_ref[:, :states], p_ref[:, states:])
                state_ref[seq, at, :states] = hr.astype(BF16)
                state_ref[seq, at, states:] = (-hi).astype(BF16)

            def first():
                made["carry", seq] = carry[seq, 0:1, :states], carry[seq, 0:1, states:]

            def last():
                carry[seq, 0:1, :states], carry[seq, 0:1, states:] = made["carry", seq]

            return [first] + [functools.partial(part, *c) for c in chunks] + [last]

        every = range(seqs)
        both = lambda one: jnp.concatenate([one(seq) for seq in every], axis=0)

        def products(name, left, right, columns, turned=False, order=None):
            def part(n):
                if turned:
                    v = dot_nt(both(left), right[n, :])
                else:
                    v = dot_nn(both(left), right[:, n])
                v = v.astype(BF16) if name == "dact" else v
                for seq in every:
                    made.setdefault((name, seq), []).append(v[seq * BLOCK : (seq + 1) * BLOCK])

            return [functools.partial(part, n) for n in (order or tiles(columns))]

        def taken(name, seq, r, first=0, count=None):
            parts = made[name, seq][first:count]
            return jnp.concatenate([v[r] for v in parts], axis=1)

        def gather(name, n, v):
            key = name, n.start
            folds[key] = folds[key] + v if key in folds else v

        def read_out():
            return products("lru", lambda seq: state_ref[seq, rows, :], wout, width)

        def activate(seq, n):
            def part(r, at):
                readout = made["lru", seq][n.start // TILE][r]
                lru = readout + skip[:, n] * normed_ref[seq, at, n].astype(F32)
                lru2 = lru * lru
                gather("lru", n, fold(lru2))
                gate = 0.5 + 0.5 * jnp.tanh(lru * (GELU_C + GELU_C * GELU_K * lru2))
                gelu = lru * gate
                slope[seq, r, n] = (gate + (gelu - gelu * gate) * (
                    2 * GELU_C + 6 * GELU_C * GELU_K * lru2
                )).astype(BF16)
                act[seq, r, n] = gelu.astype(BF16)

            return [functools.partial(part, *c) for c in pieces]

        def project():
            order = [slice(first + n.start, first + n.stop) for n in spans for first in (0, width)]
            return products("projected", lambda seq: act[seq], wglu, 2 * width, order=order)

        def branch_out(seq, n):
            def part(r, at):
                value = made["projected", seq][2 * (n.start // TILE)][r] + value_bias[:, n]
                gate = made["projected", seq][2 * (n.start // TILE) + 1][r] + gate_bias[:, n]
                gate = 0.5 + 0.5 * jnp.tanh(0.5 * gate)
                branch = value * gate
                mixed[slot, seq, r, n] = (stream_ref[seq, at, n].astype(F32) + branch).astype(BF16)
                gather("branch", n, fold(branch * branch))
                cot = cot_ref[seq, at, n].astype(F32)
                part = cot * branch
                dvalue = (cot * gate).astype(BF16)
                dgate = (part - part * gate).astype(BF16)
                dproj[seq, r, n] = dvalue
                dproj[seq, r, slice(width + n.start, width + n.stop)] = dgate
                gather("value", n, fold_low(dvalue))
                gather("gate", n, fold_low(dgate))

            return [functools.partial(part, *c) for c in pieces]

        def project_back():
            return products("dact", lambda seq: dproj[seq], wglu, width, True)

        def activate_back(seq, n):
            def part(r, at):
                dlru = made["dact", seq][n.start // TILE][r] * slope[seq, r, n]
                dlru_ref[seq, at, n] = dlru
                gather("dlru", n, fold_low(dlru))
                gather("skip", n, fold_low(dlru * normed_ref[seq, at, n]))

            return [functools.partial(part, *c) for c in pieces]

        def read_out_back():
            return products("pull", lambda seq: dlru_ref[seq, rows, :], wout, 2 * states, True)

        def glu_back():
            def part(n):
                dglu[:, n] += dot_tn(both(lambda seq: act[seq]), both(lambda seq: dproj[seq, :, n]))

            return [functools.partial(part, n) for n in tiles(2 * width)]

        def out_back():
            def part(n):
                dout[:, n] += dot_tn(
                    both(lambda seq: state_ref[seq, rows, :]), both(lambda seq: dlru_ref[seq, rows, n])
                )

            return [functools.partial(part, n) for n in tiles(width)]

        def turn(seq):
            def part(k, at):
                pull = taken("pull", seq, slice(k * CHUNK, (k + 1) * CHUNK))
                zr, zi = cmul(pull[:, :states], pull[:, states:], p_ref[:, :states], p_ref[:, states:])
                split_store(stack.at[seq], k, zr, zi)

            return [functools.partial(part, *c) for c in chunks]

        def sum_back(seq):
            def part(k, at):
                ar, ai = carry[seq, 1:2, :states], carry[seq, 1:2, states:]
                wr, wi = carry[seq, 2:3, :states], carry[seq, 2:3, states:]
                back = dot_nn(tri[...], stack[seq, k])
                back_ref[seq, at, :] = back
                fr, fi = cmul(back[0:1, :states], back[0:1, states:], first_r, first_i)
                gr, gi = cmul(fr, fi, wr, wi)
                ar, ai = ar + gr, ai + gi
                wr, wi = cmul(wr, wi, step_r, step_i)
                carry[seq, 1:2, :states] = ar
                carry[seq, 1:2, states:] = ai
                carry[seq, 2:3, :states] = wr
                carry[seq, 2:3, states:] = wi
                start_ref[seq, :, :states] = ar
                start_ref[seq, :, states:] = ai

            return [functools.partial(part, *c) for c in chunks]

        def run(*lists):
            parts = [(i / len(one), part) for one in lists for i, part in enumerate(one)]
            for _, part in sorted(parts, key=lambda item: item[0]):
                part()

        run(*[make_states(seq) for seq in every])
        readout = read_out()
        for n, part in zip(spans, readout):
            run([part])
            run(*[activate(seq, n) for seq in every])
        projected = project()

        @pl.when(step >= 2)
        def _():
            mixed_copy(step - 2).wait()

        for k, n in enumerate(spans):
            run(projected[2 * k : 2 * k + 2])
            run(*[branch_out(seq, n) for seq in every])
        mixed_copy(step).start()
        for n, part in zip(spans, project_back()):
            run([part])
            run(*[activate_back(seq, n) for seq in every])
        run(glu_back())
        run(read_out_back())
        run(*[turn(seq) for seq in every], out_back())
        run(*[sum_back(seq) for seq in every])
        for row, name in enumerate(("lru", "branch", "dlru", "skip")):
            for n in spans:
                acc_ref[8 * row : 8 * row + 8, n] += folds[name, n.start]
        for row, name in enumerate(("value", "gate")):
            for n in spans:
                gacc_ref[8 * row : 8 * row + 8, n] += folds[name, n.start]

        return 0

    steps = stream_ref.shape[1] // BLOCK
    lax.fori_loop(0, steps, run_block, 0)
    for step in range(max(steps - 2, 0), steps):
        mixed_copy(jnp.int32(step)).wait()
    batch, height, _ = keep_ref.shape
    high = width // (2 * batch)
    part = height - high
    for ref, f in ((keep_ref, place_ref[0]), (send_ref, 1 - place_ref[0])):
        for b in range(batch):
            first = pl.multiple_of((f * batch + b) * high, high)
            ref[b, :high, :] = dglu[pl.ds(first, high), :].astype(BF16)
            first = pl.multiple_of((f * batch + b) * part, part)
            ref[b, high:, :width] = dout[pl.ds(first, part), :].astype(BF16)
            ref[b, high:, width:] = dout[pl.ds(states + first, part), :].astype(BF16)


def block_pass(place, batch, sums, normed, stream, cot, p, small, halves, came):
    seqs, length, width = stream.shape
    states2 = p.shape[1]
    height = width // (2 * batch) + states2 // (4 * batch)
    return pl.pallas_call(
        lambda *refs: block_kernel(len(came), *refs),
        in_specs=[SMEM_SPEC] + [VMEM_SPEC] * (12 + len(came)),
        out_specs=[HBM_SPEC] + [VMEM_SPEC] * 8,
        out_shape=[
            pltpu.HBM((seqs, length, width), BF16),
            pltpu.VMEM((seqs, length, states2), F32),
            pltpu.VMEM((seqs, length, states2), BF16),
            pltpu.VMEM((seqs, length, width), BF16),
            jax.ShapeDtypeStruct((seqs, 1, states2), F32),
            pltpu.VMEM((batch, height, 2 * width), BF16),
            pltpu.VMEM((batch, height, 2 * width), BF16),
            pltpu.VMEM((32, width), F32),
            pltpu.VMEM((16, width), F32),
        ],
        scratch_shapes=[
            pltpu.VMEM((seqs, 8, states2), F32),
            pltpu.VMEM((seqs, BLOCK // CHUNK, 2 * CHUNK, states2), BF16),
            pltpu.VMEM((CHUNK, 2 * CHUNK), BF16),
            pltpu.VMEM((seqs, BLOCK, width), BF16),
            pltpu.VMEM((seqs, BLOCK, 2 * width), BF16),
            pltpu.VMEM((seqs, BLOCK, width), BF16),
            pltpu.VMEM((2, seqs, BLOCK, width), BF16),
            pltpu.VMEM((width, 2 * width), BF16),
            pltpu.VMEM((states2, width), BF16),
            pltpu.VMEM((width, 2 * width), F32),
            pltpu.VMEM((states2, width), F32),
            pltpu.SemaphoreType.DMA((2,)),
        ],
        input_output_aliases={1: 1},
        compiler_params=pltpu.CompilerParams(vmem_limit_bytes=20 * MIB),
        cost_estimate=cost(28),
        name="block_pass",
    )(place, *kept(sums, normed, stream, cot, p, small, *halves, *came))


def adjoint_kernel(
    hops, others, place_ref, back_ref, _, normed_ref, win_ref, q_ref, small_ref, square_ref, acc_ref, gacc_ref,
    *rest,
):
    came = rest[:hops]
    ddrive_ref, keep_ref, send_ref, carry, din = rest[hops + others :]
    states = q_ref.shape[1] // 2
    seqs, length, _ = normed_ref.shape
    every = range(seqs)
    first_r, first_i = pair(small_ref, ROW_FIRST, states)
    back_r, back_i = pair(small_ref, ROW_BACK, states)
    carries = []
    for seq in every:
        entering(carry, came, seq, small_ref, states)
        carries.append((carry[0:1, :states], carry[0:1, states:]))
    real_sum = imag_sum = real_total = imag_total = jnp.zeros((8, states), F32)
    for base in reversed(range(0, length, BLOCK)):
        for k in reversed(range(BLOCK // CHUNK)):
            for seq in every:
                at = pl.ds(base + k * CHUNK, CHUNK)
                qr, qi = cmul(*carries[seq], back_r, back_i)
                vr = back_ref[seq, at, :states] + qr
                vi = back_ref[seq, at, states:] + qi
                carries[seq] = cmul(vr[0:1], vi[0:1], first_r, first_i)
                ar, ai = cmul(vr, vi, q_ref[:, :states], q_ref[:, states:])
                hr = ddrive_ref[seq, at, :states]
                hi = ddrive_ref[seq, at, states:]
                lr, li = ar.astype(BF16), ai.astype(BF16)
                real_sum += fold((lr * hr).astype(F32) + (li * hi).astype(F32))
                imag_sum += fold((lr * hi).astype(F32) - (li * hr).astype(F32))
                real_total += fold_low(lr)
                imag_total += fold_low(li)
                ddrive_ref[seq, at, :states] = lr
                ddrive_ref[seq, at, states:] = li
        rows = pl.ds(base, BLOCK)
        product = dot_tn(
            jnp.concatenate([normed_ref[seq, rows, :] for seq in every], axis=0),
            jnp.concatenate([ddrive_ref[seq, rows, :] for seq in every], axis=0),
        )
        if base == length - BLOCK:
            din[...] = product
        else:
            din[...] += product
    width = din.shape[0]
    gain = row_of(small_ref, ROW_GAIN)
    bias = row_of(small_ref, ROW_BIAS)
    skip = row_of(small_ref, ROW_SKIP)
    weight = win_ref[...].astype(F32)
    grad = din[...]
    in_r, in_i = weight[:, :states], weight[:, states:]
    g_r, g_i = grad[:, :states], grad[:, states:]
    x_r = jnp.sum(g_r * in_r + g_i * in_i, axis=0, keepdims=True)
    x_i = jnp.sum(g_r * in_i - g_i * in_r, axis=0, keepdims=True)
    inverse = small_ref[ROW_SCALE : ROW_SCALE + 1, states:]
    column = lambda v: jnp.sum(v, axis=0, keepdims=True)
    d_r = column(real_sum) * inverse - x_r
    d_i = column(imag_sum) * inverse - x_i
    decay, rotation = pair(small_ref, ROW_RATE, states)
    gathered = dot_nt_wide(jnp.ones((8, 2 * states), F32), weight * grad)[0:1]
    total = jnp.broadcast_to(jnp.concatenate([column(real_total), column(imag_total)], axis=1), (8, 2 * states))
    d_lru = column(acc_ref[16:24, :])
    d_skip = column(acc_ref[24:32, :])
    d_bias = dot_nt_wide(total, weight)[0:1] + skip * d_lru
    d_gain = (gathered + skip * d_skip - bias * d_bias) / gain
    d_nu = -decay * d_r
    d_theta = rotation * d_i
    d_values = column(gacc_ref[0:8, :])
    d_gates = column(gacc_ref[8:16, :])
    lane = lax.broadcasted_iota(jnp.int32, (1, width // 2), 1)
    squares = jnp.zeros((1, width // 2), F32)
    sums = (
        width * jnp.sum(square_ref[:, 0:1]), jnp.sum(acc_ref[0:8, :]), jnp.sum(acc_ref[8:16, :]),
    )
    for place, v in enumerate(sums):
        squares = jnp.where(lane == place, v, squares)
    half, some = width // 2, states // 2
    batch, height, _ = keep_ref.shape
    high = width // (2 * batch)
    me = place_ref[0]

    def chosen(f, low, up):
        return jnp.where(f == 0, low, up)

    for ref, f in ((keep_ref, me), (send_ref, 1 - me)):
        wide = lambda v: chosen(f, v[:, :half], v[:, half:])
        thin = lambda v: chosen(f, v[:, :some], v[:, some:])
        d_glu = chosen(f, d_values, d_gates)
        lines = (
            wide(d_gain),
            wide(d_bias),
            jnp.concatenate([thin(d_nu), thin(d_theta)], axis=1),
            jnp.concatenate([thin(x_r), jnp.zeros((1, some), F32)], axis=1),
            wide(d_skip),
            d_glu[:, :half],
            d_glu[:, half:],
            squares,
        )
        for b in range(batch):
            first = pl.multiple_of((f * batch + b) * high, high)
            ref[b, :high, :states] = din[pl.ds(first, high), :states].astype(BF16)
            ref[b, :high, states:] = (-din[pl.ds(first, high), states:]).astype(BF16)
            line = jnp.concatenate(lines[b * 8 // batch : (b + 1) * 8 // batch], axis=1)
            line = jnp.broadcast_to(line, (height - high, width)).astype(BF16)
            ref[b, high:, :] = line


def adjoint_pass(
    place, batch, back, state, normed, wback, q, small, square, acc, gacc, came, after
):
    seqs, length, width = normed.shape
    states2 = q.shape[1]
    return pl.pallas_call(
        lambda *refs: adjoint_kernel(len(came), len(after), *refs),
        in_specs=[SMEM_SPEC] + [VMEM_SPEC] * (9 + len(came)) + specs_of(after),
        out_specs=[VMEM_SPEC] * 3,
        out_shape=[
            pltpu.VMEM((seqs, length, states2), BF16),
            pltpu.VMEM((batch, width // (2 * batch) + 16, states2), BF16),
            pltpu.VMEM((batch, width // (2 * batch) + 16, states2), BF16),
        ],
        scratch_shapes=[
            pltpu.VMEM((8, states2), F32),
            pltpu.VMEM((width, states2), F32),
        ],
        input_output_aliases={2: 0},
        compiler_params=pltpu.CompilerParams(vmem_limit_bytes=8 * MIB),
        cost_estimate=cost(7),
        name="adjoint_pass",
    )(place, *kept(back, state, normed, wback, q, small, square, acc, gacc, *came), *placed(after))


def input_kernel(seq, ddrive_ref, dlru_ref, stream_ref, cot_ref, small_ref, win_ref, *rest):
    out_ref = rest[-1]
    base = pl.program_id(0) * BLOCK
    gain = row_of(small_ref, ROW_GAIN)
    skip = row_of(small_ref, ROW_SKIP)
    rows = pl.ds(pl.multiple_of(base, BLOCK), BLOCK)
    pulled = dot_nt(ddrive_ref[seq, rows, :], win_ref[...])
    for r in range(0, BLOCK, SUB):
        at = pl.ds(pl.multiple_of(base + r, SUB), SUB)
        d = pulled[r : r + SUB] + skip * dlru_ref[seq, at, :].astype(F32)
        x = stream_ref[seq, at, :].astype(F32)
        centre = x - jnp.mean(x, axis=-1, keepdims=True)
        spread = jnp.mean(centre * centre, axis=-1, keepdims=True)
        inverse = lax.rsqrt(spread + 1e-05)
        hat = centre * inverse
        dhat = d * gain
        m1 = jnp.mean(dhat, axis=-1, keepdims=True)
        m2 = jnp.mean(dhat * hat, axis=-1, keepdims=True)
        out_ref[r : r + SUB, :] = (dhat - m1 - hat * m2) * inverse + cot_ref[seq, at, :].astype(F32)


def input_pass(seq, ddrive, dlru, stream, cot, small, win, earlier, after):
    seqs, length, width = stream.shape
    earlier = in_hbm(*earlier)
    return pl.pallas_call(
        lambda *refs: input_kernel(seq, *refs),
        grid=(length // BLOCK,),
        in_specs=[VMEM_SPEC] * 6 + [HBM_SPEC] * len(earlier) + specs_of(after),
        out_specs=pl.BlockSpec((None, BLOCK, width), lambda i: (seq, i, 0)),
        out_shape=pltpu.HBM((seqs, length, width), F32),
        input_output_aliases={6: 0} if earlier else {},
        compiler_params=pltpu.CompilerParams(vmem_limit_bytes=8 * MIB),
        cost_estimate=cost(4),
        name="input_pass",
    )(*kept(ddrive, dlru, stream, cot, small, win), *earlier, *placed(after))


def pack_kernel(count, *refs):
    out_ref = refs[count]
    parts = refs[count + 1 : -1]
    copies = [
        pltpu.make_async_copy(source, target, refs[-1].at[k])
        for k, (source, target) in enumerate(zip(refs[:count], parts))
    ]
    for c in copies:
        c.start()
    for c in copies:
        c.wait()
    row = 0
    for ref in parts:
        for first in range(0, ref.shape[0], 128):
            out_ref[row : row + 1, :] = ref[first : first + 128].reshape(1, 128)
            row += 1


def pack_vectors(*vectors):
    rows = sum(v.shape[0] for v in vectors) // 128
    return pl.pallas_call(
        lambda *refs: pack_kernel(len(vectors), *refs),
        in_specs=[HBM_SPEC] * len(vectors),
        out_specs=VMEM_SPEC,
        out_shape=pltpu.VMEM((rows, 128), BF16),
        scratch_shapes=[pltpu.VMEM(v.shape, BF16) for v in vectors]
        + [pltpu.SemaphoreType.DMA((len(vectors),))],
        compiler_params=pltpu.CompilerParams(vmem_limit_bytes=2 * MIB),
        name="pack_vectors",
    )(*in_hbm(*vectors))


def pair_kernel(others, place_ref, keep_ref, came_ref, *rest):
    for hop, ref in enumerate(rest[others:]):
        at = place_ref[1] ^ hop
        ref[...] = (keep_ref[at].astype(F32) + came_ref[at].astype(F32)).astype(BF16)


def pair_sum(place, keep, came, after=()):
    count = keep.shape[0]
    return pl.pallas_call(
        lambda *refs: pair_kernel(len(after), *refs),
        in_specs=[SMEM_SPEC] + [VMEM_SPEC] * 2 + specs_of(after),
        out_specs=[VMEM_SPEC] * count,
        out_shape=[pltpu.VMEM(keep.shape[1:], BF16)] * count,
        compiler_params=pltpu.CompilerParams(vmem_limit_bytes=4 * MIB),
        cost_estimate=cost(0.7),
        name="pair_sum",
    )(place, *kept(keep, came), *placed(after))


def add_kernel(count, *refs):
    total = refs[0][...].astype(F32)
    for ref in refs[1:count]:
        total += ref[...].astype(F32)
    refs[-1][...] = total.astype(BF16)


def add_up(got, after=()):
    return pl.pallas_call(
        lambda *refs: add_kernel(len(got), *refs),
        in_specs=[VMEM_SPEC] * len(got) + specs_of(after),
        out_specs=VMEM_SPEC,
        out_shape=pltpu.VMEM(got[0].shape, BF16),
        compiler_params=pltpu.CompilerParams(vmem_limit_bytes=4 * MIB),
        cost_estimate=cost(0.2),
        name="add_up",
    )(*kept(*got), *placed(after))


def split_kernel(count, others, place_ref, *refs):
    total = refs[0]
    pieces = refs[count + others :]
    wide = total.shape[1] // len(pieces)
    for hop, ref in enumerate(pieces):
        at = lax.rem(place_ref[2] + hop, len(pieces))
        columns = pl.ds(pl.multiple_of(at * wide, wide), wide)
        v = refs[0][:, columns].astype(F32)
        for other in refs[1:count]:
            v += other[:, columns].astype(F32)
        ref[...] = v.astype(BF16)


def add_split(place, got, ring, after=()):
    rows, columns = got[0].shape
    return pl.pallas_call(
        lambda *refs: split_kernel(len(got), len(after), *refs),
        in_specs=[SMEM_SPEC] + [VMEM_SPEC] * len(got) + specs_of(after),
        out_specs=[VMEM_SPEC] * ring,
        out_shape=[pltpu.VMEM((rows, columns // ring), BF16)] * ring,
        compiler_params=pltpu.CompilerParams(vmem_limit_bytes=4 * MIB),
        cost_estimate=cost(0.3),
        name="add_split",
    )(place, *kept(*got), *placed(after))


def finish_kernel(count, place_ref, *refs):
    first, second, out_ref = refs[:count], refs[count : 2 * count], refs[-1]
    rows, wide = first[0].shape
    span = out_ref.shape[1]
    for hop in range(count):
        at = lax.rem(place_ref[2] + count - hop, count)
        if wide < span:
            per = span // wide
            row = pl.multiple_of(lax.div(at, per) * rows, rows)
            column = pl.multiple_of(lax.rem(at, per) * wide, wide)
            out_ref[pl.ds(row, rows), pl.ds(column, wide)] = first[hop][...]
        else:
            for k in range(wide // span):
                row = pl.multiple_of((at * (wide // span) + k) * rows, rows)
                out_ref[pl.ds(row, rows), :] = first[hop][:, k * span : (k + 1) * span]
    total = second[0][...].astype(F32)
    for ref in second[1:]:
        total += ref[...].astype(F32)
    out_ref[out_ref.shape[0] - total.shape[0] :, :] = total.astype(BF16)


def finish_seq(place, first, second, after):
    rows, wide = first[0].shape
    low, span = second[0].shape
    height = rows * wide * len(first) // span + low
    return pl.pallas_call(
        lambda *refs: finish_kernel(len(first), *refs),
        in_specs=[SMEM_SPEC] + [VMEM_SPEC] * (2 * len(first)) + specs_of(after),
        out_specs=VMEM_SPEC,
        out_shape=pltpu.VMEM((height, span), BF16),
        compiler_params=pltpu.CompilerParams(vmem_limit_bytes=4 * MIB),
        cost_estimate=cost(0.5),
        name="finish_seq",
    )(place, *kept(*first, *second), *placed(after))


def unpack_kernel(count, tokens, place_ref, *refs):
    got = refs[:count]
    (
        glu_ref, outr_ref, outi_ref, inr_ref, ini_ref, gain_ref, bias_ref, nu_ref, theta_ref,
        gamma_ref, skip_ref, glub_ref, rms_ref, lines,
    ) = refs[count:]
    width = glu_ref.shape[1] // 2
    states = inr_ref.shape[1]
    high = glu_ref.shape[0] // count
    part = outr_ref.shape[0] // count
    low = 2 * (high + part)
    for hop in range(count):
        at = place_ref[1] ^ hop
        v = got[hop]
        rows = pl.ds(pl.multiple_of(at * high, high), high)
        few = pl.ds(pl.multiple_of(at * part, part), part)
        glu_ref[rows, :width] = v[:high, :].astype(F32)
        outr_ref[few, :] = v[high : high + part, :].astype(F32)
        glu_ref[rows, width:] = v[high + part : 2 * high + part, :].astype(F32)
        outi_ref[few, :] = v[2 * high + part : low, :].astype(F32)
        inr_ref[rows, :] = v[low : low + high, :states].astype(F32)
        ini_ref[rows, :] = v[low : low + high, states:].astype(F32)
        lines[pl.ds(pl.multiple_of(at * 8, 8), 8), :] = v[low + high :, :].astype(F32)[:8]
    half, some = width // 2, states // 2
    per = 8 // count
    line = lambda k: lines[k // per * 8 : k // per * 8 + 1, k % per * half : (k % per + 1) * half]
    gain_ref[...] = line(0)
    bias_ref[...] = line(1)
    nu_ref[...] = line(2)[:, :some]
    theta_ref[...] = line(2)[:, some:]
    gamma_ref[...] = line(3)[:, :some]
    skip_ref[...] = line(4)
    glub_ref[:, :half] = line(5)
    glub_ref[:, half:] = line(6)
    rms_ref[...] = jnp.sqrt(line(7)[:, :3] / tokens)


def unpack(place, got, width, states, tokens):
    count = len(got)
    flat = [width // 2, width // 2, states // 2, states // 2, states // 2, width // 2, width, 3]
    return pl.pallas_call(
        lambda *refs: unpack_kernel(count, tokens, *refs),
        in_specs=[SMEM_SPEC] + [VMEM_SPEC] * count,
        out_specs=[VMEM_SPEC] * 13,
        out_shape=[
            jax.ShapeDtypeStruct((width // 2, 2 * width), F32),
            jax.ShapeDtypeStruct((states // 2, width), F32),
            jax.ShapeDtypeStruct((states // 2, width), F32),
            jax.ShapeDtypeStruct((width // 2, states), F32),
            jax.ShapeDtypeStruct((width // 2, states), F32),
        ]
        + [jax.ShapeDtypeStruct((1, n), F32) for n in flat],
        scratch_shapes=[pltpu.VMEM((8 * count, width), F32)],
        compiler_params=pltpu.CompilerParams(vmem_limit_bytes=8 * MIB),
        name="unpack",
    )(place, *got)


def hops_of(ends, axis, reverse):
    count = lax.axis_size(axis)
    if count <= 4:
        return [
            lax.ppermute(
                ends,
                axis,
                [(i + hop, i) if reverse else (i, i + hop) for i in range(count - hop)],
            )
            for hop in range(1, count)
        ]
    place = lax.axis_index(axis)
    every = lax.all_gather(ends, axis)
    came = []
    for hop in range(1, count):
        source = place + hop if reverse else place - hop
        inside = (source >= 0) & (source < count)
        item = lax.dynamic_index_in_dim(every, jnp.clip(source, 0, count - 1), 0, False)
        came.append(jnp.where(inside, item, 0.0))
    return came


def swap(a):
    return lax.ppermute(a, "fsdp", [(0, 1), (1, 0)])


def swap_moves(axis, bit):
    return [(i, i ^ bit) for i in range(lax.axis_size(axis))]


def scatter_batch(pieces):
    return [pieces[0]] + [
        lax.ppermute(pieces[hop], "batch", swap_moves("batch", hop))
        for hop in range(1, len(pieces))
    ]


def around(pieces):
    ring = lax.axis_size("seq")
    return [pieces[0]] + [
        lax.ppermute(pieces[hop], "seq", [(i, (i + hop) % ring) for i in range(ring)])
        for hop in range(1, ring)
    ]


def share_seq(piece):
    ring = lax.axis_size("seq")
    if ring > 4:
        return [lax.psum(piece.astype(F32), "seq").astype(BF16)]
    return around([piece] * ring)


def gather_batch(piece):
    count = lax.axis_size("batch")
    return [piece] + [
        lax.ppermute(piece, "batch", swap_moves("batch", hop)) for hop in range(1, count)
    ]


def on_device(
    stream, norm_gain, norm_bias, in_real, in_imag, nu_log, theta_log, gamma_log, out_real,
    out_imag, skip_scale, glu_weight, glu_bias, cotangent,
):
    seqs, length, width = stream.shape
    states = 2 * nu_log.shape[0]
    batch = lax.axis_size("batch")
    place = jnp.stack(
        [lax.axis_index("fsdp"), lax.axis_index("batch"), lax.axis_index("seq")]
    ).astype(jnp.int32)
    place, in_real, in_imag, glu_weight, out_real, out_imag = lax.optimization_barrier(
        (place, in_real, in_imag, glu_weight, out_real, out_imag)
    )
    vectors = pack_vectors(
        norm_gain, norm_bias, skip_scale, glu_bias, nu_log, theta_log, gamma_log
    )
    into = [in_real, swap(in_real), in_imag, swap(in_imag)]
    others = [swap(glu_weight), swap(out_real), swap(out_imag)]
    (
        normed, sums, ends, p, q, small, win, wback, square, stream_kept, cot_kept, *own,
    ) = norm_pass(
        place, stream, cotangent, into, [glu_weight, out_real, out_imag], [vectors, swap(vectors)]
    )
    halves = [a for pair_of in zip(own, others) for a in pair_of]
    came = hops_of(ends, "seq", False)
    mixed, back, state, dlru, starts, keep, send, acc, gacc = block_pass(
        place, batch, sums, normed, stream_kept, cot_kept, p, small, halves, came
    )
    later = hops_of(starts, "seq", True)
    pieces = pair_sum(place, keep, swap(send), later)
    first = scatter_batch(pieces)
    ddrive, keep, send = adjoint_pass(
        place, batch, back, state, normed, wback, q, small, square, acc, gacc, later, pieces
    )
    ring = lax.axis_size("seq")
    short = ring <= 4
    first = add_split(place, first, ring if short else 1, [send])
    send, *first = lax.optimization_barrier((send, *first))
    pieces = pair_sum(place, keep, swap(send))
    second = scatter_batch(pieces)
    first = around(first) if short else share_seq(first[0])
    last = lambda seq, earlier, after: input_pass(
        seq, ddrive, dlru, stream_kept, cot_kept, small, wback, earlier, after
    )
    grads = ()
    for seq in range(seqs - 1):
        grads = (last(seq, grads, [first[0], pieces[0]]),)
    first = add_up(first, grads)
    if short:
        first = around([first] * ring)
    second = share_seq(add_up(second, [first[0], *grads]))
    grads = (last(seqs - 1, grads, [first[0], second[0]]),)
    got = gather_batch(finish_seq(place, first if short else [first], second, grads))
    grad_stream = grads[0]
    tokens = stream.size * batch * lax.axis_size("seq") * lax.axis_size("fsdp")
    (
        glu, out_r, out_i, in_r, in_i, gain, bias, nu, theta, gamma, skip, glub, rms,
    ) = unpack(place, got, width, states, float(tokens))
    flat = lambda a: a.reshape(-1)
    return (
        mixed, grad_stream, flat(gain), flat(bias), in_r, in_i, flat(nu), flat(theta), flat(gamma),
        out_r, out_i, flat(skip), glu, flat(glub), flat(rms),
    )


def solution(mesh):
    tokens = P(("batch", "fsdp"), "seq", None)
    vector = P("fsdp")
    matrix = P("fsdp", None)
    weights = (
        vector, vector, matrix, matrix, vector, vector, vector, matrix, matrix, vector, matrix,
        vector,
    )
    return jax.shard_map(
        on_device,
        mesh=mesh,
        in_specs=(tokens,) + weights + (tokens,),
        out_specs=(tokens, tokens) + weights + (P(),),
        check_vma=False,
    )
```

```python
import functools

import jax
import jax.numpy as jnp
from jax import lax
from jax.experimental import pallas as pl
from jax.experimental.pallas import tpu as pltpu
from jax.sharding import PartitionSpec as P

F32 = jnp.float32
BF16 = jnp.bfloat16
HIGHEST = lax.Precision.HIGHEST
CHUNK = 128
HALF = 64
BLOCK = 512
SUB = 64
TILE = 256
GELU_C = 0.7978845608028654
GELU_K = 0.044715
MIB = 1024 * 1024


def dot_nn(a, b):
    return jnp.dot(a, b, preferred_element_type=F32)


def dot_tn(a, b):
    return lax.dot_general(a, b, (((0,), (0,)), ((), ())), preferred_element_type=F32)


def dot_nt(a, b):
    return lax.dot_general(a, b, (((1,), (1,)), ((), ())), preferred_element_type=F32)


def dot_nt_wide(a, b):
    return lax.dot_general(
        a, b, (((1,), (1,)), ((), ())), precision=HIGHEST, preferred_element_type=F32
    )


def cmul(ar, ai, br, bi):
    return ar * br - ai * bi, ar * bi + ai * br


def fold(v):
    return jnp.sum(v.reshape(v.shape[0] // 8, 8, v.shape[1]), axis=0)


def fold_low(v):
    rows = v.shape[0] // 4
    v = (v[:rows] + v[rows : 2 * rows]) + (v[2 * rows : 3 * rows] + v[3 * rows :])
    return fold(v.astype(F32))


def split_store(stack, k, zr, zi):
    states = zr.shape[1]
    for part, v in enumerate((zr, zi)):
        columns = pl.ds(part * states, states)
        high = v.astype(BF16)
        stack[k, :CHUNK, columns] = high
        stack[k, CHUNK:, columns] = (v - high.astype(F32)).astype(BF16)


def fill_triangle(tri, upper):
    row = lax.broadcasted_iota(jnp.int32, (CHUNK, CHUNK), 0)
    column = lax.broadcasted_iota(jnp.int32, (CHUNK, CHUNK), 1)
    inside = (column >= row) if upper else (column <= row)
    ones = jnp.where(inside, 1.0, 0.0).astype(BF16)
    tri[:, :CHUNK] = ones
    tri[:, CHUNK:] = ones


ROW_STEP = 0
ROW_LAST = 1
ROW_ENTER = 2
ROW_FIRST = 3
ROW_BACK = 4
ROW_WHOLE = 5
ROW_SCALE = 6
ROW_RATE = 7
ROW_GAIN = 8
ROW_BIAS = 9
ROW_SKIP = 10
ROW_GLU = 11
TABLE_ROWS = 16


def pair(ref, row, states):
    return ref[row : row + 1, :states], ref[row : row + 1, states:]


def row_of(ref, row):
    return ref[row : row + 1, :]


def fill_tables(me, own_ref, other_ref, p_ref, q_ref, small_ref, length):
    states = q_ref.shape[1] // 2
    width = q_ref.shape[1]
    own = own_ref[...].astype(F32)
    other = other_ref[...].astype(F32)
    low = jnp.where(me == 0, own, other)
    high = jnp.where(me == 0, other, own)

    def both(first, count):
        rows = [h[first + i : first + i + 1] for h in (low, high) for i in range(count)]
        return jnp.concatenate(rows, axis=1)

    small_ref[...] = jnp.zeros_like(small_ref)
    for row, first in ((ROW_GAIN, 0), (ROW_BIAS, 2), (ROW_SKIP, 4)):
        small_ref[row : row + 1, :] = both(first, 2)
    glu = both(6, 4)
    small_ref[ROW_GLU : ROW_GLU + 1, :] = glu[:, :width]
    small_ref[ROW_GLU + 1 : ROW_GLU + 2, :] = glu[:, width:]
    decay = jnp.exp(both(10, 1))
    rotation = jnp.exp(both(11, 1))
    scale = jnp.exp(both(12, 1))
    steps = (lax.broadcasted_iota(jnp.int32, (CHUNK, states), 0) - HALF).astype(F32)
    turn = steps * rotation
    cos = jnp.cos(turn)
    sin = jnp.sin(turn)
    grow = jnp.exp(-steps * decay)
    p_ref[:, :states] = grow * cos
    p_ref[:, states:] = grow * sin
    shrink = scale * jnp.exp(steps * decay)
    q_ref[:, :states] = shrink * cos
    q_ref[:, states:] = -shrink * sin
    counts = {
        ROW_STEP: CHUNK,
        ROW_LAST: CHUNK - 1 - HALF,
        ROW_ENTER: HALF + 1,
        ROW_FIRST: HALF,
        ROW_BACK: CHUNK - HALF,
        ROW_WHOLE: length,
    }
    assert sorted(counts) == list(range(6))
    index = lax.broadcasted_iota(jnp.int32, (8, states), 0)
    count = jnp.zeros((8, states), F32)
    for row, steps in counts.items():
        count = jnp.where(index == row, float(steps), count)
    size = jnp.exp(-count * decay)
    small_ref[:6, :states] = (size * jnp.cos(count * rotation))[:6]
    small_ref[:6, states:] = (size * jnp.sin(count * rotation))[:6]
    small_ref[ROW_SCALE : ROW_SCALE + 1, :states] = scale
    small_ref[ROW_SCALE : ROW_SCALE + 1, states:] = 1.0 / scale
    small_ref[ROW_RATE : ROW_RATE + 1, :states] = decay
    small_ref[ROW_RATE : ROW_RATE + 1, states:] = rotation


def join_halves(me, whole, own, other, columns=slice(None)):
    rows = own.shape[0]
    whole[pl.ds(pl.multiple_of(me * rows, rows), rows), columns] = own[...]
    whole[pl.ds(pl.multiple_of((1 - me) * rows, rows), rows), columns] = other[...]


def cost(microseconds):
    return pl.CostEstimate(
        flops=0, transcendentals=0, bytes_accessed=int(microseconds * 3.6e6)
    )


def norm_kernel(
    length, place_ref, stream_hbm, cot_hbm, inr_hbm, ini_hbm, glu_hbm, outr_hbm, outi_hbm,
    vec_own, vec_other, inr_other, ini_other,
    normed_ref, sums_ref, end_ref, p_ref, q_ref, small_ref, win_ref, wback_ref, square_ref,
    stream_ref, cot_ref, glu_ref, outr_ref, outi_ref,
    stack, tri, inr_own, ini_own, sems,
):
    states = q_ref.shape[1] // 2
    seqs = stream_ref.shape[0]
    every = range(seqs)
    copy = lambda source, target, k: pltpu.make_async_copy(source, target, sems.at[k])
    weights = [copy(inr_hbm, inr_own, 0), copy(ini_hbm, ini_own, 1)]
    onward = [
        copy(source, target, 2 + k)
        for k, (source, target) in enumerate(
            ((glu_hbm, glu_ref), (outr_hbm, outr_ref), (outi_hbm, outi_ref), (cot_hbm, cot_ref))
        )
    ]

    def stream_copy(step):
        at = (slice(None), pl.ds(pl.multiple_of(step * BLOCK, BLOCK), BLOCK))
        return copy(stream_hbm.at[at], stream_ref.at[at], 6 + step)

    blocks = [stream_copy(step) for step in range(length // BLOCK)]
    for c in blocks[:1] + weights + blocks[1:] + onward:
        c.start()
    me = place_ref[0]
    fill_tables(me, vec_own, vec_other, p_ref, q_ref, small_ref, length)
    fill_triangle(tri, False)
    for c in weights:
        c.wait()
    join_halves(me, win_ref, inr_own, inr_other, slice(0, states))
    join_halves(me, win_ref, ini_own, ini_other, slice(states, 2 * states))
    wback_ref[:, :states] = win_ref[:, :states]
    wback_ref[:, states:] = -win_ref[:, states:]

    gain = row_of(small_ref, ROW_GAIN)
    bias = row_of(small_ref, ROW_BIAS)
    step_r, step_i = pair(small_ref, ROW_STEP, states)
    last_r, last_i = pair(small_ref, ROW_LAST, states)

    def run_block(step, state):
        squares, ends = state
        ends = list(ends)
        base = pl.multiple_of(step * BLOCK, BLOCK)
        rows = pl.ds(base, BLOCK)
        stream_copy(step).wait()
        for r in range(0, BLOCK, SUB):
            for seq in every:
                at = pl.ds(base + r, SUB)
                x = stream_ref[seq, at, :].astype(F32)
                mean = jnp.mean(x, axis=-1, keepdims=True)
                centre = x - mean
                spread = jnp.mean(centre * centre, axis=-1, keepdims=True)
                squares += fold(mean * mean + spread)
                normed_ref[seq, at, :] = (
                    centre * lax.rsqrt(spread + 1e-05) * gain + bias
                ).astype(BF16)
        left = jnp.concatenate([normed_ref[seq, rows, :] for seq in every], axis=0)
        drive = dot_nn(left, win_ref[...])
        for k in range(BLOCK // CHUNK):
            for seq in every:
                first = seq * BLOCK + k * CHUNK
                part = drive[first : first + CHUNK]
                zr, zi = cmul(
                    part[:, :states], part[:, states:], q_ref[:, :states], q_ref[:, states:]
                )
                slot = stack.at[seq]
                split_store(slot, k, zr, zi)
                s = dot_nn(tri[...], slot[k])
                sums_ref[seq, pl.ds(base + k * CHUNK, CHUNK), :] = s
                er, ei = cmul(s[CHUNK - 1 :, :states], s[CHUNK - 1 :, states:], last_r, last_i)
                nr, ni = cmul(*ends[seq], step_r, step_i)
                ends[seq] = nr + er, ni + ei
        return squares, tuple(ends)

    zero = jnp.zeros((1, states), F32)
    squares, ends = lax.fori_loop(
        0, length // BLOCK, run_block, (jnp.zeros((8, 1), F32), ((zero, zero),) * seqs)
    )
    square_ref[...] = jnp.broadcast_to(squares, square_ref.shape)
    for seq in every:
        end_ref[seq, :, :states], end_ref[seq, :, states:] = ends[seq]
    for c in onward:
        c.wait()


HBM_SPEC = pl.BlockSpec(memory_space=pltpu.HBM)
VMEM_SPEC = pl.BlockSpec(memory_space=pltpu.VMEM)
SMEM_SPEC = pl.BlockSpec(memory_space=pltpu.SMEM)


def kept(*arrays):
    return [pltpu.with_memory_space_constraint(a, pltpu.VMEM) for a in arrays]


def large(a):
    return a.size * a.dtype.itemsize > 2 * MIB


def specs_of(arrays):
    return [HBM_SPEC if large(a) else VMEM_SPEC for a in arrays]


def placed(arrays):
    return [in_hbm(a)[0] if large(a) else kept(a)[0] for a in arrays]


def in_hbm(*arrays):
    return [pltpu.with_memory_space_constraint(a, pltpu.HBM) for a in arrays]


def norm_pass(place, stream, cot, into, onward, vectors):
    seqs, length, width = stream.shape
    half, states = into[0].shape
    states2 = 2 * states
    return pl.pallas_call(
        lambda *refs: norm_kernel(length, *refs),
        in_specs=[SMEM_SPEC] + [HBM_SPEC] * 7 + [VMEM_SPEC] * 4,
        out_specs=[VMEM_SPEC] * 14,
        out_shape=[
            pltpu.VMEM((seqs, length, width), BF16),
            pltpu.VMEM((seqs, length, states2), F32),
            pltpu.VMEM((seqs, 1, states2), F32),
            pltpu.VMEM((CHUNK, states2), F32),
            pltpu.VMEM((CHUNK, states2), F32),
            pltpu.VMEM((TABLE_ROWS, states2), F32),
            pltpu.VMEM((width, states2), BF16),
            pltpu.VMEM((width, states2), BF16),
            pltpu.VMEM((8, 128), F32),
            pltpu.VMEM(stream.shape, BF16),
            pltpu.VMEM(cot.shape, BF16),
        ]
        + [pltpu.VMEM(a.shape, BF16) for a in onward],
        scratch_shapes=[
            pltpu.VMEM((seqs, BLOCK // CHUNK, 2 * CHUNK, states2), BF16),
            pltpu.VMEM((CHUNK, 2 * CHUNK), BF16),
            pltpu.VMEM((half, states), BF16),
            pltpu.VMEM((half, states), BF16),
            pltpu.SemaphoreType.DMA((length // BLOCK + 6,)),
        ],
        compiler_params=pltpu.CompilerParams(vmem_limit_bytes=8 * MIB),
        cost_estimate=cost(9),
        name="norm_pass",
    )(
        place,
        *in_hbm(stream, cot, into[0], into[2], *onward),
        *kept(*vectors, into[1], into[3]),
    )


def entering(carry, came, seq, small_ref, states):
    whole_r, whole_i = pair(small_ref, ROW_WHOLE, states)
    total_r = came[0][seq, :, :states]
    total_i = came[0][seq, :, states:]
    power_r, power_i = whole_r, whole_i
    for ref in came[1:]:
        gr, gi = cmul(ref[seq, :, :states], ref[seq, :, states:], power_r, power_i)
        total_r, total_i = total_r + gr, total_i + gi
        power_r, power_i = cmul(power_r, power_i, whole_r, whole_i)
    carry[0:1, :states] = total_r
    carry[0:1, states:] = total_i


def block_kernel(
    hops, place_ref, _, normed_ref, stream_ref, cot_ref, p_ref, small_ref, glu_own, glu_other,
    outr_own, outr_other, outi_own, outi_other, *rest,
):
    came = rest[:hops]
    (
        mixed_hbm, back_ref, state_ref, dlru_ref, start_ref, keep_ref, send_ref, acc_ref, gacc_ref,
        carry, stack, tri, act, dproj, slope, mixed, wglu, wout, dglu, dout, sems,
    ) = rest[hops:]
    states = p_ref.shape[1] // 2
    seqs, _, width = stream_ref.shape
    me = place_ref[0]
    join_halves(me, wglu, glu_own, glu_other)
    join_halves(me, wout.at[pl.ds(0, states)], outr_own, outr_other)
    join_halves(me, wout.at[pl.ds(states, states)], outi_own, outi_other)
    fill_triangle(tri, True)
    acc_ref[...] = jnp.zeros_like(acc_ref)
    gacc_ref[...] = jnp.zeros_like(gacc_ref)
    dglu[...] = jnp.zeros_like(dglu)
    dout[...] = jnp.zeros_like(dout)
    for seq in range(seqs):
        entering(carry.at[seq], came, seq, small_ref, states)
        carry[seq, 1:2, :] = jnp.zeros_like(carry[seq, 1:2, :])
        carry[seq, 2:3, :states] = jnp.ones_like(carry[seq, 2:3, :states])
        carry[seq, 2:3, states:] = jnp.zeros_like(carry[seq, 2:3, states:])

    step_r, step_i = pair(small_ref, ROW_STEP, states)
    last_r, last_i = pair(small_ref, ROW_LAST, states)
    enter_r, enter_i = pair(small_ref, ROW_ENTER, states)
    first_r, first_i = pair(small_ref, ROW_FIRST, states)
    skip = row_of(small_ref, ROW_SKIP)
    value_bias = row_of(small_ref, ROW_GLU)
    gate_bias = row_of(small_ref, ROW_GLU + 1)
    def mixed_copy(step):
        at = pl.ds(pl.multiple_of(step * BLOCK, BLOCK), BLOCK)
        slot = lax.rem(step, 2)
        return pltpu.make_async_copy(mixed.at[slot], mixed_hbm.at[:, at, :], sems.at[slot])

    def run_block(step, _):
        base = pl.multiple_of(step * BLOCK, BLOCK)
        slot = lax.rem(step, 2)
        rows = pl.ds(base, BLOCK)
        pieces = [
            (slice(r, r + SUB), pl.ds(base + r, SUB)) for r in range(0, BLOCK, SUB)
        ]
        chunks = [
            (k, pl.ds(base + k * CHUNK, CHUNK)) for k in range(BLOCK // CHUNK)
        ]
        zeros = jnp.zeros((8, width), F32)
        tiles = lambda count: [slice(n, n + TILE) for n in range(0, count, TILE)]
        spans = tiles(width)
        made = {}
        folds = {}

        def make_states(seq):
            def part(k, at):
                cr, ci = made["carry", seq]
                qr, qi = cmul(cr, ci, enter_r, enter_i)
                sr = back_ref[seq, at, :states]
                si = back_ref[seq, at, states:]
                er, ei = cmul(sr[CHUNK - 1 :], si[CHUNK - 1 :], last_r, last_i)
                nr, ni = cmul(cr, ci, step_r, step_i)
                made["carry", seq] = nr + er, ni + ei
                hr, hi = cmul(sr + qr, si + qi, p_ref[:, :states], p_ref[:, states:])
                state_ref[seq, at, :states] = hr.astype(BF16)
                state_ref[seq, at, states:] = (-hi).astype(BF16)

            def first():
                made["carry", seq] = carry[seq, 0:1, :states], carry[seq, 0:1, states:]

            def last():
                carry[seq, 0:1, :states], carry[seq, 0:1, states:] = made["carry", seq]

            return [first] + [functools.partial(part, *c) for c in chunks] + [last]

        every = range(seqs)
        both = lambda one: jnp.concatenate([one(seq) for seq in every], axis=0)

        def products(name, left, right, columns, turned=False, order=None):
            def part(n):
                if turned:
                    v = dot_nt(both(left), right[n, :])
                else:
                    v = dot_nn(both(left), right[:, n])
                v = v.astype(BF16) if name == "dact" else v
                for seq in every:
                    made.setdefault((name, seq), []).append(v[seq * BLOCK : (seq + 1) * BLOCK])

            return [functools.partial(part, n) for n in (order or tiles(columns))]

        def taken(name, seq, r, first=0, count=None):
            parts = made[name, seq][first:count]
            return jnp.concatenate([v[r] for v in parts], axis=1)

        def gather(name, n, v):
            key = name, n.start
            folds[key] = folds[key] + v if key in folds else v

        def read_out():
            return products("lru", lambda seq: state_ref[seq, rows, :], wout, width)

        def activate(seq, n):
            def part(r, at):
                readout = made["lru", seq][n.start // TILE][r]
                lru = readout + skip[:, n] * normed_ref[seq, at, n].astype(F32)
                lru2 = lru * lru
                gather("lru", n, fold(lru2))
                gate = 0.5 + 0.5 * jnp.tanh(lru * (GELU_C + GELU_C * GELU_K * lru2))
                gelu = lru * gate
                slope[seq, r, n] = (gate + (gelu - gelu * gate) * (
                    2 * GELU_C + 6 * GELU_C * GELU_K * lru2
                )).astype(BF16)
                act[seq, r, n] = gelu.astype(BF16)

            return [functools.partial(part, *c) for c in pieces]

        def project():
            order = [slice(first + n.start, first + n.stop) for n in spans for first in (0, width)]
            return products("projected", lambda seq: act[seq], wglu, 2 * width, order=order)

        def branch_out(seq, n):
            def part(r, at):
                value = made["projected", seq][2 * (n.start // TILE)][r] + value_bias[:, n]
                gate = made["projected", seq][2 * (n.start // TILE) + 1][r] + gate_bias[:, n]
                gate = 0.5 + 0.5 * jnp.tanh(0.5 * gate)
                branch = value * gate
                mixed[slot, seq, r, n] = (stream_ref[seq, at, n].astype(F32) + branch).astype(BF16)
                gather("branch", n, fold(branch * branch))
                cot = cot_ref[seq, at, n].astype(F32)
                part = cot * branch
                dvalue = (cot * gate).astype(BF16)
                dgate = (part - part * gate).astype(BF16)
                dproj[seq, r, n] = dvalue
                dproj[seq, r, slice(width + n.start, width + n.stop)] = dgate
                gather("value", n, fold_low(dvalue))
                gather("gate", n, fold_low(dgate))

            return [functools.partial(part, *c) for c in pieces]

        def project_back():
            return products("dact", lambda seq: dproj[seq], wglu, width, True)

        def activate_back(seq, n):
            def part(r, at):
                dlru = made["dact", seq][n.start // TILE][r] * slope[seq, r, n]
                dlru_ref[seq, at, n] = dlru
                gather("dlru", n, fold_low(dlru))
                gather("skip", n, fold_low(dlru * normed_ref[seq, at, n]))

            return [functools.partial(part, *c) for c in pieces]

        def read_out_back():
            return products("pull", lambda seq: dlru_ref[seq, rows, :], wout, 2 * states, True)

        def glu_back():
            def part(n):
                dglu[:, n] += dot_tn(both(lambda seq: act[seq]), both(lambda seq: dproj[seq, :, n]))

            return [functools.partial(part, n) for n in tiles(2 * width)]

        def out_back():
            def part(n):
                dout[:, n] += dot_tn(
                    both(lambda seq: state_ref[seq, rows, :]), both(lambda seq: dlru_ref[seq, rows, n])
                )

            return [functools.partial(part, n) for n in tiles(width)]

        def turn(seq):
            def part(k, at):
                pull = taken("pull", seq, slice(k * CHUNK, (k + 1) * CHUNK))
                zr, zi = cmul(pull[:, :states], pull[:, states:], p_ref[:, :states], p_ref[:, states:])
                split_store(stack.at[seq], k, zr, zi)

            return [functools.partial(part, *c) for c in chunks]

        def sum_back(seq):
            def part(k, at):
                ar, ai = carry[seq, 1:2, :states], carry[seq, 1:2, states:]
                wr, wi = carry[seq, 2:3, :states], carry[seq, 2:3, states:]
                back = dot_nn(tri[...], stack[seq, k])
                back_ref[seq, at, :] = back
                fr, fi = cmul(back[0:1, :states], back[0:1, states:], first_r, first_i)
                gr, gi = cmul(fr, fi, wr, wi)
                ar, ai = ar + gr, ai + gi
                wr, wi = cmul(wr, wi, step_r, step_i)
                carry[seq, 1:2, :states] = ar
                carry[seq, 1:2, states:] = ai
                carry[seq, 2:3, :states] = wr
                carry[seq, 2:3, states:] = wi
                start_ref[seq, :, :states] = ar
                start_ref[seq, :, states:] = ai

            return [functools.partial(part, *c) for c in chunks]

        def run(*lists):
            parts = [(i / len(one), part) for one in lists for i, part in enumerate(one)]
            for _, part in sorted(parts, key=lambda item: item[0]):
                part()

        run(*[make_states(seq) for seq in every])
        readout = read_out()
        for n, part in zip(spans, readout):
            run([part])
            run(*[activate(seq, n) for seq in every])
        projected = project()

        @pl.when(step >= 2)
        def _():
            mixed_copy(step - 2).wait()

        for k, n in enumerate(spans):
            run(projected[2 * k : 2 * k + 2])
            run(*[branch_out(seq, n) for seq in every])
        mixed_copy(step).start()
        for n, part in zip(spans, project_back()):
            run([part])
            run(*[activate_back(seq, n) for seq in every])
        run(glu_back())
        run(read_out_back())
        run(*[turn(seq) for seq in every], out_back())
        run(*[sum_back(seq) for seq in every])
        for row, name in enumerate(("lru", "branch", "dlru", "skip")):
            for n in spans:
                acc_ref[8 * row : 8 * row + 8, n] += folds[name, n.start]
        for row, name in enumerate(("value", "gate")):
            for n in spans:
                gacc_ref[8 * row : 8 * row + 8, n] += folds[name, n.start]

        return 0

    steps = stream_ref.shape[1] // BLOCK
    lax.fori_loop(0, steps, run_block, 0)
    for step in range(max(steps - 2, 0), steps):
        mixed_copy(jnp.int32(step)).wait()
    batch, height, _ = keep_ref.shape
    high = width // (2 * batch)
    part = height - high
    for ref, f in ((keep_ref, place_ref[0]), (send_ref, 1 - place_ref[0])):
        for b in range(batch):
            first = pl.multiple_of((f * batch + b) * high, high)
            ref[b, :high, :] = dglu[pl.ds(first, high), :].astype(BF16)
            first = pl.multiple_of((f * batch + b) * part, part)
            ref[b, high:, :width] = dout[pl.ds(first, part), :].astype(BF16)
            ref[b, high:, width:] = dout[pl.ds(states + first, part), :].astype(BF16)


def block_pass(place, batch, sums, normed, stream, cot, p, small, halves, came):
    seqs, length, width = stream.shape
    states2 = p.shape[1]
    height = width // (2 * batch) + states2 // (4 * batch)
    return pl.pallas_call(
        lambda *refs: block_kernel(len(came), *refs),
        in_specs=[SMEM_SPEC] + [VMEM_SPEC] * (12 + len(came)),
        out_specs=[HBM_SPEC] + [VMEM_SPEC] * 8,
        out_shape=[
            pltpu.HBM((seqs, length, width), BF16),
            pltpu.VMEM((seqs, length, states2), F32),
            pltpu.VMEM((seqs, length, states2), BF16),
            pltpu.VMEM((seqs, length, width), BF16),
            jax.ShapeDtypeStruct((seqs, 1, states2), F32),
            pltpu.VMEM((batch, height, 2 * width), BF16),
            pltpu.VMEM((batch, height, 2 * width), BF16),
            pltpu.VMEM((32, width), F32),
            pltpu.VMEM((16, width), F32),
        ],
        scratch_shapes=[
            pltpu.VMEM((seqs, 8, states2), F32),
            pltpu.VMEM((seqs, BLOCK // CHUNK, 2 * CHUNK, states2), BF16),
            pltpu.VMEM((CHUNK, 2 * CHUNK), BF16),
            pltpu.VMEM((seqs, BLOCK, width), BF16),
            pltpu.VMEM((seqs, BLOCK, 2 * width), BF16),
            pltpu.VMEM((seqs, BLOCK, width), BF16),
            pltpu.VMEM((2, seqs, BLOCK, width), BF16),
            pltpu.VMEM((width, 2 * width), BF16),
            pltpu.VMEM((states2, width), BF16),
            pltpu.VMEM((width, 2 * width), F32),
            pltpu.VMEM((states2, width), F32),
            pltpu.SemaphoreType.DMA((2,)),
        ],
        input_output_aliases={1: 1},
        compiler_params=pltpu.CompilerParams(vmem_limit_bytes=20 * MIB),
        cost_estimate=cost(28),
        name="block_pass",
    )(place, *kept(sums, normed, stream, cot, p, small, *halves, *came))


def adjoint_kernel(
    hops, others, place_ref, back_ref, _, normed_ref, win_ref, q_ref, small_ref, square_ref, acc_ref, gacc_ref,
    *rest,
):
    came = rest[:hops]
    ddrive_ref, keep_ref, send_ref, carry, din = rest[hops + others :]
    states = q_ref.shape[1] // 2
    seqs, length, _ = normed_ref.shape
    every = range(seqs)
    first_r, first_i = pair(small_ref, ROW_FIRST, states)
    back_r, back_i = pair(small_ref, ROW_BACK, states)
    carries = []
    for seq in every:
        entering(carry, came, seq, small_ref, states)
        carries.append((carry[0:1, :states], carry[0:1, states:]))
    real_sum = imag_sum = real_total = imag_total = jnp.zeros((8, states), F32)
    for base in reversed(range(0, length, BLOCK)):
        for k in reversed(range(BLOCK // CHUNK)):
            for seq in every:
                at = pl.ds(base + k * CHUNK, CHUNK)
                qr, qi = cmul(*carries[seq], back_r, back_i)
                vr = back_ref[seq, at, :states] + qr
                vi = back_ref[seq, at, states:] + qi
                carries[seq] = cmul(vr[0:1], vi[0:1], first_r, first_i)
                ar, ai = cmul(vr, vi, q_ref[:, :states], q_ref[:, states:])
                hr = ddrive_ref[seq, at, :states]
                hi = ddrive_ref[seq, at, states:]
                lr, li = ar.astype(BF16), ai.astype(BF16)
                real_sum += fold((lr * hr).astype(F32) + (li * hi).astype(F32))
                imag_sum += fold((lr * hi).astype(F32) - (li * hr).astype(F32))
                real_total += fold_low(lr)
                imag_total += fold_low(li)
                ddrive_ref[seq, at, :states] = lr
                ddrive_ref[seq, at, states:] = li
        rows = pl.ds(base, BLOCK)
        product = dot_tn(
            jnp.concatenate([normed_ref[seq, rows, :] for seq in every], axis=0),
            jnp.concatenate([ddrive_ref[seq, rows, :] for seq in every], axis=0),
        )
        if base == length - BLOCK:
            din[...] = product
        else:
            din[...] += product
    width = din.shape[0]
    gain = row_of(small_ref, ROW_GAIN)
    bias = row_of(small_ref, ROW_BIAS)
    skip = row_of(small_ref, ROW_SKIP)
    weight = win_ref[...].astype(F32)
    grad = din[...]
    in_r, in_i = weight[:, :states], weight[:, states:]
    g_r, g_i = grad[:, :states], grad[:, states:]
    x_r = jnp.sum(g_r * in_r + g_i * in_i, axis=0, keepdims=True)
    x_i = jnp.sum(g_r * in_i - g_i * in_r, axis=0, keepdims=True)
    inverse = small_ref[ROW_SCALE : ROW_SCALE + 1, states:]
    column = lambda v: jnp.sum(v, axis=0, keepdims=True)
    d_r = column(real_sum) * inverse - x_r
    d_i = column(imag_sum) * inverse - x_i
    decay, rotation = pair(small_ref, ROW_RATE, states)
    gathered = dot_nt_wide(jnp.ones((8, 2 * states), F32), weight * grad)[0:1]
    total = jnp.broadcast_to(jnp.concatenate([column(real_total), column(imag_total)], axis=1), (8, 2 * states))
    d_lru = column(acc_ref[16:24, :])
    d_skip = column(acc_ref[24:32, :])
    d_bias = dot_nt_wide(total, weight)[0:1] + skip * d_lru
    d_gain = (gathered + skip * d_skip - bias * d_bias) / gain
    d_nu = -decay * d_r
    d_theta = rotation * d_i
    d_values = column(gacc_ref[0:8, :])
    d_gates = column(gacc_ref[8:16, :])
    lane = lax.broadcasted_iota(jnp.int32, (1, width // 2), 1)
    squares = jnp.zeros((1, width // 2), F32)
    sums = (
        width * jnp.sum(square_ref[:, 0:1]), jnp.sum(acc_ref[0:8, :]), jnp.sum(acc_ref[8:16, :]),
    )
    for place, v in enumerate(sums):
        squares = jnp.where(lane == place, v, squares)
    half, some = width // 2, states // 2
    batch, height, _ = keep_ref.shape
    high = width // (2 * batch)
    me = place_ref[0]

    def chosen(f, low, up):
        return jnp.where(f == 0, low, up)

    for ref, f in ((keep_ref, me), (send_ref, 1 - me)):
        wide = lambda v: chosen(f, v[:, :half], v[:, half:])
        thin = lambda v: chosen(f, v[:, :some], v[:, some:])
        d_glu = chosen(f, d_values, d_gates)
        lines = (
            wide(d_gain),
            wide(d_bias),
            jnp.concatenate([thin(d_nu), thin(d_theta)], axis=1),
            jnp.concatenate([thin(x_r), jnp.zeros((1, some), F32)], axis=1),
            wide(d_skip),
            d_glu[:, :half],
            d_glu[:, half:],
            squares,
        )
        for b in range(batch):
            first = pl.multiple_of((f * batch + b) * high, high)
            ref[b, :high, :states] = din[pl.ds(first, high), :states].astype(BF16)
            ref[b, :high, states:] = (-din[pl.ds(first, high), states:]).astype(BF16)
            line = jnp.concatenate(lines[b * 8 // batch : (b + 1) * 8 // batch], axis=1)
            line = jnp.broadcast_to(line, (height - high, width)).astype(BF16)
            ref[b, high:, :] = line


def adjoint_pass(
    place, batch, back, state, normed, wback, q, small, square, acc, gacc, came, after
):
    seqs, length, width = normed.shape
    states2 = q.shape[1]
    return pl.pallas_call(
        lambda *refs: adjoint_kernel(len(came), len(after), *refs),
        in_specs=[SMEM_SPEC] + [VMEM_SPEC] * (9 + len(came)) + specs_of(after),
        out_specs=[VMEM_SPEC] * 3,
        out_shape=[
            pltpu.VMEM((seqs, length, states2), BF16),
            pltpu.VMEM((batch, width // (2 * batch) + 16, states2), BF16),
            pltpu.VMEM((batch, width // (2 * batch) + 16, states2), BF16),
        ],
        scratch_shapes=[
            pltpu.VMEM((8, states2), F32),
            pltpu.VMEM((width, states2), F32),
        ],
        input_output_aliases={2: 0},
        compiler_params=pltpu.CompilerParams(vmem_limit_bytes=8 * MIB),
        cost_estimate=cost(7),
        name="adjoint_pass",
    )(place, *kept(back, state, normed, wback, q, small, square, acc, gacc, *came), *placed(after))


def input_kernel(seq, skipped, ddrive_ref, dlru_ref, stream_ref, cot_ref, small_ref, win_ref, *rest):
    out_ref = rest[-1]
    base = (pl.program_id(0) + skipped) * BLOCK
    gain = row_of(small_ref, ROW_GAIN)
    skip = row_of(small_ref, ROW_SKIP)
    rows = pl.ds(pl.multiple_of(base, BLOCK), BLOCK)
    pulled = dot_nt(ddrive_ref[seq, rows, :], win_ref[...])
    for r in range(0, BLOCK, SUB):
        at = pl.ds(pl.multiple_of(base + r, SUB), SUB)
        d = pulled[r : r + SUB] + skip * dlru_ref[seq, at, :].astype(F32)
        x = stream_ref[seq, at, :].astype(F32)
        centre = x - jnp.mean(x, axis=-1, keepdims=True)
        spread = jnp.mean(centre * centre, axis=-1, keepdims=True)
        inverse = lax.rsqrt(spread + 1e-05)
        hat = centre * inverse
        dhat = d * gain
        m1 = jnp.mean(dhat, axis=-1, keepdims=True)
        m2 = jnp.mean(dhat * hat, axis=-1, keepdims=True)
        out_ref[r : r + SUB, :] = (dhat - m1 - hat * m2) * inverse + cot_ref[seq, at, :].astype(F32)


def input_pass(part, ddrive, dlru, stream, cot, small, win, earlier, after):
    seq, skipped, blocks = part
    seqs, length, width = stream.shape
    earlier = in_hbm(*earlier)
    return pl.pallas_call(
        lambda *refs: input_kernel(seq, skipped, *refs),
        grid=(blocks,),
        in_specs=[VMEM_SPEC] * 6 + [HBM_SPEC] * len(earlier) + specs_of(after),
        out_specs=pl.BlockSpec((None, BLOCK, width), lambda i: (seq, i + skipped, 0)),
        out_shape=pltpu.HBM((seqs, length, width), F32),
        input_output_aliases={6: 0} if earlier else {},
        compiler_params=pltpu.CompilerParams(vmem_limit_bytes=8 * MIB),
        cost_estimate=cost(1.1 * blocks),
        name="input_pass",
    )(*kept(ddrive, dlru, stream, cot, small, win), *earlier, *placed(after))


def pack_kernel(count, *refs):
    out_ref = refs[count]
    parts = refs[count + 1 : -1]
    copies = [
        pltpu.make_async_copy(source, target, refs[-1].at[k])
        for k, (source, target) in enumerate(zip(refs[:count], parts))
    ]
    for c in copies:
        c.start()
    for c in copies:
        c.wait()
    row = 0
    for ref in parts:
        for first in range(0, ref.shape[0], 128):
            out_ref[row : row + 1, :] = ref[first : first + 128].reshape(1, 128)
            row += 1


def pack_vectors(*vectors):
    rows = sum(v.shape[0] for v in vectors) // 128
    return pl.pallas_call(
        lambda *refs: pack_kernel(len(vectors), *refs),
        in_specs=[HBM_SPEC] * len(vectors),
        out_specs=VMEM_SPEC,
        out_shape=pltpu.VMEM((rows, 128), BF16),
        scratch_shapes=[pltpu.VMEM(v.shape, BF16) for v in vectors]
        + [pltpu.SemaphoreType.DMA((len(vectors),))],
        compiler_params=pltpu.CompilerParams(vmem_limit_bytes=2 * MIB),
        name="pack_vectors",
    )(*in_hbm(*vectors))


def pair_kernel(others, place_ref, keep_ref, came_ref, *rest):
    for hop, ref in enumerate(rest[others:]):
        at = place_ref[1] ^ hop
        ref[...] = (keep_ref[at].astype(F32) + came_ref[at].astype(F32)).astype(BF16)


def pair_sum(place, keep, came, after=()):
    count = keep.shape[0]
    return pl.pallas_call(
        lambda *refs: pair_kernel(len(after), *refs),
        in_specs=[SMEM_SPEC] + [VMEM_SPEC] * 2 + specs_of(after),
        out_specs=[VMEM_SPEC] * count,
        out_shape=[pltpu.VMEM(keep.shape[1:], BF16)] * count,
        compiler_params=pltpu.CompilerParams(vmem_limit_bytes=4 * MIB),
        cost_estimate=cost(0.7),
        name="pair_sum",
    )(place, *kept(keep, came), *placed(after))


def add_kernel(count, *refs):
    total = refs[0][...].astype(F32)
    for ref in refs[1:count]:
        total += ref[...].astype(F32)
    refs[-1][...] = total.astype(BF16)


def add_up(got, after=()):
    return pl.pallas_call(
        lambda *refs: add_kernel(len(got), *refs),
        in_specs=[VMEM_SPEC] * len(got) + specs_of(after),
        out_specs=VMEM_SPEC,
        out_shape=pltpu.VMEM(got[0].shape, BF16),
        compiler_params=pltpu.CompilerParams(vmem_limit_bytes=4 * MIB),
        cost_estimate=cost(0.2),
        name="add_up",
    )(*kept(*got), *placed(after))


def split_kernel(count, others, place_ref, *refs):
    total = refs[0]
    pieces = refs[count + others :]
    wide = total.shape[1] // len(pieces)
    for hop, ref in enumerate(pieces):
        at = lax.rem(place_ref[2] + hop, len(pieces))
        columns = pl.ds(pl.multiple_of(at * wide, wide), wide)
        v = refs[0][:, columns].astype(F32)
        for other in refs[1:count]:
            v += other[:, columns].astype(F32)
        ref[...] = v.astype(BF16)


def add_split(place, got, ring, after=()):
    rows, columns = got[0].shape
    return pl.pallas_call(
        lambda *refs: split_kernel(len(got), len(after), *refs),
        in_specs=[SMEM_SPEC] + [VMEM_SPEC] * len(got) + specs_of(after),
        out_specs=[VMEM_SPEC] * ring,
        out_shape=[pltpu.VMEM((rows, columns // ring), BF16)] * ring,
        compiler_params=pltpu.CompilerParams(vmem_limit_bytes=4 * MIB),
        cost_estimate=cost(0.3),
        name="add_split",
    )(place, *kept(*got), *placed(after))


def finish_kernel(count, place_ref, *refs):
    first, second, out_ref = refs[:count], refs[count : 2 * count], refs[-1]
    rows, wide = first[0].shape
    span = out_ref.shape[1]
    for hop in range(count):
        at = lax.rem(place_ref[2] + count - hop, count)
        if wide < span:
            per = span // wide
            row = pl.multiple_of(lax.div(at, per) * rows, rows)
            column = pl.multiple_of(lax.rem(at, per) * wide, wide)
            out_ref[pl.ds(row, rows), pl.ds(column, wide)] = first[hop][...]
        else:
            for k in range(wide // span):
                row = pl.multiple_of((at * (wide // span) + k) * rows, rows)
                out_ref[pl.ds(row, rows), :] = first[hop][:, k * span : (k + 1) * span]
    total = second[0][...].astype(F32)
    for ref in second[1:]:
        total += ref[...].astype(F32)
    out_ref[out_ref.shape[0] - total.shape[0] :, :] = total.astype(BF16)


def finish_seq(place, first, second, after):
    rows, wide = first[0].shape
    low, span = second[0].shape
    height = rows * wide * len(first) // span + low
    return pl.pallas_call(
        lambda *refs: finish_kernel(len(first), *refs),
        in_specs=[SMEM_SPEC] + [VMEM_SPEC] * (2 * len(first)) + specs_of(after),
        out_specs=VMEM_SPEC,
        out_shape=pltpu.VMEM((height, span), BF16),
        compiler_params=pltpu.CompilerParams(vmem_limit_bytes=4 * MIB),
        cost_estimate=cost(0.5),
        name="finish_seq",
    )(place, *kept(*first, *second), *placed(after))


def unpack_kernel(count, others, tokens, place_ref, *refs):
    got = refs[:count]
    (
        glu_ref, outr_ref, outi_ref, inr_ref, ini_ref, gain_ref, bias_ref, nu_ref, theta_ref,
        gamma_ref, skip_ref, glub_ref, rms_ref, lines,
    ) = refs[count + others :]
    width = glu_ref.shape[1] // 2
    states = inr_ref.shape[1]
    high = glu_ref.shape[0] // count
    part = outr_ref.shape[0] // count
    low = 2 * (high + part)
    for hop in range(count):
        at = place_ref[1] ^ hop
        v = got[hop]
        rows = pl.ds(pl.multiple_of(at * high, high), high)
        few = pl.ds(pl.multiple_of(at * part, part), part)
        glu_ref[rows, :width] = v[:high, :].astype(F32)
        outr_ref[few, :] = v[high : high + part, :].astype(F32)
        glu_ref[rows, width:] = v[high + part : 2 * high + part, :].astype(F32)
        outi_ref[few, :] = v[2 * high + part : low, :].astype(F32)
        inr_ref[rows, :] = v[low : low + high, :states].astype(F32)
        ini_ref[rows, :] = v[low : low + high, states:].astype(F32)
        lines[pl.ds(pl.multiple_of(at * 8, 8), 8), :] = v[low + high :, :].astype(F32)[:8]
    half, some = width // 2, states // 2
    per = 8 // count
    line = lambda k: lines[k // per * 8 : k // per * 8 + 1, k % per * half : (k % per + 1) * half]
    gain_ref[...] = line(0)
    bias_ref[...] = line(1)
    nu_ref[...] = line(2)[:, :some]
    theta_ref[...] = line(2)[:, some:]
    gamma_ref[...] = line(3)[:, :some]
    skip_ref[...] = line(4)
    glub_ref[:, :half] = line(5)
    glub_ref[:, half:] = line(6)
    rms_ref[...] = jnp.sqrt(line(7)[:, :3] / tokens)


def unpack(place, got, width, states, tokens, after):
    count = len(got)
    flat = [width // 2, width // 2, states // 2, states // 2, states // 2, width // 2, width, 3]
    return pl.pallas_call(
        lambda *refs: unpack_kernel(count, len(after), tokens, *refs),
        in_specs=[SMEM_SPEC] + [VMEM_SPEC] * count + specs_of(after),
        out_specs=[VMEM_SPEC] * 13,
        out_shape=[
            jax.ShapeDtypeStruct((width // 2, 2 * width), F32),
            jax.ShapeDtypeStruct((states // 2, width), F32),
            jax.ShapeDtypeStruct((states // 2, width), F32),
            jax.ShapeDtypeStruct((width // 2, states), F32),
            jax.ShapeDtypeStruct((width // 2, states), F32),
        ]
        + [jax.ShapeDtypeStruct((1, n), F32) for n in flat],
        scratch_shapes=[pltpu.VMEM((8 * count, width), F32)],
        compiler_params=pltpu.CompilerParams(vmem_limit_bytes=8 * MIB),
        name="unpack",
    )(place, *got, *placed(after))


def hops_of(ends, axis, reverse):
    count = lax.axis_size(axis)
    if count <= 4:
        return [
            lax.ppermute(
                ends,
                axis,
                [(i + hop, i) if reverse else (i, i + hop) for i in range(count - hop)],
            )
            for hop in range(1, count)
        ]
    place = lax.axis_index(axis)
    every = lax.all_gather(ends, axis)
    came = []
    for hop in range(1, count):
        source = place + hop if reverse else place - hop
        inside = (source >= 0) & (source < count)
        item = lax.dynamic_index_in_dim(every, jnp.clip(source, 0, count - 1), 0, False)
        came.append(jnp.where(inside, item, 0.0))
    return came


def swap(a):
    return lax.ppermute(a, "fsdp", [(0, 1), (1, 0)])


def swap_moves(axis, bit):
    return [(i, i ^ bit) for i in range(lax.axis_size(axis))]


def scatter_batch(pieces):
    return [pieces[0]] + [
        lax.ppermute(pieces[hop], "batch", swap_moves("batch", hop))
        for hop in range(1, len(pieces))
    ]


def around(pieces):
    ring = lax.axis_size("seq")
    return [pieces[0]] + [
        lax.ppermute(pieces[hop], "seq", [(i, (i + hop) % ring) for i in range(ring)])
        for hop in range(1, ring)
    ]


def share_seq(piece):
    ring = lax.axis_size("seq")
    if ring > 4:
        return [lax.psum(piece.astype(F32), "seq").astype(BF16)]
    return around([piece] * ring)


def gather_batch(piece):
    count = lax.axis_size("batch")
    return [piece] + [
        lax.ppermute(piece, "batch", swap_moves("batch", hop)) for hop in range(1, count)
    ]


def on_device(
    stream, norm_gain, norm_bias, in_real, in_imag, nu_log, theta_log, gamma_log, out_real,
    out_imag, skip_scale, glu_weight, glu_bias, cotangent,
):
    seqs, length, width = stream.shape
    states = 2 * nu_log.shape[0]
    batch = lax.axis_size("batch")
    place = jnp.stack(
        [lax.axis_index("fsdp"), lax.axis_index("batch"), lax.axis_index("seq")]
    ).astype(jnp.int32)
    place, in_real, in_imag, glu_weight, out_real, out_imag = lax.optimization_barrier(
        (place, in_real, in_imag, glu_weight, out_real, out_imag)
    )
    vectors = pack_vectors(
        norm_gain, norm_bias, skip_scale, glu_bias, nu_log, theta_log, gamma_log
    )
    into = [in_real, swap(in_real), in_imag, swap(in_imag)]
    others = [swap(glu_weight), swap(out_real), swap(out_imag)]
    (
        normed, sums, ends, p, q, small, win, wback, square, stream_kept, cot_kept, *own,
    ) = norm_pass(
        place, stream, cotangent, into, [glu_weight, out_real, out_imag], [vectors, swap(vectors)]
    )
    halves = [a for pair_of in zip(own, others) for a in pair_of]
    came = hops_of(ends, "seq", False)
    mixed, back, state, dlru, starts, keep, send, acc, gacc = block_pass(
        place, batch, sums, normed, stream_kept, cot_kept, p, small, halves, came
    )
    later = hops_of(starts, "seq", True)
    pieces = pair_sum(place, keep, swap(send), later)
    first = scatter_batch(pieces)
    ddrive, keep, send = adjoint_pass(
        place, batch, back, state, normed, wback, q, small, square, acc, gacc, later, pieces
    )
    ring = lax.axis_size("seq")
    short = ring <= 4
    first = add_split(place, first, ring if short else 1, [send])
    send, *first = lax.optimization_barrier((send, *first))
    pieces = pair_sum(place, keep, swap(send))
    second = scatter_batch(pieces)
    first = around(first) if short else share_seq(first[0])
    last = lambda part, earlier, after: input_pass(
        part, ddrive, dlru, stream_kept, cot_kept, small, wback, earlier, after
    )
    blocks = length // BLOCK
    grads = (last((0, 0, blocks // 2), (), [first[0], pieces[0]]),)
    first = add_up(first, grads)
    if short:
        first = around([first] * ring)
    second = share_seq(add_up(second, [first[0], *grads]))
    for seq in range(1, seqs):
        grads = (last((seq, 0, blocks), grads, [first[0], second[0]]),)
    got = gather_batch(finish_seq(place, first if short else [first], second, grads))
    grads = (last((0, blocks // 2, blocks - blocks // 2), grads, got[:1]),)
    grad_stream = grads[0]
    tokens = stream.size * batch * lax.axis_size("seq") * lax.axis_size("fsdp")
    (
        glu, out_r, out_i, in_r, in_i, gain, bias, nu, theta, gamma, skip, glub, rms,
    ) = unpack(place, got, width, states, float(tokens), grads)
    flat = lambda a: a.reshape(-1)
    return (
        mixed, grad_stream, flat(gain), flat(bias), in_r, in_i, flat(nu), flat(theta), flat(gamma),
        out_r, out_i, flat(skip), glu, flat(glub), flat(rms),
    )


def solution(mesh):
    tokens = P(("batch", "fsdp"), "seq", None)
    vector = P("fsdp")
    matrix = P("fsdp", None)
    weights = (
        vector, vector, matrix, matrix, vector, vector, vector, matrix, matrix, vector, matrix,
        vector,
    )
    return jax.shard_map(
        on_device,
        mesh=mesh,
        in_specs=(tokens,) + weights + (tokens,),
        out_specs=(tokens, tokens) + weights + (P(),),
        check_vma=False,
    )
```

```python
import functools

import jax
import jax.numpy as jnp
from jax import lax
from jax.experimental import pallas as pl
from jax.experimental.pallas import tpu as pltpu
from jax.sharding import PartitionSpec as P

F32 = jnp.float32
BF16 = jnp.bfloat16
HIGHEST = lax.Precision.HIGHEST
CHUNK = 128
HALF = 64
BLOCK = 512
SUB = 64
TILE = 256
GELU_C = 0.7978845608028654
GELU_K = 0.044715
MIB = 1024 * 1024


def dot_nn(a, b):
    return jnp.dot(a, b, preferred_element_type=F32)


def dot_tn(a, b):
    return lax.dot_general(a, b, (((0,), (0,)), ((), ())), preferred_element_type=F32)


def dot_nt(a, b):
    return lax.dot_general(a, b, (((1,), (1,)), ((), ())), preferred_element_type=F32)


def dot_nt_wide(a, b):
    return lax.dot_general(
        a, b, (((1,), (1,)), ((), ())), precision=HIGHEST, preferred_element_type=F32
    )


def cmul(ar, ai, br, bi):
    return ar * br - ai * bi, ar * bi + ai * br


def fold(v):
    return jnp.sum(v.reshape(v.shape[0] // 8, 8, v.shape[1]), axis=0)


def fold_low(v):
    rows = v.shape[0] // 4
    v = (v[:rows] + v[rows : 2 * rows]) + (v[2 * rows : 3 * rows] + v[3 * rows :])
    return fold(v.astype(F32))


def split_store(stack, k, zr, zi):
    states = zr.shape[1]
    for part, v in enumerate((zr, zi)):
        columns = pl.ds(part * states, states)
        high = v.astype(BF16)
        stack[k, :CHUNK, columns] = high
        stack[k, CHUNK:, columns] = (v - high.astype(F32)).astype(BF16)


def fill_triangle(tri, upper):
    row = lax.broadcasted_iota(jnp.int32, (CHUNK, CHUNK), 0)
    column = lax.broadcasted_iota(jnp.int32, (CHUNK, CHUNK), 1)
    inside = (column >= row) if upper else (column <= row)
    ones = jnp.where(inside, 1.0, 0.0).astype(BF16)
    tri[:, :CHUNK] = ones
    tri[:, CHUNK:] = ones


ROW_STEP = 0
ROW_LAST = 1
ROW_ENTER = 2
ROW_FIRST = 3
ROW_BACK = 4
ROW_WHOLE = 5
ROW_SCALE = 6
ROW_RATE = 7
ROW_GAIN = 8
ROW_BIAS = 9
ROW_SKIP = 10
ROW_GLU = 11
TABLE_ROWS = 16


def pair(ref, row, states):
    return ref[row : row + 1, :states], ref[row : row + 1, states:]


def row_of(ref, row):
    return ref[row : row + 1, :]


def fill_tables(me, own_ref, other_ref, p_ref, q_ref, small_ref, length):
    states = q_ref.shape[1] // 2
    width = q_ref.shape[1]
    own = own_ref[...].astype(F32)
    other = other_ref[...].astype(F32)
    low = jnp.where(me == 0, own, other)
    high = jnp.where(me == 0, other, own)

    def both(first, count):
        rows = [h[first + i : first + i + 1] for h in (low, high) for i in range(count)]
        return jnp.concatenate(rows, axis=1)

    small_ref[...] = jnp.zeros_like(small_ref)
    for row, first in ((ROW_GAIN, 0), (ROW_BIAS, 2), (ROW_SKIP, 4)):
        small_ref[row : row + 1, :] = both(first, 2)
    glu = both(6, 4)
    small_ref[ROW_GLU : ROW_GLU + 1, :] = glu[:, :width]
    small_ref[ROW_GLU + 1 : ROW_GLU + 2, :] = glu[:, width:]
    decay = jnp.exp(both(10, 1))
    rotation = jnp.exp(both(11, 1))
    scale = jnp.exp(both(12, 1))
    steps = (lax.broadcasted_iota(jnp.int32, (CHUNK, states), 0) - HALF).astype(F32)
    turn = steps * rotation
    cos = jnp.cos(turn)
    sin = jnp.sin(turn)
    grow = jnp.exp(-steps * decay)
    p_ref[:, :states] = grow * cos
    p_ref[:, states:] = grow * sin
    shrink = scale * jnp.exp(steps * decay)
    q_ref[:, :states] = shrink * cos
    q_ref[:, states:] = -shrink * sin
    counts = {
        ROW_STEP: CHUNK,
        ROW_LAST: CHUNK - 1 - HALF,
        ROW_ENTER: HALF + 1,
        ROW_FIRST: HALF,
        ROW_BACK: CHUNK - HALF,
        ROW_WHOLE: length,
    }
    assert sorted(counts) == list(range(6))
    index = lax.broadcasted_iota(jnp.int32, (8, states), 0)
    count = jnp.zeros((8, states), F32)
    for row, steps in counts.items():
        count = jnp.where(index == row, float(steps), count)
    size = jnp.exp(-count * decay)
    small_ref[:6, :states] = (size * jnp.cos(count * rotation))[:6]
    small_ref[:6, states:] = (size * jnp.sin(count * rotation))[:6]
    small_ref[ROW_SCALE : ROW_SCALE + 1, :states] = scale
    small_ref[ROW_SCALE : ROW_SCALE + 1, states:] = 1.0 / scale
    small_ref[ROW_RATE : ROW_RATE + 1, :states] = decay
    small_ref[ROW_RATE : ROW_RATE + 1, states:] = rotation


def join_halves(me, whole, own, other, columns=slice(None)):
    rows = own.shape[0]
    whole[pl.ds(pl.multiple_of(me * rows, rows), rows), columns] = own[...]
    whole[pl.ds(pl.multiple_of((1 - me) * rows, rows), rows), columns] = other[...]


def cost(microseconds):
    return pl.CostEstimate(
        flops=0, transcendentals=0, bytes_accessed=int(microseconds * 3.6e6)
    )


def norm_kernel(
    length, place_ref, stream_hbm, cot_hbm, inr_hbm, ini_hbm, glu_hbm, outr_hbm, outi_hbm,
    vec_own, vec_other, inr_other, ini_other,
    normed_ref, sums_ref, end_ref, p_ref, q_ref, small_ref, win_ref, wback_ref, square_ref,
    stream_ref, cot_ref, glu_ref, outr_ref, outi_ref,
    stack, tri, inr_own, ini_own, sems,
):
    states = q_ref.shape[1] // 2
    seqs = stream_ref.shape[0]
    every = range(seqs)
    copy = lambda source, target, k: pltpu.make_async_copy(source, target, sems.at[k])
    weights = [copy(inr_hbm, inr_own, 0), copy(ini_hbm, ini_own, 1)]
    onward = [
        copy(source, target, 2 + k)
        for k, (source, target) in enumerate(
            ((glu_hbm, glu_ref), (outr_hbm, outr_ref), (outi_hbm, outi_ref), (cot_hbm, cot_ref))
        )
    ]

    def stream_copy(step):
        at = (slice(None), pl.ds(pl.multiple_of(step * BLOCK, BLOCK), BLOCK))
        return copy(stream_hbm.at[at], stream_ref.at[at], 6 + step)

    blocks = [stream_copy(step) for step in range(length // BLOCK)]
    for c in blocks[:1] + weights + blocks[1:] + onward:
        c.start()
    me = place_ref[0]
    fill_tables(me, vec_own, vec_other, p_ref, q_ref, small_ref, length)
    fill_triangle(tri, False)
    for c in weights:
        c.wait()
    join_halves(me, win_ref, inr_own, inr_other, slice(0, states))
    join_halves(me, win_ref, ini_own, ini_other, slice(states, 2 * states))
    wback_ref[:, :states] = win_ref[:, :states]
    wback_ref[:, states:] = -win_ref[:, states:]

    gain = row_of(small_ref, ROW_GAIN)
    bias = row_of(small_ref, ROW_BIAS)
    step_r, step_i = pair(small_ref, ROW_STEP, states)
    last_r, last_i = pair(small_ref, ROW_LAST, states)

    def run_block(step, state):
        squares, ends = state
        ends = list(ends)
        base = pl.multiple_of(step * BLOCK, BLOCK)
        rows = pl.ds(base, BLOCK)
        stream_copy(step).wait()
        for r in range(0, BLOCK, SUB):
            for seq in every:
                at = pl.ds(base + r, SUB)
                x = stream_ref[seq, at, :].astype(F32)
                mean = jnp.mean(x, axis=-1, keepdims=True)
                centre = x - mean
                spread = jnp.mean(centre * centre, axis=-1, keepdims=True)
                squares += fold(mean * mean + spread)
                normed_ref[seq, at, :] = (
                    centre * lax.rsqrt(spread + 1e-05) * gain + bias
                ).astype(BF16)
        left = jnp.concatenate([normed_ref[seq, rows, :] for seq in every], axis=0)
        drive = dot_nn(left, win_ref[...])
        for k in range(BLOCK // CHUNK):
            for seq in every:
                first = seq * BLOCK + k * CHUNK
                part = drive[first : first + CHUNK]
                zr, zi = cmul(
                    part[:, :states], part[:, states:], q_ref[:, :states], q_ref[:, states:]
                )
                slot = stack.at[seq]
                split_store(slot, k, zr, zi)
                s = dot_nn(tri[...], slot[k])
                sums_ref[seq, pl.ds(base + k * CHUNK, CHUNK), :] = s
                er, ei = cmul(s[CHUNK - 1 :, :states], s[CHUNK - 1 :, states:], last_r, last_i)
                nr, ni = cmul(*ends[seq], step_r, step_i)
                ends[seq] = nr + er, ni + ei
        return squares, tuple(ends)

    zero = jnp.zeros((1, states), F32)
    squares, ends = lax.fori_loop(
        0, length // BLOCK, run_block, (jnp.zeros((8, 1), F32), ((zero, zero),) * seqs)
    )
    square_ref[...] = jnp.broadcast_to(squares, square_ref.shape)
    for seq in every:
        end_ref[seq, :, :states], end_ref[seq, :, states:] = ends[seq]
    for c in onward:
        c.wait()


HBM_SPEC = pl.BlockSpec(memory_space=pltpu.HBM)
VMEM_SPEC = pl.BlockSpec(memory_space=pltpu.VMEM)
SMEM_SPEC = pl.BlockSpec(memory_space=pltpu.SMEM)


def kept(*arrays):
    return [pltpu.with_memory_space_constraint(a, pltpu.VMEM) for a in arrays]


def large(a):
    return a.size * a.dtype.itemsize > 2 * MIB


def specs_of(arrays):
    return [HBM_SPEC if large(a) else VMEM_SPEC for a in arrays]


def placed(arrays):
    return [in_hbm(a)[0] if large(a) else kept(a)[0] for a in arrays]


def in_hbm(*arrays):
    return [pltpu.with_memory_space_constraint(a, pltpu.HBM) for a in arrays]


def norm_pass(place, stream, cot, into, onward, vectors):
    seqs, length, width = stream.shape
    half, states = into[0].shape
    states2 = 2 * states
    return pl.pallas_call(
        lambda *refs: norm_kernel(length, *refs),
        in_specs=[SMEM_SPEC] + [HBM_SPEC] * 7 + [VMEM_SPEC] * 4,
        out_specs=[VMEM_SPEC] * 14,
        out_shape=[
            pltpu.VMEM((seqs, length, width), BF16),
            pltpu.VMEM((seqs, length, states2), F32),
            pltpu.VMEM((seqs, 1, states2), F32),
            pltpu.VMEM((CHUNK, states2), F32),
            pltpu.VMEM((CHUNK, states2), F32),
            pltpu.VMEM((TABLE_ROWS, states2), F32),
            pltpu.VMEM((width, states2), BF16),
            pltpu.VMEM((width, states2), BF16),
            pltpu.VMEM((8, 128), F32),
            pltpu.VMEM(stream.shape, BF16),
            pltpu.VMEM(cot.shape, BF16),
        ]
        + [pltpu.VMEM(a.shape, BF16) for a in onward],
        scratch_shapes=[
            pltpu.VMEM((seqs, BLOCK // CHUNK, 2 * CHUNK, states2), BF16),
            pltpu.VMEM((CHUNK, 2 * CHUNK), BF16),
            pltpu.VMEM((half, states), BF16),
            pltpu.VMEM((half, states), BF16),
            pltpu.SemaphoreType.DMA((length // BLOCK + 6,)),
        ],
        compiler_params=pltpu.CompilerParams(vmem_limit_bytes=8 * MIB),
        cost_estimate=cost(9),
        name="norm_pass",
    )(
        place,
        *in_hbm(stream, cot, into[0], into[2], *onward),
        *kept(*vectors, into[1], into[3]),
    )


def entering(carry, came, seq, small_ref, states):
    whole_r, whole_i = pair(small_ref, ROW_WHOLE, states)
    total_r = came[0][seq, :, :states]
    total_i = came[0][seq, :, states:]
    power_r, power_i = whole_r, whole_i
    for ref in came[1:]:
        gr, gi = cmul(ref[seq, :, :states], ref[seq, :, states:], power_r, power_i)
        total_r, total_i = total_r + gr, total_i + gi
        power_r, power_i = cmul(power_r, power_i, whole_r, whole_i)
    carry[0:1, :states] = total_r
    carry[0:1, states:] = total_i


def block_kernel(
    hops, place_ref, _, normed_ref, stream_ref, cot_ref, p_ref, small_ref, glu_own, glu_other,
    outr_own, outr_other, outi_own, outi_other, *rest,
):
    came = rest[:hops]
    (
        mixed_hbm, back_ref, state_ref, dlru_ref, start_ref, keep_ref, send_ref, acc_ref, gacc_ref,
        carry, stack, tri, act, dproj, slope, mixed, wglu, wout, dglu, dout, sems,
    ) = rest[hops:]
    states = p_ref.shape[1] // 2
    seqs, _, width = stream_ref.shape
    me = place_ref[0]
    join_halves(me, wglu, glu_own, glu_other)
    join_halves(me, wout.at[pl.ds(0, states)], outr_own, outr_other)
    join_halves(me, wout.at[pl.ds(states, states)], outi_own, outi_other)
    fill_triangle(tri, True)
    acc_ref[...] = jnp.zeros_like(acc_ref)
    gacc_ref[...] = jnp.zeros_like(gacc_ref)
    dglu[...] = jnp.zeros_like(dglu)
    dout[...] = jnp.zeros_like(dout)
    for seq in range(seqs):
        entering(carry.at[seq], came, seq, small_ref, states)
        carry[seq, 1:2, :] = jnp.zeros_like(carry[seq, 1:2, :])
        carry[seq, 2:3, :states] = jnp.ones_like(carry[seq, 2:3, :states])
        carry[seq, 2:3, states:] = jnp.zeros_like(carry[seq, 2:3, states:])

    step_r, step_i = pair(small_ref, ROW_STEP, states)
    last_r, last_i = pair(small_ref, ROW_LAST, states)
    enter_r, enter_i = pair(small_ref, ROW_ENTER, states)
    first_r, first_i = pair(small_ref, ROW_FIRST, states)
    skip = row_of(small_ref, ROW_SKIP)
    value_bias = row_of(small_ref, ROW_GLU)
    gate_bias = row_of(small_ref, ROW_GLU + 1)
    def mixed_copy(step):
        at = pl.ds(pl.multiple_of(step * BLOCK, BLOCK), BLOCK)
        slot = lax.rem(step, 2)
        return pltpu.make_async_copy(mixed.at[slot], mixed_hbm.at[:, at, :], sems.at[slot])

    def run_block(step, _):
        base = pl.multiple_of(step * BLOCK, BLOCK)
        slot = lax.rem(step, 2)
        rows = pl.ds(base, BLOCK)
        pieces = [
            (slice(r, r + SUB), pl.ds(base + r, SUB)) for r in range(0, BLOCK, SUB)
        ]
        chunks = [
            (k, pl.ds(base + k * CHUNK, CHUNK)) for k in range(BLOCK // CHUNK)
        ]
        zeros = jnp.zeros((8, width), F32)
        tiles = lambda count: [slice(n, n + TILE) for n in range(0, count, TILE)]
        spans = tiles(width)
        made = {}
        folds = {}

        def make_states(seq):
            def part(k, at):
                cr, ci = made["carry", seq]
                qr, qi = cmul(cr, ci, enter_r, enter_i)
                sr = back_ref[seq, at, :states]
                si = back_ref[seq, at, states:]
                er, ei = cmul(sr[CHUNK - 1 :], si[CHUNK - 1 :], last_r, last_i)
                nr, ni = cmul(cr, ci, step_r, step_i)
                made["carry", seq] = nr + er, ni + ei
                hr, hi = cmul(sr + qr, si + qi, p_ref[:, :states], p_ref[:, states:])
                state_ref[seq, at, :states] = hr.astype(BF16)
                state_ref[seq, at, states:] = (-hi).astype(BF16)

            def first():
                made["carry", seq] = carry[seq, 0:1, :states], carry[seq, 0:1, states:]

            def last():
                carry[seq, 0:1, :states], carry[seq, 0:1, states:] = made["carry", seq]

            return [first] + [functools.partial(part, *c) for c in chunks] + [last]

        every = range(seqs)
        both = lambda one: jnp.concatenate([one(seq) for seq in every], axis=0)

        def products(name, left, right, columns, turned=False, order=None):
            def part(n):
                if turned:
                    v = dot_nt(both(left), right[n, :])
                else:
                    v = dot_nn(both(left), right[:, n])
                v = v.astype(BF16) if name == "dact" else v
                for seq in every:
                    made.setdefault((name, seq), []).append(v[seq * BLOCK : (seq + 1) * BLOCK])

            return [functools.partial(part, n) for n in (order or tiles(columns))]

        def taken(name, seq, r, first=0, count=None):
            parts = made[name, seq][first:count]
            return jnp.concatenate([v[r] for v in parts], axis=1)

        def gather(name, n, v):
            key = name, n.start
            folds[key] = folds[key] + v if key in folds else v

        def read_out():
            return products("lru", lambda seq: state_ref[seq, rows, :], wout, width)

        def activate(seq, n):
            def part(r, at):
                readout = made["lru", seq][n.start // TILE][r]
                lru = readout + skip[:, n] * normed_ref[seq, at, n].astype(F32)
                lru2 = lru * lru
                gather("lru", n, fold_low(lru2.astype(BF16)))
                gate = 0.5 + 0.5 * jnp.tanh(lru * (GELU_C + GELU_C * GELU_K * lru2))
                gelu = lru * gate
                slope[seq, r, n] = (gate + (gelu - gelu * gate) * (
                    2 * GELU_C + 6 * GELU_C * GELU_K * lru2
                )).astype(BF16)
                act[seq, r, n] = gelu.astype(BF16)

            return [functools.partial(part, *c) for c in pieces]

        def project():
            order = [slice(first + n.start, first + n.stop) for n in spans for first in (0, width)]
            return products("projected", lambda seq: act[seq], wglu, 2 * width, order=order)

        def branch_out(seq, n):
            def part(r, at):
                value = made["projected", seq][2 * (n.start // TILE)][r] + value_bias[:, n]
                gate = made["projected", seq][2 * (n.start // TILE) + 1][r] + gate_bias[:, n]
                gate = 0.5 + 0.5 * jnp.tanh(0.5 * gate)
                branch = value * gate
                mixed[slot, seq, r, n] = (stream_ref[seq, at, n].astype(F32) + branch).astype(BF16)
                gather("branch", n, fold_low((branch * branch).astype(BF16)))
                cot = cot_ref[seq, at, n].astype(F32)
                part = cot * branch
                dvalue = (cot * gate).astype(BF16)
                dgate = (part - part * gate).astype(BF16)
                dproj[seq, r, n] = dvalue
                dproj[seq, r, slice(width + n.start, width + n.stop)] = dgate
                gather("value", n, fold_low(dvalue))
                gather("gate", n, fold_low(dgate))

            return [functools.partial(part, *c) for c in pieces]

        def project_back():
            return products("dact", lambda seq: dproj[seq], wglu, width, True)

        def activate_back(seq, n):
            def part(r, at):
                dlru = made["dact", seq][n.start // TILE][r] * slope[seq, r, n]
                dlru_ref[seq, at, n] = dlru
                gather("dlru", n, fold_low(dlru))
                gather("skip", n, fold_low(dlru * normed_ref[seq, at, n]))

            return [functools.partial(part, *c) for c in pieces]

        def read_out_back():
            return products("pull", lambda seq: dlru_ref[seq, rows, :], wout, 2 * states, True)

        def glu_back():
            def part(n):
                dglu[:, n] += dot_tn(both(lambda seq: act[seq]), both(lambda seq: dproj[seq, :, n]))

            return [functools.partial(part, n) for n in tiles(2 * width)]

        def out_back():
            def part(n):
                dout[:, n] += dot_tn(
                    both(lambda seq: state_ref[seq, rows, :]), both(lambda seq: dlru_ref[seq, rows, n])
                )

            return [functools.partial(part, n) for n in tiles(width)]

        def turn(seq):
            def part(k, at):
                pull = taken("pull", seq, slice(k * CHUNK, (k + 1) * CHUNK))
                zr, zi = cmul(pull[:, :states], pull[:, states:], p_ref[:, :states], p_ref[:, states:])
                split_store(stack.at[seq], k, zr, zi)

            return [functools.partial(part, *c) for c in chunks]

        def sum_back(seq):
            def part(k, at):
                ar, ai = carry[seq, 1:2, :states], carry[seq, 1:2, states:]
                wr, wi = carry[seq, 2:3, :states], carry[seq, 2:3, states:]
                back = dot_nn(tri[...], stack[seq, k])
                back_ref[seq, at, :] = back
                fr, fi = cmul(back[0:1, :states], back[0:1, states:], first_r, first_i)
                gr, gi = cmul(fr, fi, wr, wi)
                ar, ai = ar + gr, ai + gi
                wr, wi = cmul(wr, wi, step_r, step_i)
                carry[seq, 1:2, :states] = ar
                carry[seq, 1:2, states:] = ai
                carry[seq, 2:3, :states] = wr
                carry[seq, 2:3, states:] = wi
                start_ref[seq, :, :states] = ar
                start_ref[seq, :, states:] = ai

            return [functools.partial(part, *c) for c in chunks]

        def run(*lists):
            parts = [(i / len(one), part) for one in lists for i, part in enumerate(one)]
            for _, part in sorted(parts, key=lambda item: item[0]):
                part()

        run(*[make_states(seq) for seq in every])
        readout = read_out()
        for n, part in zip(spans, readout):
            run([part])
            run(*[activate(seq, n) for seq in every])
        projected = project()

        @pl.when(step >= 2)
        def _():
            mixed_copy(step - 2).wait()

        for k, n in enumerate(spans):
            run(projected[2 * k : 2 * k + 2])
            run(*[branch_out(seq, n) for seq in every])
        mixed_copy(step).start()
        for n, part in zip(spans, project_back()):
            run([part])
            run(*[activate_back(seq, n) for seq in every])
        run(read_out_back())
        run(*[turn(seq) for seq in every], out_back() + glu_back())
        run(*[sum_back(seq) for seq in every])
        for row, name in enumerate(("lru", "branch", "dlru", "skip")):
            for n in spans:
                acc_ref[8 * row : 8 * row + 8, n] += folds[name, n.start]
        for row, name in enumerate(("value", "gate")):
            for n in spans:
                gacc_ref[8 * row : 8 * row + 8, n] += folds[name, n.start]

        return 0

    steps = stream_ref.shape[1] // BLOCK
    lax.fori_loop(0, steps, run_block, 0)
    for step in range(max(steps - 2, 0), steps):
        mixed_copy(jnp.int32(step)).wait()
    batch, height, _ = keep_ref.shape
    high = width // (2 * batch)
    part = height - high
    for ref, f in ((keep_ref, place_ref[0]), (send_ref, 1 - place_ref[0])):
        for b in range(batch):
            first = pl.multiple_of((f * batch + b) * high, high)
            ref[b, :high, :] = dglu[pl.ds(first, high), :].astype(BF16)
            first = pl.multiple_of((f * batch + b) * part, part)
            ref[b, high:, :width] = dout[pl.ds(first, part), :].astype(BF16)
            ref[b, high:, width:] = dout[pl.ds(states + first, part), :].astype(BF16)


def block_pass(place, batch, sums, normed, stream, cot, p, small, halves, came):
    seqs, length, width = stream.shape
    states2 = p.shape[1]
    height = width // (2 * batch) + states2 // (4 * batch)
    return pl.pallas_call(
        lambda *refs: block_kernel(len(came), *refs),
        in_specs=[SMEM_SPEC] + [VMEM_SPEC] * (12 + len(came)),
        out_specs=[HBM_SPEC] + [VMEM_SPEC] * 8,
        out_shape=[
            pltpu.HBM((seqs, length, width), BF16),
            pltpu.VMEM((seqs, length, states2), F32),
            pltpu.VMEM((seqs, length, states2), BF16),
            pltpu.VMEM((seqs, length, width), BF16),
            jax.ShapeDtypeStruct((seqs, 1, states2), F32),
            pltpu.VMEM((batch, height, 2 * width), BF16),
            pltpu.VMEM((batch, height, 2 * width), BF16),
            pltpu.VMEM((32, width), F32),
            pltpu.VMEM((16, width), F32),
        ],
        scratch_shapes=[
            pltpu.VMEM((seqs, 8, states2), F32),
            pltpu.VMEM((seqs, BLOCK // CHUNK, 2 * CHUNK, states2), BF16),
            pltpu.VMEM((CHUNK, 2 * CHUNK), BF16),
            pltpu.VMEM((seqs, BLOCK, width), BF16),
            pltpu.VMEM((seqs, BLOCK, 2 * width), BF16),
            pltpu.VMEM((seqs, BLOCK, width), BF16),
            pltpu.VMEM((2, seqs, BLOCK, width), BF16),
            pltpu.VMEM((width, 2 * width), BF16),
            pltpu.VMEM((states2, width), BF16),
            pltpu.VMEM((width, 2 * width), F32),
            pltpu.VMEM((states2, width), F32),
            pltpu.SemaphoreType.DMA((2,)),
        ],
        input_output_aliases={1: 1},
        compiler_params=pltpu.CompilerParams(vmem_limit_bytes=20 * MIB),
        cost_estimate=cost(28),
        name="block_pass",
    )(place, *kept(sums, normed, stream, cot, p, small, *halves, *came))


def adjoint_kernel(
    hops, others, place_ref, back_ref, _, normed_ref, win_ref, q_ref, small_ref, square_ref, acc_ref, gacc_ref,
    *rest,
):
    came = rest[:hops]
    ddrive_ref, keep_ref, send_ref, carry, din = rest[hops + others :]
    states = q_ref.shape[1] // 2
    seqs, length, _ = normed_ref.shape
    every = range(seqs)
    first_r, first_i = pair(small_ref, ROW_FIRST, states)
    back_r, back_i = pair(small_ref, ROW_BACK, states)
    carries = []
    for seq in every:
        entering(carry, came, seq, small_ref, states)
        carries.append((carry[0:1, :states], carry[0:1, states:]))
    real_sum = imag_sum = real_total = imag_total = jnp.zeros((8, states), F32)
    for base in reversed(range(0, length, BLOCK)):
        for k in reversed(range(BLOCK // CHUNK)):
            for seq in every:
                at = pl.ds(base + k * CHUNK, CHUNK)
                qr, qi = cmul(*carries[seq], back_r, back_i)
                vr = back_ref[seq, at, :states] + qr
                vi = back_ref[seq, at, states:] + qi
                carries[seq] = cmul(vr[0:1], vi[0:1], first_r, first_i)
                ar, ai = cmul(vr, vi, q_ref[:, :states], q_ref[:, states:])
                hr = ddrive_ref[seq, at, :states]
                hi = ddrive_ref[seq, at, states:]
                lr, li = ar.astype(BF16), ai.astype(BF16)
                real_sum += fold((lr * hr).astype(F32) + (li * hi).astype(F32))
                imag_sum += fold((lr * hi).astype(F32) - (li * hr).astype(F32))
                real_total += fold_low(lr)
                imag_total += fold_low(li)
                ddrive_ref[seq, at, :states] = lr
                ddrive_ref[seq, at, states:] = li
        rows = pl.ds(base, BLOCK)
        product = dot_tn(
            jnp.concatenate([normed_ref[seq, rows, :] for seq in every], axis=0),
            jnp.concatenate([ddrive_ref[seq, rows, :] for seq in every], axis=0),
        )
        if base == length - BLOCK:
            din[...] = product
        else:
            din[...] += product
    width = din.shape[0]
    gain = row_of(small_ref, ROW_GAIN)
    bias = row_of(small_ref, ROW_BIAS)
    skip = row_of(small_ref, ROW_SKIP)
    weight = win_ref[...].astype(F32)
    grad = din[...]
    in_r, in_i = weight[:, :states], weight[:, states:]
    g_r, g_i = grad[:, :states], grad[:, states:]
    x_r = jnp.sum(g_r * in_r + g_i * in_i, axis=0, keepdims=True)
    x_i = jnp.sum(g_r * in_i - g_i * in_r, axis=0, keepdims=True)
    inverse = small_ref[ROW_SCALE : ROW_SCALE + 1, states:]
    column = lambda v: jnp.sum(v, axis=0, keepdims=True)
    d_r = column(real_sum) * inverse - x_r
    d_i = column(imag_sum) * inverse - x_i
    decay, rotation = pair(small_ref, ROW_RATE, states)
    gathered = dot_nt_wide(jnp.ones((8, 2 * states), F32), weight * grad)[0:1]
    total = jnp.broadcast_to(jnp.concatenate([column(real_total), column(imag_total)], axis=1), (8, 2 * states))
    d_lru = column(acc_ref[16:24, :])
    d_skip = column(acc_ref[24:32, :])
    d_bias = dot_nt_wide(total, weight)[0:1] + skip * d_lru
    d_gain = (gathered + skip * d_skip - bias * d_bias) / gain
    d_nu = -decay * d_r
    d_theta = rotation * d_i
    d_values = column(gacc_ref[0:8, :])
    d_gates = column(gacc_ref[8:16, :])
    lane = lax.broadcasted_iota(jnp.int32, (1, width // 2), 1)
    squares = jnp.zeros((1, width // 2), F32)
    sums = (
        width * jnp.sum(square_ref[:, 0:1]), jnp.sum(acc_ref[0:8, :]), jnp.sum(acc_ref[8:16, :]),
    )
    for place, v in enumerate(sums):
        squares = jnp.where(lane == place, v, squares)
    half, some = width // 2, states // 2
    batch, height, _ = keep_ref.shape
    high = width // (2 * batch)
    me = place_ref[0]

    def chosen(f, low, up):
        return jnp.where(f == 0, low, up)

    for ref, f in ((keep_ref, me), (send_ref, 1 - me)):
        wide = lambda v: chosen(f, v[:, :half], v[:, half:])
        thin = lambda v: chosen(f, v[:, :some], v[:, some:])
        d_glu = chosen(f, d_values, d_gates)
        lines = (
            wide(d_gain),
            wide(d_bias),
            jnp.concatenate([thin(d_nu), thin(d_theta)], axis=1),
            jnp.concatenate([thin(x_r), jnp.zeros((1, some), F32)], axis=1),
            wide(d_skip),
            d_glu[:, :half],
            d_glu[:, half:],
            squares,
        )
        for b in range(batch):
            first = pl.multiple_of((f * batch + b) * high, high)
            ref[b, :high, :states] = din[pl.ds(first, high), :states].astype(BF16)
            ref[b, :high, states:] = (-din[pl.ds(first, high), states:]).astype(BF16)
            line = jnp.concatenate(lines[b * 8 // batch : (b + 1) * 8 // batch], axis=1)
            line = jnp.broadcast_to(line, (height - high, width)).astype(BF16)
            ref[b, high:, :] = line


def adjoint_pass(
    place, batch, back, state, normed, wback, q, small, square, acc, gacc, came, after
):
    seqs, length, width = normed.shape
    states2 = q.shape[1]
    return pl.pallas_call(
        lambda *refs: adjoint_kernel(len(came), len(after), *refs),
        in_specs=[SMEM_SPEC] + [VMEM_SPEC] * (9 + len(came)) + specs_of(after),
        out_specs=[VMEM_SPEC] * 3,
        out_shape=[
            pltpu.VMEM((seqs, length, states2), BF16),
            pltpu.VMEM((batch, width // (2 * batch) + 16, states2), BF16),
            pltpu.VMEM((batch, width // (2 * batch) + 16, states2), BF16),
        ],
        scratch_shapes=[
            pltpu.VMEM((8, states2), F32),
            pltpu.VMEM((width, states2), F32),
        ],
        input_output_aliases={2: 0},
        compiler_params=pltpu.CompilerParams(vmem_limit_bytes=8 * MIB),
        cost_estimate=cost(7),
        name="adjoint_pass",
    )(place, *kept(back, state, normed, wback, q, small, square, acc, gacc, *came), *placed(after))


def input_kernel(seq, skipped, ddrive_ref, dlru_ref, stream_ref, cot_ref, small_ref, win_ref, *rest):
    out_ref = rest[-1]
    base = (pl.program_id(0) + skipped) * BLOCK
    gain = row_of(small_ref, ROW_GAIN)
    skip = row_of(small_ref, ROW_SKIP)
    rows = pl.ds(pl.multiple_of(base, BLOCK), BLOCK)
    pulled = dot_nt(ddrive_ref[seq, rows, :], win_ref[...])
    for r in range(0, BLOCK, SUB):
        at = pl.ds(pl.multiple_of(base + r, SUB), SUB)
        d = pulled[r : r + SUB] + skip * dlru_ref[seq, at, :].astype(F32)
        x = stream_ref[seq, at, :].astype(F32)
        centre = x - jnp.mean(x, axis=-1, keepdims=True)
        spread = jnp.mean(centre * centre, axis=-1, keepdims=True)
        inverse = lax.rsqrt(spread + 1e-05)
        hat = centre * inverse
        dhat = d * gain
        m1 = jnp.mean(dhat, axis=-1, keepdims=True)
        m2 = jnp.mean(dhat * hat, axis=-1, keepdims=True)
        out_ref[r : r + SUB, :] = (dhat - m1 - hat * m2) * inverse + cot_ref[seq, at, :].astype(F32)


def input_pass(part, ddrive, dlru, stream, cot, small, win, earlier, after):
    seq, skipped, blocks = part
    seqs, length, width = stream.shape
    earlier = in_hbm(*earlier)
    return pl.pallas_call(
        lambda *refs: input_kernel(seq, skipped, *refs),
        grid=(blocks,),
        in_specs=[VMEM_SPEC] * 6 + [HBM_SPEC] * len(earlier) + specs_of(after),
        out_specs=pl.BlockSpec((None, BLOCK, width), lambda i: (seq, i + skipped, 0)),
        out_shape=pltpu.HBM((seqs, length, width), F32),
        input_output_aliases={6: 0} if earlier else {},
        compiler_params=pltpu.CompilerParams(vmem_limit_bytes=8 * MIB),
        cost_estimate=cost(1.1 * blocks),
        name="input_pass",
    )(*kept(ddrive, dlru, stream, cot, small, win), *earlier, *placed(after))


def pack_kernel(count, *refs):
    out_ref = refs[count]
    parts = refs[count + 1 : -1]
    copies = [
        pltpu.make_async_copy(source, target, refs[-1].at[k])
        for k, (source, target) in enumerate(zip(refs[:count], parts))
    ]
    for c in copies:
        c.start()
    for c in copies:
        c.wait()
    row = 0
    for ref in parts:
        for first in range(0, ref.shape[0], 128):
            out_ref[row : row + 1, :] = ref[first : first + 128].reshape(1, 128)
            row += 1


def pack_vectors(*vectors):
    rows = sum(v.shape[0] for v in vectors) // 128
    return pl.pallas_call(
        lambda *refs: pack_kernel(len(vectors), *refs),
        in_specs=[HBM_SPEC] * len(vectors),
        out_specs=VMEM_SPEC,
        out_shape=pltpu.VMEM((rows, 128), BF16),
        scratch_shapes=[pltpu.VMEM(v.shape, BF16) for v in vectors]
        + [pltpu.SemaphoreType.DMA((len(vectors),))],
        compiler_params=pltpu.CompilerParams(vmem_limit_bytes=2 * MIB),
        name="pack_vectors",
    )(*in_hbm(*vectors))


def pair_kernel(others, place_ref, keep_ref, came_ref, *rest):
    for hop, ref in enumerate(rest[others:]):
        at = place_ref[1] ^ hop
        ref[...] = (keep_ref[at].astype(F32) + came_ref[at].astype(F32)).astype(BF16)


def pair_sum(place, keep, came, after=()):
    count = keep.shape[0]
    return pl.pallas_call(
        lambda *refs: pair_kernel(len(after), *refs),
        in_specs=[SMEM_SPEC] + [VMEM_SPEC] * 2 + specs_of(after),
        out_specs=[VMEM_SPEC] * count,
        out_shape=[pltpu.VMEM(keep.shape[1:], BF16)] * count,
        compiler_params=pltpu.CompilerParams(vmem_limit_bytes=4 * MIB),
        cost_estimate=cost(0.7),
        name="pair_sum",
    )(place, *kept(keep, came), *placed(after))


def add_kernel(count, *refs):
    total = refs[0][...].astype(F32)
    for ref in refs[1:count]:
        total += ref[...].astype(F32)
    refs[-1][...] = total.astype(BF16)


def add_up(got, after=()):
    return pl.pallas_call(
        lambda *refs: add_kernel(len(got), *refs),
        in_specs=[VMEM_SPEC] * len(got) + specs_of(after),
        out_specs=VMEM_SPEC,
        out_shape=pltpu.VMEM(got[0].shape, BF16),
        compiler_params=pltpu.CompilerParams(vmem_limit_bytes=4 * MIB),
        cost_estimate=cost(0.2),
        name="add_up",
    )(*kept(*got), *placed(after))


def split_kernel(count, others, place_ref, *refs):
    total = refs[0]
    pieces = refs[count + others :]
    wide = total.shape[1] // len(pieces)
    for hop, ref in enumerate(pieces):
        at = lax.rem(place_ref[2] + hop, len(pieces))
        columns = pl.ds(pl.multiple_of(at * wide, wide), wide)
        v = refs[0][:, columns].astype(F32)
        for other in refs[1:count]:
            v += other[:, columns].astype(F32)
        ref[...] = v.astype(BF16)


def add_split(place, got, ring, after=()):
    rows, columns = got[0].shape
    return pl.pallas_call(
        lambda *refs: split_kernel(len(got), len(after), *refs),
        in_specs=[SMEM_SPEC] + [VMEM_SPEC] * len(got) + specs_of(after),
        out_specs=[VMEM_SPEC] * ring,
        out_shape=[pltpu.VMEM((rows, columns // ring), BF16)] * ring,
        compiler_params=pltpu.CompilerParams(vmem_limit_bytes=4 * MIB),
        cost_estimate=cost(0.3),
        name="add_split",
    )(place, *kept(*got), *placed(after))


def finish_kernel(count, place_ref, *refs):
    first, second, out_ref = refs[:count], refs[count : 2 * count], refs[-1]
    rows, wide = first[0].shape
    span = out_ref.shape[1]
    for hop in range(count):
        at = lax.rem(place_ref[2] + count - hop, count)
        if wide < span:
            per = span // wide
            row = pl.multiple_of(lax.div(at, per) * rows, rows)
            column = pl.multiple_of(lax.rem(at, per) * wide, wide)
            out_ref[pl.ds(row, rows), pl.ds(column, wide)] = first[hop][...]
        else:
            for k in range(wide // span):
                row = pl.multiple_of((at * (wide // span) + k) * rows, rows)
                out_ref[pl.ds(row, rows), :] = first[hop][:, k * span : (k + 1) * span]
    total = second[0][...].astype(F32)
    for ref in second[1:]:
        total += ref[...].astype(F32)
    out_ref[out_ref.shape[0] - total.shape[0] :, :] = total.astype(BF16)


def finish_seq(place, first, second, after):
    rows, wide = first[0].shape
    low, span = second[0].shape
    height = rows * wide * len(first) // span + low
    return pl.pallas_call(
        lambda *refs: finish_kernel(len(first), *refs),
        in_specs=[SMEM_SPEC] + [VMEM_SPEC] * (2 * len(first)) + specs_of(after),
        out_specs=VMEM_SPEC,
        out_shape=pltpu.VMEM((height, span), BF16),
        compiler_params=pltpu.CompilerParams(vmem_limit_bytes=4 * MIB),
        cost_estimate=cost(0.5),
        name="finish_seq",
    )(place, *kept(*first, *second), *placed(after))


def unpack_kernel(count, others, tokens, place_ref, *refs):
    got = refs[:count]
    (
        glu_ref, outr_ref, outi_ref, inr_ref, ini_ref, gain_ref, bias_ref, nu_ref, theta_ref,
        gamma_ref, skip_ref, glub_ref, rms_ref, lines,
    ) = refs[count + others :]
    width = glu_ref.shape[1] // 2
    states = inr_ref.shape[1]
    high = glu_ref.shape[0] // count
    part = outr_ref.shape[0] // count
    low = 2 * (high + part)
    for hop in range(count):
        at = place_ref[1] ^ hop
        v = got[hop]
        rows = pl.ds(pl.multiple_of(at * high, high), high)
        few = pl.ds(pl.multiple_of(at * part, part), part)
        glu_ref[rows, :width] = v[:high, :].astype(F32)
        outr_ref[few, :] = v[high : high + part, :].astype(F32)
        glu_ref[rows, width:] = v[high + part : 2 * high + part, :].astype(F32)
        outi_ref[few, :] = v[2 * high + part : low, :].astype(F32)
        inr_ref[rows, :] = v[low : low + high, :states].astype(F32)
        ini_ref[rows, :] = v[low : low + high, states:].astype(F32)
        lines[pl.ds(pl.multiple_of(at * 8, 8), 8), :] = v[low + high :, :].astype(F32)[:8]
    half, some = width // 2, states // 2
    per = 8 // count
    line = lambda k: lines[k // per * 8 : k // per * 8 + 1, k % per * half : (k % per + 1) * half]
    gain_ref[...] = line(0)
    bias_ref[...] = line(1)
    nu_ref[...] = line(2)[:, :some]
    theta_ref[...] = line(2)[:, some:]
    gamma_ref[...] = line(3)[:, :some]
    skip_ref[...] = line(4)
    glub_ref[:, :half] = line(5)
    glub_ref[:, half:] = line(6)
    rms_ref[...] = jnp.sqrt(line(7)[:, :3] / tokens)


def unpack(place, got, width, states, tokens, after):
    count = len(got)
    flat = [width // 2, width // 2, states // 2, states // 2, states // 2, width // 2, width, 3]
    return pl.pallas_call(
        lambda *refs: unpack_kernel(count, len(after), tokens, *refs),
        in_specs=[SMEM_SPEC] + [VMEM_SPEC] * count + specs_of(after),
        out_specs=[VMEM_SPEC] * 13,
        out_shape=[
            jax.ShapeDtypeStruct((width // 2, 2 * width), F32),
            jax.ShapeDtypeStruct((states // 2, width), F32),
            jax.ShapeDtypeStruct((states // 2, width), F32),
            jax.ShapeDtypeStruct((width // 2, states), F32),
            jax.ShapeDtypeStruct((width // 2, states), F32),
        ]
        + [jax.ShapeDtypeStruct((1, n), F32) for n in flat],
        scratch_shapes=[pltpu.VMEM((8 * count, width), F32)],
        compiler_params=pltpu.CompilerParams(vmem_limit_bytes=8 * MIB),
        name="unpack",
    )(place, *got, *placed(after))


def hops_of(ends, axis, reverse):
    count = lax.axis_size(axis)
    if count <= 4:
        return [
            lax.ppermute(
                ends,
                axis,
                [(i + hop, i) if reverse else (i, i + hop) for i in range(count - hop)],
            )
            for hop in range(1, count)
        ]
    place = lax.axis_index(axis)
    every = lax.all_gather(ends, axis)
    came = []
    for hop in range(1, count):
        source = place + hop if reverse else place - hop
        inside = (source >= 0) & (source < count)
        item = lax.dynamic_index_in_dim(every, jnp.clip(source, 0, count - 1), 0, False)
        came.append(jnp.where(inside, item, 0.0))
    return came


def swap(a):
    return lax.ppermute(a, "fsdp", [(0, 1), (1, 0)])


def swap_moves(axis, bit):
    return [(i, i ^ bit) for i in range(lax.axis_size(axis))]


def scatter_batch(pieces):
    return [pieces[0]] + [
        lax.ppermute(pieces[hop], "batch", swap_moves("batch", hop))
        for hop in range(1, len(pieces))
    ]


def around(pieces):
    ring = lax.axis_size("seq")
    return [pieces[0]] + [
        lax.ppermute(pieces[hop], "seq", [(i, (i + hop) % ring) for i in range(ring)])
        for hop in range(1, ring)
    ]


def share_seq(piece):
    ring = lax.axis_size("seq")
    if ring > 4:
        return [lax.psum(piece.astype(F32), "seq").astype(BF16)]
    return around([piece] * ring)


def gather_batch(piece):
    count = lax.axis_size("batch")
    return [piece] + [
        lax.ppermute(piece, "batch", swap_moves("batch", hop)) for hop in range(1, count)
    ]


def on_device(
    stream, norm_gain, norm_bias, in_real, in_imag, nu_log, theta_log, gamma_log, out_real,
    out_imag, skip_scale, glu_weight, glu_bias, cotangent,
):
    seqs, length, width = stream.shape
    states = 2 * nu_log.shape[0]
    batch = lax.axis_size("batch")
    place = jnp.stack(
        [lax.axis_index("fsdp"), lax.axis_index("batch"), lax.axis_index("seq")]
    ).astype(jnp.int32)
    place, in_real, in_imag, glu_weight, out_real, out_imag = lax.optimization_barrier(
        (place, in_real, in_imag, glu_weight, out_real, out_imag)
    )
    vectors = pack_vectors(
        norm_gain, norm_bias, skip_scale, glu_bias, nu_log, theta_log, gamma_log
    )
    into = [in_real, swap(in_real), in_imag, swap(in_imag)]
    others = [swap(glu_weight), swap(out_real), swap(out_imag)]
    (
        normed, sums, ends, p, q, small, win, wback, square, stream_kept, cot_kept, *own,
    ) = norm_pass(
        place, stream, cotangent, into, [glu_weight, out_real, out_imag], [vectors, swap(vectors)]
    )
    halves = [a for pair_of in zip(own, others) for a in pair_of]
    came = hops_of(ends, "seq", False)
    mixed, back, state, dlru, starts, keep, send, acc, gacc = block_pass(
        place, batch, sums, normed, stream_kept, cot_kept, p, small, halves, came
    )
    later = hops_of(starts, "seq", True)
    pieces = pair_sum(place, keep, swap(send), later)
    first = scatter_batch(pieces)
    ddrive, keep, send = adjoint_pass(
        place, batch, back, state, normed, wback, q, small, square, acc, gacc, later, pieces
    )
    ring = lax.axis_size("seq")
    short = ring <= 4
    first = add_split(place, first, ring if short else 1, [send])
    send, *first = lax.optimization_barrier((send, *first))
    pieces = pair_sum(place, keep, swap(send))
    second = scatter_batch(pieces)
    first = around(first) if short else share_seq(first[0])
    last = lambda part, earlier, after: input_pass(
        part, ddrive, dlru, stream_kept, cot_kept, small, wback, earlier, after
    )
    blocks = length // BLOCK
    grads = (last((0, 0, blocks // 2), (), [first[0], pieces[0]]),)
    first = add_up(first, grads)
    if short:
        first = around([first] * ring)
    second = share_seq(add_up(second, [first[0], *grads]))
    for seq in range(1, seqs):
        grads = (last((seq, 0, blocks), grads, [first[0], second[0]]),)
    got = gather_batch(finish_seq(place, first if short else [first], second, grads))
    grads = (last((0, blocks // 2, blocks - blocks // 2), grads, got[:1]),)
    grad_stream = grads[0]
    tokens = stream.size * batch * lax.axis_size("seq") * lax.axis_size("fsdp")
    (
        glu, out_r, out_i, in_r, in_i, gain, bias, nu, theta, gamma, skip, glub, rms,
    ) = unpack(place, got, width, states, float(tokens), grads)
    flat = lambda a: a.reshape(-1)
    return (
        mixed, grad_stream, flat(gain), flat(bias), in_r, in_i, flat(nu), flat(theta), flat(gamma),
        out_r, out_i, flat(skip), glu, flat(glub), flat(rms),
    )


def solution(mesh):
    tokens = P(("batch", "fsdp"), "seq", None)
    vector = P("fsdp")
    matrix = P("fsdp", None)
    weights = (
        vector, vector, matrix, matrix, vector, vector, vector, matrix, matrix, vector, matrix,
        vector,
    )
    return jax.shard_map(
        on_device,
        mesh=mesh,
        in_specs=(tokens,) + weights + (tokens,),
        out_specs=(tokens, tokens) + weights + (P(),),
        check_vma=False,
    )
```

```python
import functools

import jax
import jax.numpy as jnp
from jax import lax
from jax.experimental import pallas as pl
from jax.experimental.pallas import tpu as pltpu
from jax.sharding import PartitionSpec as P

F32 = jnp.float32
BF16 = jnp.bfloat16
HIGHEST = lax.Precision.HIGHEST
CHUNK = 128
HALF = 64
BLOCK = 512
SUB = 64
TILE = 256
GELU_C = 0.7978845608028654
GELU_K = 0.044715
MIB = 1024 * 1024


def dot_nn(a, b):
    return jnp.dot(a, b, preferred_element_type=F32)


def dot_tn(a, b):
    return lax.dot_general(a, b, (((0,), (0,)), ((), ())), preferred_element_type=F32)


def dot_nt(a, b):
    return lax.dot_general(a, b, (((1,), (1,)), ((), ())), preferred_element_type=F32)


def dot_nt_wide(a, b):
    return lax.dot_general(
        a, b, (((1,), (1,)), ((), ())), precision=HIGHEST, preferred_element_type=F32
    )


def cmul(ar, ai, br, bi):
    return ar * br - ai * bi, ar * bi + ai * br


def fold(v):
    return jnp.sum(v.reshape(v.shape[0] // 8, 8, v.shape[1]), axis=0)


def fold_low(v):
    rows = v.shape[0] // 4
    v = (v[:rows] + v[rows : 2 * rows]) + (v[2 * rows : 3 * rows] + v[3 * rows :])
    return fold(v.astype(F32))


def split_store(stack, k, zr, zi):
    states = zr.shape[1]
    for part, v in enumerate((zr, zi)):
        columns = pl.ds(part * states, states)
        high = v.astype(BF16)
        stack[k, :CHUNK, columns] = high
        stack[k, CHUNK:, columns] = (v - high.astype(F32)).astype(BF16)


def fill_triangle(tri, upper):
    row = lax.broadcasted_iota(jnp.int32, (CHUNK, CHUNK), 0)
    column = lax.broadcasted_iota(jnp.int32, (CHUNK, CHUNK), 1)
    inside = (column >= row) if upper else (column <= row)
    ones = jnp.where(inside, 1.0, 0.0).astype(BF16)
    tri[:, :CHUNK] = ones
    tri[:, CHUNK:] = ones


ROW_STEP = 0
ROW_LAST = 1
ROW_ENTER = 2
ROW_FIRST = 3
ROW_BACK = 4
ROW_WHOLE = 5
ROW_SCALE = 6
ROW_RATE = 7
ROW_GAIN = 8
ROW_BIAS = 9
ROW_SKIP = 10
ROW_GLU = 11
TABLE_ROWS = 16


def pair(ref, row, states):
    return ref[row : row + 1, :states], ref[row : row + 1, states:]


def row_of(ref, row):
    return ref[row : row + 1, :]


def fill_tables(me, own_ref, other_ref, p_ref, q_ref, small_ref, length):
    states = q_ref.shape[1] // 2
    width = q_ref.shape[1]
    own = own_ref[...].astype(F32)
    other = other_ref[...].astype(F32)
    low = jnp.where(me == 0, own, other)
    high = jnp.where(me == 0, other, own)

    def both(first, count):
        rows = [h[first + i : first + i + 1] for h in (low, high) for i in range(count)]
        return jnp.concatenate(rows, axis=1)

    small_ref[...] = jnp.zeros_like(small_ref)
    for row, first in ((ROW_GAIN, 0), (ROW_BIAS, 2), (ROW_SKIP, 4)):
        small_ref[row : row + 1, :] = both(first, 2)
    glu = both(6, 4)
    small_ref[ROW_GLU : ROW_GLU + 1, :] = glu[:, :width]
    small_ref[ROW_GLU + 1 : ROW_GLU + 2, :] = glu[:, width:]
    decay = jnp.exp(both(10, 1))
    rotation = jnp.exp(both(11, 1))
    scale = jnp.exp(both(12, 1))
    steps = (lax.broadcasted_iota(jnp.int32, (CHUNK, states), 0) - HALF).astype(F32)
    turn = steps * rotation
    cos = jnp.cos(turn)
    sin = jnp.sin(turn)
    grow = jnp.exp(-steps * decay)
    p_ref[:, :states] = grow * cos
    p_ref[:, states:] = grow * sin
    shrink = scale * jnp.exp(steps * decay)
    q_ref[:, :states] = shrink * cos
    q_ref[:, states:] = -shrink * sin
    counts = {
        ROW_STEP: CHUNK,
        ROW_LAST: CHUNK - 1 - HALF,
        ROW_ENTER: HALF + 1,
        ROW_FIRST: HALF,
        ROW_BACK: CHUNK - HALF,
        ROW_WHOLE: length,
    }
    assert sorted(counts) == list(range(6))
    index = lax.broadcasted_iota(jnp.int32, (8, states), 0)
    count = jnp.zeros((8, states), F32)
    for row, steps in counts.items():
        count = jnp.where(index == row, float(steps), count)
    size = jnp.exp(-count * decay)
    small_ref[:6, :states] = (size * jnp.cos(count * rotation))[:6]
    small_ref[:6, states:] = (size * jnp.sin(count * rotation))[:6]
    small_ref[ROW_SCALE : ROW_SCALE + 1, :states] = scale
    small_ref[ROW_SCALE : ROW_SCALE + 1, states:] = 1.0 / scale
    small_ref[ROW_RATE : ROW_RATE + 1, :states] = decay
    small_ref[ROW_RATE : ROW_RATE + 1, states:] = rotation


def join_halves(me, whole, own, other, columns=slice(None)):
    rows = own.shape[0]
    whole[pl.ds(pl.multiple_of(me * rows, rows), rows), columns] = own[...]
    whole[pl.ds(pl.multiple_of((1 - me) * rows, rows), rows), columns] = other[...]


def cost(microseconds):
    return pl.CostEstimate(
        flops=0, transcendentals=0, bytes_accessed=int(microseconds * 3.6e6)
    )


def norm_kernel(
    length, place_ref, stream_hbm, cot_hbm, inr_hbm, ini_hbm, glu_hbm, outr_hbm, outi_hbm,
    vec_own, vec_other, inr_other, ini_other,
    normed_ref, sums_ref, end_ref, p_ref, q_ref, small_ref, win_ref, wback_ref, square_ref,
    stream_ref, cot_ref, glu_ref, outr_ref, outi_ref,
    stack, tri, inr_own, ini_own, sems,
):
    states = q_ref.shape[1] // 2
    seqs = stream_ref.shape[0]
    every = range(seqs)
    copy = lambda source, target, k: pltpu.make_async_copy(source, target, sems.at[k])
    weights = [copy(inr_hbm, inr_own, 0), copy(ini_hbm, ini_own, 1)]
    onward = [
        copy(source, target, 2 + k)
        for k, (source, target) in enumerate(
            ((glu_hbm, glu_ref), (outr_hbm, outr_ref), (outi_hbm, outi_ref), (cot_hbm, cot_ref))
        )
    ]

    def stream_copy(step):
        at = (slice(None), pl.ds(pl.multiple_of(step * BLOCK, BLOCK), BLOCK))
        return copy(stream_hbm.at[at], stream_ref.at[at], 6 + step)

    blocks = [stream_copy(step) for step in range(length // BLOCK)]
    for c in blocks[:1] + weights + blocks[1:] + onward:
        c.start()
    me = place_ref[0]
    fill_tables(me, vec_own, vec_other, p_ref, q_ref, small_ref, length)
    fill_triangle(tri, False)
    for c in weights:
        c.wait()
    join_halves(me, win_ref, inr_own, inr_other, slice(0, states))
    join_halves(me, win_ref, ini_own, ini_other, slice(states, 2 * states))
    wback_ref[:, :states] = win_ref[:, :states]
    wback_ref[:, states:] = -win_ref[:, states:]

    gain = row_of(small_ref, ROW_GAIN)
    bias = row_of(small_ref, ROW_BIAS)
    step_r, step_i = pair(small_ref, ROW_STEP, states)
    last_r, last_i = pair(small_ref, ROW_LAST, states)

    def run_block(step, state):
        squares, ends = state
        ends = list(ends)
        base = pl.multiple_of(step * BLOCK, BLOCK)
        rows = pl.ds(base, BLOCK)
        stream_copy(step).wait()
        for r in range(0, BLOCK, SUB):
            for seq in every:
                at = pl.ds(base + r, SUB)
                x = stream_ref[seq, at, :].astype(F32)
                mean = jnp.mean(x, axis=-1, keepdims=True)
                centre = x - mean
                spread = jnp.mean(centre * centre, axis=-1, keepdims=True)
                squares += fold(mean * mean + spread)
                normed_ref[seq, at, :] = (
                    centre * lax.rsqrt(spread + 1e-05) * gain + bias
                ).astype(BF16)
        left = jnp.concatenate([normed_ref[seq, rows, :] for seq in every], axis=0)
        drive = dot_nn(left, win_ref[...])
        for k in range(BLOCK // CHUNK):
            for seq in every:
                first = seq * BLOCK + k * CHUNK
                part = drive[first : first + CHUNK]
                zr, zi = cmul(
                    part[:, :states], part[:, states:], q_ref[:, :states], q_ref[:, states:]
                )
                slot = stack.at[seq]
                split_store(slot, k, zr, zi)
                s = dot_nn(tri[...], slot[k])
                sums_ref[seq, pl.ds(base + k * CHUNK, CHUNK), :] = s
                er, ei = cmul(s[CHUNK - 1 :, :states], s[CHUNK - 1 :, states:], last_r, last_i)
                nr, ni = cmul(*ends[seq], step_r, step_i)
                ends[seq] = nr + er, ni + ei
        return squares, tuple(ends)

    zero = jnp.zeros((1, states), F32)
    squares, ends = lax.fori_loop(
        0, length // BLOCK, run_block, (jnp.zeros((8, 1), F32), ((zero, zero),) * seqs)
    )
    square_ref[...] = jnp.broadcast_to(squares, square_ref.shape)
    for seq in every:
        end_ref[seq, :, :states], end_ref[seq, :, states:] = ends[seq]
    for c in onward:
        c.wait()


HBM_SPEC = pl.BlockSpec(memory_space=pltpu.HBM)
VMEM_SPEC = pl.BlockSpec(memory_space=pltpu.VMEM)
SMEM_SPEC = pl.BlockSpec(memory_space=pltpu.SMEM)


def kept(*arrays):
    return [pltpu.with_memory_space_constraint(a, pltpu.VMEM) for a in arrays]


def large(a):
    return a.size * a.dtype.itemsize > 2 * MIB


def specs_of(arrays):
    return [HBM_SPEC if large(a) else VMEM_SPEC for a in arrays]


def placed(arrays):
    return [in_hbm(a)[0] if large(a) else kept(a)[0] for a in arrays]


def in_hbm(*arrays):
    return [pltpu.with_memory_space_constraint(a, pltpu.HBM) for a in arrays]


def norm_pass(place, stream, cot, into, onward, vectors):
    seqs, length, width = stream.shape
    half, states = into[0].shape
    states2 = 2 * states
    return pl.pallas_call(
        lambda *refs: norm_kernel(length, *refs),
        in_specs=[SMEM_SPEC] + [HBM_SPEC] * 7 + [VMEM_SPEC] * 4,
        out_specs=[VMEM_SPEC] * 14,
        out_shape=[
            pltpu.VMEM((seqs, length, width), BF16),
            pltpu.VMEM((seqs, length, states2), F32),
            pltpu.VMEM((seqs, 1, states2), F32),
            pltpu.VMEM((CHUNK, states2), F32),
            pltpu.VMEM((CHUNK, states2), F32),
            pltpu.VMEM((TABLE_ROWS, states2), F32),
            pltpu.VMEM((width, states2), BF16),
            pltpu.VMEM((width, states2), BF16),
            pltpu.VMEM((8, 128), F32),
            pltpu.VMEM(stream.shape, BF16),
            pltpu.VMEM(cot.shape, BF16),
        ]
        + [pltpu.VMEM(a.shape, BF16) for a in onward],
        scratch_shapes=[
            pltpu.VMEM((seqs, BLOCK // CHUNK, 2 * CHUNK, states2), BF16),
            pltpu.VMEM((CHUNK, 2 * CHUNK), BF16),
            pltpu.VMEM((half, states), BF16),
            pltpu.VMEM((half, states), BF16),
            pltpu.SemaphoreType.DMA((length // BLOCK + 6,)),
        ],
        compiler_params=pltpu.CompilerParams(vmem_limit_bytes=8 * MIB),
        cost_estimate=cost(9),
        name="norm_pass",
    )(
        place,
        *in_hbm(stream, cot, into[0], into[2], *onward),
        *kept(*vectors, into[1], into[3]),
    )


def entering(carry, came, seq, small_ref, states):
    whole_r, whole_i = pair(small_ref, ROW_WHOLE, states)
    total_r = came[0][seq, :, :states]
    total_i = came[0][seq, :, states:]
    power_r, power_i = whole_r, whole_i
    for ref in came[1:]:
        gr, gi = cmul(ref[seq, :, :states], ref[seq, :, states:], power_r, power_i)
        total_r, total_i = total_r + gr, total_i + gi
        power_r, power_i = cmul(power_r, power_i, whole_r, whole_i)
    carry[0:1, :states] = total_r
    carry[0:1, states:] = total_i


def block_kernel(
    hops, place_ref, _, normed_ref, stream_ref, cot_ref, p_ref, small_ref, glu_own, glu_other,
    outr_own, outr_other, outi_own, outi_other, *rest,
):
    came = rest[:hops]
    (
        mixed_hbm, back_ref, state_ref, dlru_ref, start_ref, keep_ref, send_ref, acc_ref, gacc_ref,
        carry, stack, tri, act, dproj, slope, mixed, wglu, wout, dglu, dout, sems,
    ) = rest[hops:]
    states = p_ref.shape[1] // 2
    seqs, _, width = stream_ref.shape
    me = place_ref[0]
    join_halves(me, wglu, glu_own, glu_other)
    join_halves(me, wout.at[pl.ds(0, states)], outr_own, outr_other)
    join_halves(me, wout.at[pl.ds(states, states)], outi_own, outi_other)
    fill_triangle(tri, True)
    acc_ref[...] = jnp.zeros_like(acc_ref)
    gacc_ref[...] = jnp.zeros_like(gacc_ref)
    dglu[...] = jnp.zeros_like(dglu)
    dout[...] = jnp.zeros_like(dout)
    for seq in range(seqs):
        entering(carry.at[seq], came, seq, small_ref, states)
        carry[seq, 1:2, :] = jnp.zeros_like(carry[seq, 1:2, :])
        carry[seq, 2:3, :states] = jnp.ones_like(carry[seq, 2:3, :states])
        carry[seq, 2:3, states:] = jnp.zeros_like(carry[seq, 2:3, states:])

    step_r, step_i = pair(small_ref, ROW_STEP, states)
    last_r, last_i = pair(small_ref, ROW_LAST, states)
    enter_r, enter_i = pair(small_ref, ROW_ENTER, states)
    first_r, first_i = pair(small_ref, ROW_FIRST, states)
    skip = row_of(small_ref, ROW_SKIP)
    value_bias = row_of(small_ref, ROW_GLU)
    gate_bias = row_of(small_ref, ROW_GLU + 1)
    def mixed_copy(step):
        at = pl.ds(pl.multiple_of(step * BLOCK, BLOCK), BLOCK)
        slot = lax.rem(step, 2)
        return pltpu.make_async_copy(mixed.at[slot], mixed_hbm.at[:, at, :], sems.at[slot])

    def run_block(step, _):
        base = pl.multiple_of(step * BLOCK, BLOCK)
        slot = lax.rem(step, 2)
        rows = pl.ds(base, BLOCK)
        pieces = [
            (slice(r, r + SUB), pl.ds(base + r, SUB)) for r in range(0, BLOCK, SUB)
        ]
        chunks = [
            (k, pl.ds(base + k * CHUNK, CHUNK)) for k in range(BLOCK // CHUNK)
        ]
        zeros = jnp.zeros((8, width), F32)
        tiles = lambda count: [slice(n, n + TILE) for n in range(0, count, TILE)]
        spans = tiles(width)
        made = {}
        folds = {}

        def make_states(seq):
            def part(k, at):
                cr, ci = made["carry", seq]
                qr, qi = cmul(cr, ci, enter_r, enter_i)
                sr = back_ref[seq, at, :states]
                si = back_ref[seq, at, states:]
                er, ei = cmul(sr[CHUNK - 1 :], si[CHUNK - 1 :], last_r, last_i)
                nr, ni = cmul(cr, ci, step_r, step_i)
                made["carry", seq] = nr + er, ni + ei
                hr, hi = cmul(sr + qr, si + qi, p_ref[:, :states], p_ref[:, states:])
                state_ref[seq, at, :states] = hr.astype(BF16)
                state_ref[seq, at, states:] = (-hi).astype(BF16)

            def first():
                made["carry", seq] = carry[seq, 0:1, :states], carry[seq, 0:1, states:]

            def last():
                carry[seq, 0:1, :states], carry[seq, 0:1, states:] = made["carry", seq]

            return [first] + [functools.partial(part, *c) for c in chunks] + [last]

        every = range(seqs)
        both = lambda one: jnp.concatenate([one(seq) for seq in every], axis=0)

        def products(name, left, right, columns, turned=False, order=None):
            def part(n):
                if turned:
                    v = dot_nt(both(left), right[n, :])
                else:
                    v = dot_nn(both(left), right[:, n])
                v = v.astype(BF16) if name == "dact" else v
                for seq in every:
                    made.setdefault((name, seq), []).append(v[seq * BLOCK : (seq + 1) * BLOCK])

            return [functools.partial(part, n) for n in (order or tiles(columns))]

        def taken(name, seq, r, first=0, count=None):
            parts = made[name, seq][first:count]
            return jnp.concatenate([v[r] for v in parts], axis=1)

        def gather(name, n, v):
            key = name, n.start
            folds[key] = folds[key] + v if key in folds else v

        def read_out():
            return products("lru", lambda seq: state_ref[seq, rows, :], wout, width)

        def activate(seq, n):
            def part(r, at):
                readout = made["lru", seq][n.start // TILE][r]
                lru = readout + skip[:, n] * normed_ref[seq, at, n].astype(F32)
                lru2 = lru * lru
                gather("lru", n, fold(lru2))
                gate = 0.5 + 0.5 * jnp.tanh(lru * (GELU_C + GELU_C * GELU_K * lru2))
                gelu = lru * gate
                slope[seq, r, n] = (gate + (gelu - gelu * gate) * (
                    2 * GELU_C + 6 * GELU_C * GELU_K * lru2
                )).astype(BF16)
                act[seq, r, n] = gelu.astype(BF16)

            return [functools.partial(part, *c) for c in pieces]

        def project():
            order = [slice(first + n.start, first + n.stop) for n in spans for first in (0, width)]
            return products("projected", lambda seq: act[seq], wglu, 2 * width, order=order)

        def branch_out(seq, n):
            def part(r, at):
                value = made["projected", seq][2 * (n.start // TILE)][r] + value_bias[:, n]
                gate = made["projected", seq][2 * (n.start // TILE) + 1][r] + gate_bias[:, n]
                gate = 0.5 + 0.5 * jnp.tanh(0.5 * gate)
                branch = value * gate
                mixed[slot, seq, r, n] = (stream_ref[seq, at, n].astype(F32) + branch).astype(BF16)
                gather("branch", n, fold(branch * branch))
                cot = cot_ref[seq, at, n].astype(F32)
                part = cot * branch
                dvalue = (cot * gate).astype(BF16)
                dgate = (part - part * gate).astype(BF16)
                dproj[seq, r, n] = dvalue
                dproj[seq, r, slice(width + n.start, width + n.stop)] = dgate
                gather("value", n, fold_low(dvalue))
                gather("gate", n, fold_low(dgate))

            return [functools.partial(part, *c) for c in pieces]

        def project_back():
            return products("dact", lambda seq: dproj[seq], wglu, width, True)

        def activate_back(seq, n):
            def part(r, at):
                dlru = made["dact", seq][n.start // TILE][r] * slope[seq, r, n]
                dlru_ref[seq, at, n] = dlru
                gather("dlru", n, fold_low(dlru))
                gather("skip", n, fold_low(dlru * normed_ref[seq, at, n]))

            return [functools.partial(part, *c) for c in pieces]

        def read_out_back():
            return products("pull", lambda seq: dlru_ref[seq, rows, :], wout, 2 * states, True)

        def glu_back():
            def part(n):
                dglu[:, n] += dot_tn(both(lambda seq: act[seq]), both(lambda seq: dproj[seq, :, n]))

            return [functools.partial(part, n) for n in tiles(2 * width)]

        def out_back():
            def part(n):
                dout[:, n] += dot_tn(
                    both(lambda seq: state_ref[seq, rows, :]), both(lambda seq: dlru_ref[seq, rows, n])
                )

            return [functools.partial(part, n) for n in tiles(width)]

        def turn(seq):
            def part(k, at):
                pull = taken("pull", seq, slice(k * CHUNK, (k + 1) * CHUNK))
                zr, zi = cmul(pull[:, :states], pull[:, states:], p_ref[:, :states], p_ref[:, states:])
                split_store(stack.at[seq], k, zr, zi)

            return [functools.partial(part, *c) for c in chunks]

        def sum_back(seq):
            def part(k, at):
                ar, ai = carry[seq, 1:2, :states], carry[seq, 1:2, states:]
                wr, wi = carry[seq, 2:3, :states], carry[seq, 2:3, states:]
                back = dot_nn(tri[...], stack[seq, k])
                back_ref[seq, at, :] = back
                fr, fi = cmul(back[0:1, :states], back[0:1, states:], first_r, first_i)
                gr, gi = cmul(fr, fi, wr, wi)
                ar, ai = ar + gr, ai + gi
                wr, wi = cmul(wr, wi, step_r, step_i)
                carry[seq, 1:2, :states] = ar
                carry[seq, 1:2, states:] = ai
                carry[seq, 2:3, :states] = wr
                carry[seq, 2:3, states:] = wi
                start_ref[seq, :, :states] = ar
                start_ref[seq, :, states:] = ai

            return [functools.partial(part, *c) for c in chunks]

        def run(*lists):
            parts = [(i / len(one), part) for one in lists for i, part in enumerate(one)]
            for _, part in sorted(parts, key=lambda item: item[0]):
                part()

        run(*[make_states(seq) for seq in every])
        readout = read_out()
        for n, part in zip(spans, readout):
            run([part])
            run(*[activate(seq, n) for seq in every])
        projected = project()

        @pl.when(step >= 2)
        def _():
            mixed_copy(step - 2).wait()

        for k, n in enumerate(spans):
            run(projected[2 * k : 2 * k + 2])
            run(*[branch_out(seq, n) for seq in every])
        mixed_copy(step).start()
        for n, part in zip(spans, project_back()):
            run([part])
            run(*[activate_back(seq, n) for seq in every])
        run(glu_back())
        run(read_out_back())
        run(*[turn(seq) for seq in every], out_back())
        run(*[sum_back(seq) for seq in every])
        for row, name in enumerate(("lru", "branch", "dlru", "skip")):
            for n in spans:
                acc_ref[8 * row : 8 * row + 8, n] += folds[name, n.start]
        for row, name in enumerate(("value", "gate")):
            for n in spans:
                gacc_ref[8 * row : 8 * row + 8, n] += folds[name, n.start]

        return 0

    steps = stream_ref.shape[1] // BLOCK
    lax.fori_loop(0, steps, run_block, 0)
    for step in range(max(steps - 2, 0), steps):
        mixed_copy(jnp.int32(step)).wait()
    batch, height, _ = keep_ref.shape
    high = width // (2 * batch)
    part = height - high
    for ref, f in ((keep_ref, place_ref[0]), (send_ref, 1 - place_ref[0])):
        for b in range(batch):
            first = pl.multiple_of((f * batch + b) * high, high)
            ref[b, :high, :] = dglu[pl.ds(first, high), :].astype(BF16)
            first = pl.multiple_of((f * batch + b) * part, part)
            ref[b, high:, :width] = dout[pl.ds(first, part), :].astype(BF16)
            ref[b, high:, width:] = dout[pl.ds(states + first, part), :].astype(BF16)


def block_pass(place, batch, sums, normed, stream, cot, p, small, halves, came):
    seqs, length, width = stream.shape
    states2 = p.shape[1]
    height = width // (2 * batch) + states2 // (4 * batch)
    return pl.pallas_call(
        lambda *refs: block_kernel(len(came), *refs),
        in_specs=[SMEM_SPEC] + [VMEM_SPEC] * (12 + len(came)),
        out_specs=[HBM_SPEC] + [VMEM_SPEC] * 8,
        out_shape=[
            pltpu.HBM((seqs, length, width), BF16),
            pltpu.VMEM((seqs, length, states2), F32),
            pltpu.VMEM((seqs, length, states2), BF16),
            pltpu.VMEM((seqs, length, width), BF16),
            jax.ShapeDtypeStruct((seqs, 1, states2), F32),
            pltpu.VMEM((batch, height, 2 * width), BF16),
            pltpu.VMEM((batch, height, 2 * width), BF16),
            pltpu.VMEM((32, width), F32),
            pltpu.VMEM((16, width), F32),
        ],
        scratch_shapes=[
            pltpu.VMEM((seqs, 8, states2), F32),
            pltpu.VMEM((seqs, BLOCK // CHUNK, 2 * CHUNK, states2), BF16),
            pltpu.VMEM((CHUNK, 2 * CHUNK), BF16),
            pltpu.VMEM((seqs, BLOCK, width), BF16),
            pltpu.VMEM((seqs, BLOCK, 2 * width), BF16),
            pltpu.VMEM((seqs, BLOCK, width), BF16),
            pltpu.VMEM((2, seqs, BLOCK, width), BF16),
            pltpu.VMEM((width, 2 * width), BF16),
            pltpu.VMEM((states2, width), BF16),
            pltpu.VMEM((width, 2 * width), F32),
            pltpu.VMEM((states2, width), F32),
            pltpu.SemaphoreType.DMA((2,)),
        ],
        input_output_aliases={1: 1},
        compiler_params=pltpu.CompilerParams(vmem_limit_bytes=20 * MIB),
        cost_estimate=cost(28),
        name="block_pass",
    )(place, *kept(sums, normed, stream, cot, p, small, *halves, *came))


def adjoint_kernel(
    hops, others, place_ref, back_ref, _, normed_ref, win_ref, q_ref, small_ref, square_ref, acc_ref, gacc_ref,
    *rest,
):
    came = rest[:hops]
    ddrive_ref, keep_ref, send_ref, carry, din = rest[hops + others :]
    states = q_ref.shape[1] // 2
    seqs, length, _ = normed_ref.shape
    every = range(seqs)
    first_r, first_i = pair(small_ref, ROW_FIRST, states)
    back_r, back_i = pair(small_ref, ROW_BACK, states)
    carries = []
    for seq in every:
        entering(carry, came, seq, small_ref, states)
        carries.append((carry[0:1, :states], carry[0:1, states:]))
    real_sum = imag_sum = real_total = imag_total = jnp.zeros((8, states), F32)
    for base in reversed(range(0, length, BLOCK)):
        for k in reversed(range(BLOCK // CHUNK)):
            for seq in every:
                at = pl.ds(base + k * CHUNK, CHUNK)
                qr, qi = cmul(*carries[seq], back_r, back_i)
                vr = back_ref[seq, at, :states] + qr
                vi = back_ref[seq, at, states:] + qi
                carries[seq] = cmul(vr[0:1], vi[0:1], first_r, first_i)
                ar, ai = cmul(vr, vi, q_ref[:, :states], q_ref[:, states:])
                hr = ddrive_ref[seq, at, :states]
                hi = ddrive_ref[seq, at, states:]
                lr, li = ar.astype(BF16), ai.astype(BF16)
                real_sum += fold((lr * hr).astype(F32) + (li * hi).astype(F32))
                imag_sum += fold((lr * hi).astype(F32) - (li * hr).astype(F32))
                real_total += fold_low(lr)
                imag_total += fold_low(li)
                ddrive_ref[seq, at, :states] = lr
                ddrive_ref[seq, at, states:] = li
        rows = pl.ds(base, BLOCK)
        product = dot_tn(
            jnp.concatenate([normed_ref[seq, rows, :] for seq in every], axis=0),
            jnp.concatenate([ddrive_ref[seq, rows, :] for seq in every], axis=0),
        )
        if base == length - BLOCK:
            din[...] = product
        else:
            din[...] += product
    width = din.shape[0]
    gain = row_of(small_ref, ROW_GAIN)
    bias = row_of(small_ref, ROW_BIAS)
    skip = row_of(small_ref, ROW_SKIP)
    weight = win_ref[...].astype(F32)
    grad = din[...]
    in_r, in_i = weight[:, :states], weight[:, states:]
    g_r, g_i = grad[:, :states], grad[:, states:]
    x_r = jnp.sum(g_r * in_r + g_i * in_i, axis=0, keepdims=True)
    x_i = jnp.sum(g_r * in_i - g_i * in_r, axis=0, keepdims=True)
    inverse = small_ref[ROW_SCALE : ROW_SCALE + 1, states:]
    column = lambda v: jnp.sum(v, axis=0, keepdims=True)
    d_r = column(real_sum) * inverse - x_r
    d_i = column(imag_sum) * inverse - x_i
    decay, rotation = pair(small_ref, ROW_RATE, states)
    gathered = dot_nt_wide(jnp.ones((8, 2 * states), F32), weight * grad)[0:1]
    total = jnp.broadcast_to(jnp.concatenate([column(real_total), column(imag_total)], axis=1), (8, 2 * states))
    d_lru = column(acc_ref[16:24, :])
    d_skip = column(acc_ref[24:32, :])
    d_bias = dot_nt_wide(total, weight)[0:1] + skip * d_lru
    d_gain = (gathered + skip * d_skip - bias * d_bias) / gain
    d_nu = -decay * d_r
    d_theta = rotation * d_i
    d_values = column(gacc_ref[0:8, :])
    d_gates = column(gacc_ref[8:16, :])
    lane = lax.broadcasted_iota(jnp.int32, (1, width // 2), 1)
    squares = jnp.zeros((1, width // 2), F32)
    sums = (
        width * jnp.sum(square_ref[:, 0:1]), jnp.sum(acc_ref[0:8, :]), jnp.sum(acc_ref[8:16, :]),
    )
    for place, v in enumerate(sums):
        squares = jnp.where(lane == place, v, squares)
    half, some = width // 2, states // 2
    batch, height, _ = keep_ref.shape
    high = width // (2 * batch)
    me = place_ref[0]

    def chosen(f, low, up):
        return jnp.where(f == 0, low, up)

    for ref, f in ((keep_ref, me), (send_ref, 1 - me)):
        wide = lambda v: chosen(f, v[:, :half], v[:, half:])
        thin = lambda v: chosen(f, v[:, :some], v[:, some:])
        d_glu = chosen(f, d_values, d_gates)
        lines = (
            wide(d_gain),
            wide(d_bias),
            jnp.concatenate([thin(d_nu), thin(d_theta)], axis=1),
            jnp.concatenate([thin(x_r), jnp.zeros((1, some), F32)], axis=1),
            wide(d_skip),
            d_glu[:, :half],
            d_glu[:, half:],
            squares,
        )
        for b in range(batch):
            first = pl.multiple_of((f * batch + b) * high, high)
            ref[b, :high, :states] = din[pl.ds(first, high), :states].astype(BF16)
            ref[b, :high, states:] = (-din[pl.ds(first, high), states:]).astype(BF16)
            line = jnp.concatenate(lines[b * 8 // batch : (b + 1) * 8 // batch], axis=1)
            line = jnp.broadcast_to(line, (height - high, width)).astype(BF16)
            ref[b, high:, :] = line


def adjoint_pass(
    place, batch, back, state, normed, wback, q, small, square, acc, gacc, came, after
):
    seqs, length, width = normed.shape
    states2 = q.shape[1]
    return pl.pallas_call(
        lambda *refs: adjoint_kernel(len(came), len(after), *refs),
        in_specs=[SMEM_SPEC] + [VMEM_SPEC] * (9 + len(came)) + specs_of(after),
        out_specs=[VMEM_SPEC] * 3,
        out_shape=[
            pltpu.VMEM((seqs, length, states2), BF16),
            pltpu.VMEM((batch, width // (2 * batch) + 16, states2), BF16),
            pltpu.VMEM((batch, width // (2 * batch) + 16, states2), BF16),
        ],
        scratch_shapes=[
            pltpu.VMEM((8, states2), F32),
            pltpu.VMEM((width, states2), F32),
        ],
        input_output_aliases={2: 0},
        compiler_params=pltpu.CompilerParams(vmem_limit_bytes=8 * MIB),
        cost_estimate=cost(7),
        name="adjoint_pass",
    )(place, *kept(back, state, normed, wback, q, small, square, acc, gacc, *came), *placed(after))


def input_kernel(seq, skipped, ddrive_ref, dlru_ref, stream_ref, cot_ref, small_ref, win_ref, *rest):
    out_ref = rest[-1]
    base = (pl.program_id(0) + skipped) * BLOCK
    gain = row_of(small_ref, ROW_GAIN)
    skip = row_of(small_ref, ROW_SKIP)
    rows = pl.ds(pl.multiple_of(base, BLOCK), BLOCK)
    pulled = dot_nt(ddrive_ref[seq, rows, :], win_ref[...])
    for r in range(0, BLOCK, SUB):
        at = pl.ds(pl.multiple_of(base + r, SUB), SUB)
        d = pulled[r : r + SUB] + skip * dlru_ref[seq, at, :].astype(F32)
        x = stream_ref[seq, at, :].astype(F32)
        centre = x - jnp.mean(x, axis=-1, keepdims=True)
        spread = jnp.mean(centre * centre, axis=-1, keepdims=True)
        inverse = lax.rsqrt(spread + 1e-05)
        hat = centre * inverse
        dhat = d * gain
        m1 = jnp.mean(dhat, axis=-1, keepdims=True)
        m2 = jnp.mean(dhat * hat, axis=-1, keepdims=True)
        out_ref[r : r + SUB, :] = (dhat - m1 - hat * m2) * inverse + cot_ref[seq, at, :].astype(F32)


def input_pass(part, ddrive, dlru, stream, cot, small, win, earlier, after):
    seq, skipped, blocks = part
    seqs, length, width = stream.shape
    earlier = in_hbm(*earlier)
    return pl.pallas_call(
        lambda *refs: input_kernel(seq, skipped, *refs),
        grid=(blocks,),
        in_specs=[VMEM_SPEC] * 6 + [HBM_SPEC] * len(earlier) + specs_of(after),
        out_specs=pl.BlockSpec((None, BLOCK, width), lambda i: (seq, i + skipped, 0)),
        out_shape=pltpu.HBM((seqs, length, width), F32),
        input_output_aliases={6: 0} if earlier else {},
        compiler_params=pltpu.CompilerParams(vmem_limit_bytes=8 * MIB),
        cost_estimate=cost(1.1 * blocks),
        name="input_pass",
    )(*kept(ddrive, dlru, stream, cot, small, win), *earlier, *placed(after))


def pack_kernel(count, *refs):
    out_ref = refs[count]
    parts = refs[count + 1 : -1]
    copies = [
        pltpu.make_async_copy(source, target, refs[-1].at[k])
        for k, (source, target) in enumerate(zip(refs[:count], parts))
    ]
    for c in copies:
        c.start()
    for c in copies:
        c.wait()
    row = 0
    for ref in parts:
        for first in range(0, ref.shape[0], 128):
            out_ref[row : row + 1, :] = ref[first : first + 128].reshape(1, 128)
            row += 1


def pack_vectors(*vectors):
    rows = sum(v.shape[0] for v in vectors) // 128
    return pl.pallas_call(
        lambda *refs: pack_kernel(len(vectors), *refs),
        in_specs=[HBM_SPEC] * len(vectors),
        out_specs=VMEM_SPEC,
        out_shape=pltpu.VMEM((rows, 128), BF16),
        scratch_shapes=[pltpu.VMEM(v.shape, BF16) for v in vectors]
        + [pltpu.SemaphoreType.DMA((len(vectors),))],
        compiler_params=pltpu.CompilerParams(vmem_limit_bytes=2 * MIB),
        name="pack_vectors",
    )(*in_hbm(*vectors))


def pair_kernel(others, place_ref, keep_ref, came_ref, *rest):
    for hop, ref in enumerate(rest[others:]):
        at = place_ref[1] ^ hop
        ref[...] = (keep_ref[at].astype(F32) + came_ref[at].astype(F32)).astype(BF16)


def pair_sum(place, keep, came, after=()):
    count = keep.shape[0]
    return pl.pallas_call(
        lambda *refs: pair_kernel(len(after), *refs),
        in_specs=[SMEM_SPEC] + [VMEM_SPEC] * 2 + specs_of(after),
        out_specs=[VMEM_SPEC] * count,
        out_shape=[pltpu.VMEM(keep.shape[1:], BF16)] * count,
        compiler_params=pltpu.CompilerParams(vmem_limit_bytes=4 * MIB),
        cost_estimate=cost(0.7),
        name="pair_sum",
    )(place, *kept(keep, came), *placed(after))


def add_kernel(count, *refs):
    total = refs[0][...].astype(F32)
    for ref in refs[1:count]:
        total += ref[...].astype(F32)
    refs[-1][...] = total.astype(BF16)


def add_up(got, after=()):
    return pl.pallas_call(
        lambda *refs: add_kernel(len(got), *refs),
        in_specs=[VMEM_SPEC] * len(got) + specs_of(after),
        out_specs=VMEM_SPEC,
        out_shape=pltpu.VMEM(got[0].shape, BF16),
        compiler_params=pltpu.CompilerParams(vmem_limit_bytes=4 * MIB),
        cost_estimate=cost(0.2),
        name="add_up",
    )(*kept(*got), *placed(after))


def split_kernel(count, others, place_ref, *refs):
    total = refs[0]
    pieces = refs[count + others :]
    wide = total.shape[1] // len(pieces)
    for hop, ref in enumerate(pieces):
        at = lax.rem(place_ref[2] + hop, len(pieces))
        columns = pl.ds(pl.multiple_of(at * wide, wide), wide)
        v = refs[0][:, columns].astype(F32)
        for other in refs[1:count]:
            v += other[:, columns].astype(F32)
        ref[...] = v.astype(BF16)


def add_split(place, got, ring, after=()):
    rows, columns = got[0].shape
    return pl.pallas_call(
        lambda *refs: split_kernel(len(got), len(after), *refs),
        in_specs=[SMEM_SPEC] + [VMEM_SPEC] * len(got) + specs_of(after),
        out_specs=[VMEM_SPEC] * ring,
        out_shape=[pltpu.VMEM((rows, columns // ring), BF16)] * ring,
        compiler_params=pltpu.CompilerParams(vmem_limit_bytes=4 * MIB),
        cost_estimate=cost(0.3),
        name="add_split",
    )(place, *kept(*got), *placed(after))


def finish_kernel(count, place_ref, *refs):
    first, second, out_ref = refs[:count], refs[count : 2 * count], refs[-1]
    rows, wide = first[0].shape
    span = out_ref.shape[1]
    for hop in range(count):
        at = lax.rem(place_ref[2] + count - hop, count)
        if wide < span:
            per = span // wide
            row = pl.multiple_of(lax.div(at, per) * rows, rows)
            column = pl.multiple_of(lax.rem(at, per) * wide, wide)
            out_ref[pl.ds(row, rows), pl.ds(column, wide)] = first[hop][...]
        else:
            for k in range(wide // span):
                row = pl.multiple_of((at * (wide // span) + k) * rows, rows)
                out_ref[pl.ds(row, rows), :] = first[hop][:, k * span : (k + 1) * span]
    total = second[0][...].astype(F32)
    for ref in second[1:]:
        total += ref[...].astype(F32)
    out_ref[out_ref.shape[0] - total.shape[0] :, :] = total.astype(BF16)


def finish_seq(place, first, second, after):
    rows, wide = first[0].shape
    low, span = second[0].shape
    height = rows * wide * len(first) // span + low
    return pl.pallas_call(
        lambda *refs: finish_kernel(len(first), *refs),
        in_specs=[SMEM_SPEC] + [VMEM_SPEC] * (2 * len(first)) + specs_of(after),
        out_specs=VMEM_SPEC,
        out_shape=pltpu.VMEM((height, span), BF16),
        compiler_params=pltpu.CompilerParams(vmem_limit_bytes=4 * MIB),
        cost_estimate=cost(0.5),
        name="finish_seq",
    )(place, *kept(*first, *second), *placed(after))


def unpack_kernel(count, others, tokens, place_ref, *refs):
    got = refs[:count]
    (
        glu_ref, outr_ref, outi_ref, inr_ref, ini_ref, gain_ref, bias_ref, nu_ref, theta_ref,
        gamma_ref, skip_ref, glub_ref, rms_ref, lines,
    ) = refs[count + others :]
    width = glu_ref.shape[1] // 2
    states = inr_ref.shape[1]
    high = glu_ref.shape[0] // count
    part = outr_ref.shape[0] // count
    low = 2 * (high + part)
    for hop in range(count):
        at = place_ref[1] ^ hop
        v = got[hop]
        rows = pl.ds(pl.multiple_of(at * high, high), high)
        few = pl.ds(pl.multiple_of(at * part, part), part)
        glu_ref[rows, :width] = v[:high, :].astype(F32)
        outr_ref[few, :] = v[high : high + part, :].astype(F32)
        glu_ref[rows, width:] = v[high + part : 2 * high + part, :].astype(F32)
        outi_ref[few, :] = v[2 * high + part : low, :].astype(F32)
        inr_ref[rows, :] = v[low : low + high, :states].astype(F32)
        ini_ref[rows, :] = v[low : low + high, states:].astype(F32)
        lines[pl.ds(pl.multiple_of(at * 8, 8), 8), :] = v[low + high :, :].astype(F32)[:8]
    half, some = width // 2, states // 2
    per = 8 // count
    line = lambda k: lines[k // per * 8 : k // per * 8 + 1, k % per * half : (k % per + 1) * half]
    gain_ref[...] = line(0)
    bias_ref[...] = line(1)
    nu_ref[...] = line(2)[:, :some]
    theta_ref[...] = line(2)[:, some:]
    gamma_ref[...] = line(3)[:, :some]
    skip_ref[...] = line(4)
    glub_ref[:, :half] = line(5)
    glub_ref[:, half:] = line(6)
    rms_ref[...] = jnp.sqrt(line(7)[:, :3] / tokens)


def unpack(place, got, width, states, tokens, after):
    count = len(got)
    flat = [width // 2, width // 2, states // 2, states // 2, states // 2, width // 2, width, 3]
    return pl.pallas_call(
        lambda *refs: unpack_kernel(count, len(after), tokens, *refs),
        in_specs=[SMEM_SPEC] + [VMEM_SPEC] * count + specs_of(after),
        out_specs=[VMEM_SPEC] * 13,
        out_shape=[
            jax.ShapeDtypeStruct((width // 2, 2 * width), F32),
            jax.ShapeDtypeStruct((states // 2, width), F32),
            jax.ShapeDtypeStruct((states // 2, width), F32),
            jax.ShapeDtypeStruct((width // 2, states), F32),
            jax.ShapeDtypeStruct((width // 2, states), F32),
        ]
        + [jax.ShapeDtypeStruct((1, n), F32) for n in flat],
        scratch_shapes=[pltpu.VMEM((8 * count, width), F32)],
        compiler_params=pltpu.CompilerParams(vmem_limit_bytes=8 * MIB),
        name="unpack",
    )(place, *got, *placed(after))


def hops_of(ends, axis, reverse):
    count = lax.axis_size(axis)
    if count <= 4:
        return [
            lax.ppermute(
                ends,
                axis,
                [(i + hop, i) if reverse else (i, i + hop) for i in range(count - hop)],
            )
            for hop in range(1, count)
        ]
    place = lax.axis_index(axis)
    every = lax.all_gather(ends, axis)
    came = []
    for hop in range(1, count):
        source = place + hop if reverse else place - hop
        inside = (source >= 0) & (source < count)
        item = lax.dynamic_index_in_dim(every, jnp.clip(source, 0, count - 1), 0, False)
        came.append(jnp.where(inside, item, 0.0))
    return came


def swap(a):
    return lax.ppermute(a, "fsdp", [(0, 1), (1, 0)])


def swap_moves(axis, bit):
    return [(i, i ^ bit) for i in range(lax.axis_size(axis))]


def scatter_batch(pieces):
    return [pieces[0]] + [
        lax.ppermute(pieces[hop], "batch", swap_moves("batch", hop))
        for hop in range(1, len(pieces))
    ]


def around(pieces):
    ring = lax.axis_size("seq")
    return [pieces[0]] + [
        lax.ppermute(pieces[hop], "seq", [(i, (i + hop) % ring) for i in range(ring)])
        for hop in range(1, ring)
    ]


def share_seq(piece):
    ring = lax.axis_size("seq")
    if ring > 4:
        return [lax.psum(piece.astype(F32), "seq").astype(BF16)]
    return around([piece] * ring)


def gather_batch(piece):
    count = lax.axis_size("batch")
    return [piece] + [
        lax.ppermute(piece, "batch", swap_moves("batch", hop)) for hop in range(1, count)
    ]


def on_device(
    stream, norm_gain, norm_bias, in_real, in_imag, nu_log, theta_log, gamma_log, out_real,
    out_imag, skip_scale, glu_weight, glu_bias, cotangent,
):
    seqs, length, width = stream.shape
    states = 2 * nu_log.shape[0]
    batch = lax.axis_size("batch")
    place = jnp.stack(
        [lax.axis_index("fsdp"), lax.axis_index("batch"), lax.axis_index("seq")]
    ).astype(jnp.int32)
    place, in_real, in_imag, glu_weight, out_real, out_imag = lax.optimization_barrier(
        (place, in_real, in_imag, glu_weight, out_real, out_imag)
    )
    vectors = pack_vectors(
        norm_gain, norm_bias, skip_scale, glu_bias, nu_log, theta_log, gamma_log
    )
    into = [in_real, swap(in_real), in_imag, swap(in_imag)]
    others = [swap(glu_weight), swap(out_real), swap(out_imag)]
    (
        normed, sums, ends, p, q, small, win, wback, square, stream_kept, cot_kept, *own,
    ) = norm_pass(
        place, stream, cotangent, into, [glu_weight, out_real, out_imag], [vectors, swap(vectors)]
    )
    halves = [a for pair_of in zip(own, others) for a in pair_of]
    came = hops_of(ends, "seq", False)
    mixed, back, state, dlru, starts, keep, send, acc, gacc = block_pass(
        place, batch, sums, normed, stream_kept, cot_kept, p, small, halves, came
    )
    later = hops_of(starts, "seq", True)
    pieces = pair_sum(place, keep, swap(send), later)
    first = scatter_batch(pieces)
    ddrive, keep, send = adjoint_pass(
        place, batch, back, state, normed, wback, q, small, square, acc, gacc, later, pieces
    )
    ring = lax.axis_size("seq")
    short = ring <= 4
    send, *first = lax.optimization_barrier((send, *first))
    pieces = pair_sum(place, keep, swap(send))
    second = scatter_batch(pieces)
    first = add_split(place, first, ring if short else 1, pieces[:1])
    first = around(first) if short else share_seq(first[0])
    last = lambda part, earlier, after: input_pass(
        part, ddrive, dlru, stream_kept, cot_kept, small, wback, earlier, after
    )
    blocks = length // BLOCK
    grads = (last((0, 0, blocks // 2), (), [first[0], pieces[0]]),)
    first = add_up(first, grads)
    if short:
        first = around([first] * ring)
    second = share_seq(add_up(second, [first[0], *grads]))
    for seq in range(1, seqs):
        grads = (last((seq, 0, blocks), grads, [first[0], second[0]]),)
    got = gather_batch(finish_seq(place, first if short else [first], second, grads))
    grads = (last((0, blocks // 2, blocks - blocks // 2), grads, got[:1]),)
    grad_stream = grads[0]
    tokens = stream.size * batch * lax.axis_size("seq") * lax.axis_size("fsdp")
    (
        glu, out_r, out_i, in_r, in_i, gain, bias, nu, theta, gamma, skip, glub, rms,
    ) = unpack(place, got, width, states, float(tokens), grads)
    flat = lambda a: a.reshape(-1)
    return (
        mixed, grad_stream, flat(gain), flat(bias), in_r, in_i, flat(nu), flat(theta), flat(gamma),
        out_r, out_i, flat(skip), glu, flat(glub), flat(rms),
    )


def solution(mesh):
    tokens = P(("batch", "fsdp"), "seq", None)
    vector = P("fsdp")
    matrix = P("fsdp", None)
    weights = (
        vector, vector, matrix, matrix, vector, vector, vector, matrix, matrix, vector, matrix,
        vector,
    )
    return jax.shard_map(
        on_device,
        mesh=mesh,
        in_specs=(tokens,) + weights + (tokens,),
        out_specs=(tokens, tokens) + weights + (P(),),
        check_vma=False,
    )
```
